32 devices in a mesh: pipe: 2 (over x), row: 8 (over z, core), col: 2 (over y).
Axes of the slice: x: 2, y: 2, z: 4, core: 2. Of those that a mesh axis runs over, the one named last changes fastest.
Arguments:
- inputs: bfloat16 [4, 8, 1024, 512], P(None, 'row', 'col'), may hold values from -6 to 6
- first_gain: float32 [2, 512], P('pipe'), may hold values from 0.5 to 1.5
- first_shift: float32 [2, 512], P('pipe'), may hold values from -1.75 to 1.75
- qkv_weight: bfloat16 [2, 3, 512, 512], P('pipe', None, 'row', 'col'), may hold values from -0.25 to 0.25
- query_bias: float32 [2, 512], P('pipe', 'col'), may hold values from -3 to 3
- value_bias: float32 [2, 512], P('pipe', 'col'), may hold values from -1.75 to 1.75
- proj_weight: bfloat16 [2, 512, 512], P('pipe', 'col', 'row'), may hold values from -1 to 1
- proj_bias: float32 [2, 512], P('pipe'), may hold values from -1.75 to 1.75
- second_gain: float32 [2, 512], P('pipe'), may hold values from 0.5 to 1.5
- second_shift: float32 [2, 512], P('pipe'), may hold values from -1.75 to 1.75
- up_weight: bfloat16 [2, 512, 2048], P('pipe', 'row', 'col'), may hold values from -0.25 to 0.25
- up_bias: float32 [2, 2048], P('pipe', 'col'), may hold values from -3 to 3
- down_weight: bfloat16 [2, 2048, 512], P('pipe', 'col', 'row'), may hold values from -0.125 to 0.125
- down_bias: float32 [2, 512], P('pipe'), may hold values from -1.75 to 1.75
- cotangent: bfloat16 [4, 8, 1024, 512], P(None, 'row', 'col'), may hold values from -6 to 6
- live_clips: int32 [4, 8], P(None, 'row'), may hold values 0 or 1
Outputs:
- states: bfloat16 [2, 4, 8, 1024, 512], P('pipe', None, 'row', 'col')
- state_grads: float32 [2, 4, 8, 1024, 512], P('pipe', None, 'row', 'col')
- grad_first_gain: float32 [2, 512], P('pipe')
- grad_first_shift: float32 [2, 512], P('pipe')
- grad_qkv_weight: float32 [2, 3, 512, 512], P('pipe', None, 'row', 'col')
- grad_query_bias: float32 [2, 512], P('pipe', 'col')
- grad_value_bias: float32 [2, 512], P('pipe', 'col')
- grad_proj_weight: float32 [2, 512, 512], P('pipe', 'col', 'row')
- grad_proj_bias: float32 [2, 512], P('pipe')
- grad_second_gain: float32 [2, 512], P('pipe')
- grad_second_shift: float32 [2, 512], P('pipe')
- grad_up_weight: float32 [2, 512, 2048], P('pipe', 'row', 'col')
- grad_up_bias: float32 [2, 2048], P('pipe', 'col')
- grad_down_weight: float32 [2, 2048, 512], P('pipe', 'col', 'row')
- grad_down_bias: float32 [2, 512], P('pipe')
The draws below stay inside these ranges and needn't reach their ends.
All inputs are finite; a program needn't handle non-finite values. No bound on the sum of `live_clips` on one device may be relied on, other than what follows from the above.
Results may differ from the reference program's by a relative error of at most 0.015.
Values may be sent and summed in bfloat16 or wider, within the bound.
A program may use at most 192 MiB of HBM per device.

```python
import math
import jax
import jax.numpy as jnp
from jax import lax

D = 512
HD = 64
FF = 2048
SEQ = 1024
LAYERS = 2
MICRO = 4
CLIPS = 8


def set_ends(array, rng, least, high):
    longest = array.shape.index(max(array.shape))
    spots = []
    for shift in (0, 1):
        where = [jax.random.randint(jax.random.fold_in(rng, axis), (), 0, length) for axis, length in enumerate(array.shape)]
        where[longest] = (where[longest] + shift) % array.shape[longest]
        spots.append(tuple(where))
    return array.at[spots[0]].set(least).at[spots[1]].set(high)


def levels(own_key, dims, cuts, least, top_value):
    def one(dim, blocks):
        steps = jax.random.uniform(jax.random.fold_in(jax.random.fold_in(own_key, 6), dim), (blocks,), jnp.float32, least / len(cuts), top_value / len(cuts))
        return jnp.repeat(jnp.exp(steps), dims[dim] // blocks).reshape((-1,) + (1,) * (len(dims) - dim - 1))

    level = one(*cuts[0])
    for cut in cuts[1:]:
        level = level * one(*cut)
    return level


def noise(own_key, extent, width, reach, pieces=(), dtype=jnp.bfloat16):
    drawn = jax.random.normal(own_key, extent, jnp.float32) * width
    if len(pieces) > 0:
        drawn = levels(own_key, extent, pieces, -0.22, 0.18) * drawn
    return jnp.clip(drawn, min=-reach, max=reach).astype(dtype)


def setup_inputs(seed: int = 0) -> dict:
    arg_keys = jax.random.split(jax.random.key(seed), 17)
    return {
        "inputs": noise(arg_keys[0], (MICRO, CLIPS, SEQ, D), 1.0, 6.0, ((1, 8), (2, 2))),
        "first_gain": jnp.clip(1.0 + 0.1 * jax.random.normal(arg_keys[1], (LAYERS, D), jnp.float32), 0.5, 1.5),
        "first_shift": noise(arg_keys[2], (LAYERS, D), 0.3, 1.75, ((0, 2),), jnp.float32),
        "qkv_weight": noise(arg_keys[3], (LAYERS, 3, D, D), D ** -0.5, 0.25, ((0, 2), (2, 8), (3, 2))),
        "query_bias": noise(arg_keys[4], (LAYERS, D), 0.5, 3.0, ((0, 2), (1, 2)), jnp.float32),
        "value_bias": noise(arg_keys[5], (LAYERS, D), 0.3, 1.75, ((0, 2), (1, 2)), jnp.float32),
        "proj_weight": noise(arg_keys[6], (LAYERS, D, D), (D // 16) ** -0.5, 1.0, ((0, 2), (1, 2), (2, 8))),
        "proj_bias": noise(arg_keys[7], (LAYERS, D), 0.3, 1.75, ((0, 2),), jnp.float32),
        "second_gain": jnp.clip(1.0 + 0.1 * jax.random.normal(arg_keys[8], (LAYERS, D), jnp.float32), 0.5, 1.5),
        "second_shift": noise(arg_keys[9], (LAYERS, D), 0.3, 1.75, ((0, 2),), jnp.float32),
        "up_weight": noise(arg_keys[10], (LAYERS, D, FF), D ** -0.5, 0.25, ((0, 2), (1, 8), (2, 2))),
        "up_bias": noise(arg_keys[11], (LAYERS, FF), 0.5, 3.0, ((0, 2), (1, 2)), jnp.float32),
        "down_weight": noise(arg_keys[12], (LAYERS, FF, D), FF ** -0.5, 0.125, ((0, 2), (1, 2), (2, 8))),
        "down_bias": noise(arg_keys[13], (LAYERS, D), 0.3, 1.75, ((0, 2),), jnp.float32),
        "cotangent": noise(arg_keys[14], (MICRO, CLIPS, SEQ, D), 1.0, 6.0, ((1, 8), (2, 2))),
        "live_clips": set_ends((jax.random.randint(arg_keys[15], (MICRO, CLIPS), 0, 5) < 4).astype(jnp.int32), jax.random.fold_in(arg_keys[15], 1), 0, 1),
    }


@jax.custom_vjp
def low(v):
    return lax.optimization_barrier(v.astype(jnp.bfloat16)).astype(jnp.float32)

@jax.custom_vjp
def low_back(v):
    return v

def low_keep(v):
    return (low(v), None)

def low_pass(kept, grad):
    return (grad,)

def back_keep(v):
    return (v, None)

def back_low(kept, grad):
    return (low(grad),)
low.defvjp(low_keep, low_pass)
low_back.defvjp(back_keep, back_low)
epsilon = 1e-05

def layer_norm(values, gain, shift):
    row_mean = lax.optimization_barrier(jnp.mean(values, axis=-1, keepdims=True))
    row_var = lax.optimization_barrier(jnp.mean(jnp.square(values - row_mean), axis=-1, keepdims=True))
    return (values - row_mean) * lax.rsqrt(row_var + epsilon) * gain + shift

def encoder_layer(layer_params, values):
    first_gain, first_shift, qkv_weight, query_bias, value_bias, proj_weight, proj_bias, second_gain, second_shift, up_weight, up_bias, down_weight, down_bias = layer_params
    highest = lax.Precision.HIGHEST
    head_count = D // HD
    normed_one = low(layer_norm(values, first_gain, first_shift))
    query_heads = low(low_back(jnp.dot(normed_one, qkv_weight[0], precision=highest)) + query_bias).reshape(SEQ, head_count, HD)
    key_heads = low(low_back(jnp.dot(normed_one, qkv_weight[1], precision=highest))).reshape(SEQ, head_count, HD)
    value_heads = low(low_back(jnp.dot(normed_one, qkv_weight[2], precision=highest)) + value_bias).reshape(SEQ, head_count, HD)
    scores = low_back(jnp.einsum('qhd,khd->hqk', query_heads, key_heads, precision=highest) * (1.0 / math.sqrt(HD)))
    softmax_out = low(jax.nn.softmax(scores, axis=-1))
    context = low(low_back(jnp.einsum('hqk,khd->qhd', softmax_out, value_heads, precision=highest).reshape(SEQ, D)))
    hidden = values + low_back(jnp.dot(context, proj_weight, precision=highest)) + proj_bias
    normed_two = low(layer_norm(hidden, second_gain, second_shift))
    pre_act = low_back(jnp.dot(normed_two, up_weight, precision=highest)) + up_bias
    activated = low(jax.nn.gelu(pre_act, approximate=False))
    return hidden + low_back(jnp.dot(activated, down_weight, precision=highest)) + down_bias

def clip_layers(params, clip_rows, offset):
    first = encoder_layer(tuple((part[0] for part in params)), clip_rows)
    sent = low(low_back(first)) + offset
    return (sent, encoder_layer(tuple((part[1] for part in params)), sent))

def reference(inputs, first_gain, first_shift, qkv_weight, query_bias, value_bias, proj_weight, proj_bias, second_gain, second_shift, up_weight, up_bias, down_weight, down_bias, cotangent, live_clips):
    params = tuple((part.astype(jnp.float32) for part in (first_gain, first_shift, qkv_weight, query_bias, value_bias, proj_weight, proj_bias, second_gain, second_shift, up_weight, up_bias, down_weight, down_bias)))
    clip_count = MICRO * CLIPS
    clips = inputs.reshape(clip_count, SEQ, D).astype(jnp.float32)
    offsets = jnp.zeros_like(clips)

    def forward(clips, offsets, params):

        def per_clip(pair):
            return clip_layers(params, pair[0], pair[1])
        return lax.map(jax.checkpoint(per_clip), (clips, offsets))
    (sent, final), pull = jax.vjp(forward, clips, offsets, params)
    live_weight = live_clips.reshape(clip_count).astype(jnp.float32)
    cot_rows = cotangent.reshape(clip_count, SEQ, D).astype(jnp.float32) * live_weight[:, None, None]
    grad_clips, grad_offsets, grad_params = pull((jnp.zeros_like(sent), cot_rows))
    states = jnp.stack([sent, final]).reshape(LAYERS, MICRO, CLIPS, SEQ, D).astype(jnp.bfloat16)
    state_grads = jnp.stack([grad_clips, grad_offsets]).reshape(LAYERS, MICRO, CLIPS, SEQ, D)
    return (states, state_grads, grad_params[0], grad_params[1], grad_params[2], grad_params[3], grad_params[4], grad_params[5], grad_params[6], grad_params[7], grad_params[8], grad_params[9], grad_params[10], grad_params[11], grad_params[12])
```

```python
import functools
import math

import jax
import jax.numpy as jnp
from jax import lax
from jax.experimental import pallas as pl
from jax.experimental.pallas import tpu as pltpu
from jax.sharding import PartitionSpec as P

HD = 64


epsilon = 1e-05


def from_behind(value, axis, steps):
    count = lax.axis_size(axis)
    first, last = (max(0, -steps), min(count, count - steps))
    return lax.ppermute(value, axis, [(source, source + steps) for source in range(first, last)])


def exact_gelu(values):
    return jax.nn.gelu(values, approximate=False)


def spread_features(normed):
    return lax.all_gather(normed, "col", axis=0, tiled=True)


def sum_columns(partial_rows):
    return lax.psum_scatter(partial_rows, "col", scatter_dimension=0, tiled=True)


def spread_grads(grad_low):
    return lax.all_gather(grad_low, "col", axis=0, tiled=True)


def sum_grad_columns(partial_rows):
    return lax.psum_scatter(partial_rows, "col", scatter_dimension=0, tiled=True)


def norm_forward(values, gain, shift):
    row_mean = jnp.mean(values, axis=-1, keepdims=True)
    row_var = jnp.mean(jnp.square(values - row_mean), axis=-1, keepdims=True)
    inv_std = lax.rsqrt(row_var + epsilon)
    centered = (values - row_mean) * inv_std
    return (centered, inv_std[:, 0], (centered * gain + shift).astype(jnp.bfloat16))


def norm_backward(grad_norm, centered, inv_std, gain):
    grad_gain = jnp.sum(grad_norm * centered, axis=0)
    grad_shift = jnp.sum(grad_norm, axis=0)
    scaled = grad_norm * gain
    first = jnp.mean(scaled, axis=-1, keepdims=True)
    second = jnp.mean(scaled * centered, axis=-1, keepdims=True)
    grad_in = inv_std[:, None] * (scaled - first - centered * second)
    return (grad_in, grad_gain, grad_shift)


def attention_probs(query_heads, key_heads):
    score_scale = 1.0 / math.sqrt(HD)
    scores = (
        jnp.einsum("qhd,khd->hqk", query_heads, key_heads, preferred_element_type=jnp.float32)
        * score_scale
    )
    return jax.nn.softmax(scores, axis=-1)


def layer_forward(values, weights, params):
    qkv_full, proj_full, up_full, down_full = weights
    (
        gain_one,
        shift_one,
        query_bias,
        value_bias,
        proj_bias,
        gain_two,
        shift_two,
        up_bias,
        down_bias,
    ) = params
    head_count = qkv_full.shape[2] // HD
    centered_one, inv_one, normed_one = norm_forward(values, gain_one, shift_one)
    attn_input = spread_features(normed_one)
    frame_count = attn_input.shape[0]
    projected = jnp.einsum("sd,jde->jse", attn_input, qkv_full, preferred_element_type=jnp.float32)
    query_heads = (
        (projected[0] + query_bias).astype(jnp.bfloat16).reshape(frame_count, head_count, HD)
    )
    key_heads = projected[1].astype(jnp.bfloat16).reshape(frame_count, head_count, HD)
    value_heads = (
        (projected[2] + value_bias).astype(jnp.bfloat16).reshape(frame_count, head_count, HD)
    )
    softmax_out = attention_probs(query_heads, key_heads)
    context = jnp.einsum(
        "hqk,khd->qhd",
        softmax_out.astype(jnp.bfloat16),
        value_heads,
        preferred_element_type=jnp.float32,
    )
    context = context.reshape(frame_count, head_count * HD).astype(jnp.bfloat16)
    attended = (
        sum_columns(jnp.dot(context, proj_full, preferred_element_type=jnp.float32)) + proj_bias
    )
    hidden = values + attended
    centered_two, inv_two, normed_two = norm_forward(hidden, gain_two, shift_two)
    mlp_input = spread_features(normed_two)
    pre_act = jnp.dot(mlp_input, up_full, preferred_element_type=jnp.float32) + up_bias
    activated = exact_gelu(pre_act).astype(jnp.bfloat16)
    output = (
        hidden
        + sum_columns(jnp.dot(activated, down_full, preferred_element_type=jnp.float32))
        + down_bias
    )
    kept = (
        centered_one,
        inv_one,
        attn_input,
        query_heads,
        key_heads,
        value_heads,
        context,
        centered_two,
        inv_two,
        mlp_input,
        pre_act,
        activated,
    )
    return (output, kept)


def layer_backward(grad_out, kept, weights, params):
    qkv_full, proj_full, up_full, down_full = weights
    (
        gain_one,
        shift_one,
        query_bias,
        value_bias,
        proj_bias,
        gain_two,
        shift_two,
        up_bias,
        down_bias,
    ) = params
    (
        centered_one,
        inv_one,
        attn_input,
        query_heads,
        key_heads,
        value_heads,
        context,
        centered_two,
        inv_two,
        mlp_input,
        pre_act,
        activated,
    ) = kept
    frame_count = attn_input.shape[0]
    score_scale = 1.0 / math.sqrt(HD)
    grad_down_bias = jnp.sum(grad_out, axis=0)
    down_grad = spread_grads(grad_out.astype(jnp.bfloat16))
    grad_down = jnp.einsum("sf,sd->fd", activated, down_grad, preferred_element_type=jnp.float32)
    grad_act = jnp.einsum("sd,fd->sf", down_grad, down_full, preferred_element_type=jnp.float32)
    unused, gelu_pull = jax.vjp(exact_gelu, pre_act)
    grad_pre = gelu_pull(grad_act)[0]
    grad_up_bias = jnp.sum(grad_pre, axis=0)
    grad_pre_low = grad_pre.astype(jnp.bfloat16)
    grad_up = jnp.einsum("sd,sf->df", mlp_input, grad_pre_low, preferred_element_type=jnp.float32)
    grad_normed_two = sum_grad_columns(
        jnp.einsum("sf,df->sd", grad_pre_low, up_full, preferred_element_type=jnp.float32)
    )
    grad_hidden_norm, grad_gain_two, grad_shift_two = norm_backward(
        grad_normed_two, centered_two, inv_two, gain_two
    )
    grad_hidden = grad_out + grad_hidden_norm
    grad_proj_bias = jnp.sum(grad_hidden, axis=0)
    proj_grad = spread_grads(grad_hidden.astype(jnp.bfloat16))
    grad_proj = jnp.einsum("se,sd->ed", context, proj_grad, preferred_element_type=jnp.float32)
    grad_context = jnp.einsum("sd,ed->se", proj_grad, proj_full, preferred_element_type=jnp.float32)
    grad_context = grad_context.astype(jnp.bfloat16).reshape(query_heads.shape)
    softmax_out = attention_probs(query_heads, key_heads)
    grad_probs = jnp.einsum(
        "qhd,khd->hqk", grad_context, value_heads, preferred_element_type=jnp.float32
    )
    grad_value = jnp.einsum(
        "hqk,qhd->khd",
        softmax_out.astype(jnp.bfloat16),
        grad_context,
        preferred_element_type=jnp.float32,
    )
    grad_scores = softmax_out * (
        grad_probs - jnp.sum(softmax_out * grad_probs, axis=-1, keepdims=True)
    )
    scores_low = grad_scores.astype(jnp.bfloat16)
    grad_query = (
        jnp.einsum("hqk,khd->qhd", scores_low, key_heads, preferred_element_type=jnp.float32)
        * score_scale
    )
    grad_key = (
        jnp.einsum("hqk,qhd->khd", scores_low, query_heads, preferred_element_type=jnp.float32)
        * score_scale
    )
    grad_query = grad_query.reshape(frame_count, -1)
    grad_key = grad_key.reshape(frame_count, -1)
    grad_value = grad_value.reshape(frame_count, -1)
    grad_query_bias = jnp.sum(grad_query, axis=0)
    grad_value_bias = jnp.sum(grad_value, axis=0)
    grad_qkv_low = jnp.stack([grad_query, grad_key, grad_value]).astype(jnp.bfloat16)
    grad_qkv = jnp.einsum(
        "sd,jse->jde", attn_input, grad_qkv_low, preferred_element_type=jnp.float32
    )
    grad_normed_one = sum_grad_columns(
        jnp.einsum("jse,jde->sd", grad_qkv_low, qkv_full, preferred_element_type=jnp.float32)
    )
    grad_in_norm, grad_gain_one, grad_shift_one = norm_backward(
        grad_normed_one, centered_one, inv_one, gain_one
    )
    grad_in = grad_hidden + grad_in_norm
    weight_grads = (grad_qkv, grad_proj, grad_up, grad_down)
    vector_grads = (
        grad_gain_one,
        grad_shift_one,
        grad_query_bias,
        grad_value_bias,
        grad_proj_bias,
        grad_gain_two,
        grad_shift_two,
        grad_up_bias,
        grad_down_bias,
    )
    return (grad_in, weight_grads, vector_grads)


def store_slot(buffer, slot_index, is_valid, value):
    current = lax.dynamic_index_in_dim(buffer, slot_index, 0, keepdims=False)
    return lax.dynamic_update_index_in_dim(
        buffer, jnp.where(is_valid, value, current), slot_index, 0
    )


def reduce_end(weight_acc):
    return (
        lax.psum_scatter(
            weight_acc[0].astype(jnp.bfloat16), "row", scatter_dimension=1, tiled=True
        ).astype(jnp.float32),
        lax.psum_scatter(
            weight_acc[1].astype(jnp.bfloat16), "row", scatter_dimension=1, tiled=True
        ).astype(jnp.float32),
        lax.psum_scatter(
            weight_acc[2].astype(jnp.bfloat16), "row", scatter_dimension=0, tiled=True
        ).astype(jnp.float32),
        lax.psum_scatter(
            weight_acc[3].astype(jnp.bfloat16), "row", scatter_dimension=1, tiled=True
        ).astype(jnp.float32),
    )


def on_device(
    inputs,
    first_gain,
    first_shift,
    qkv_weight,
    query_bias,
    value_bias,
    proj_weight,
    proj_bias,
    second_gain,
    second_shift,
    up_weight,
    up_bias,
    down_weight,
    down_bias,
    cotangent,
    live_clips,
):
    micro_count = inputs.shape[0]
    row_count = inputs.shape[2]
    feature_count = inputs.shape[3]
    section_index = lax.axis_index("pipe")
    weights = (
        lax.all_gather(qkv_weight[0], "row", axis=1, tiled=True),
        lax.all_gather(proj_weight[0], "row", axis=1, tiled=True),
        lax.all_gather(up_weight[0], "row", axis=0, tiled=True),
        lax.all_gather(down_weight[0], "row", axis=1, tiled=True),
    )
    params = (
        first_gain[0],
        first_shift[0],
        query_bias[0],
        value_bias[0],
        proj_bias[0],
        second_gain[0],
        second_shift[0],
        up_bias[0],
        down_bias[0],
    )
    kept_buffers = ()
    zero_rows = jnp.zeros((row_count, feature_count), jnp.bfloat16)
    zero_stack = jnp.zeros((micro_count, row_count, feature_count), jnp.bfloat16)
    own_inputs = inputs[:, 0]

    def forward_tick(state_carry, tick_index):
        received, outputs, layer_inputs, buffers = state_carry
        batch_index = tick_index - section_index
        is_valid = (batch_index >= 0) & (batch_index < micro_count)
        slot_index = jnp.clip(batch_index, 0, micro_count - 1)
        own_input = lax.dynamic_index_in_dim(
            own_inputs, jnp.minimum(tick_index, micro_count - 1), 0, keepdims=False
        )
        layer_input = jnp.where(section_index == 0, own_input, received)
        output, kept = layer_forward(layer_input.astype(jnp.float32), weights, params)
        output_low = output.astype(jnp.bfloat16)
        passed = from_behind(output_low, "pipe", 1)
        outputs = store_slot(outputs, slot_index, is_valid, output_low)
        layer_inputs = store_slot(layer_inputs, slot_index, is_valid, layer_input)
        return ((passed, outputs, layer_inputs, buffers), None)

    tick_range = jnp.arange(micro_count + 1)
    forward_out, unused = lax.scan(
        forward_tick, (zero_rows, zero_stack, zero_stack, kept_buffers), tick_range
    )
    unused_rows, outputs, layer_inputs, kept_buffers = forward_out
    weight_acc = tuple((jnp.zeros(part.shape, jnp.float32) for part in weights))
    vector_acc = tuple((jnp.zeros(part.shape, jnp.float32) for part in params))
    grads_init = jnp.zeros((micro_count, row_count, feature_count), jnp.float32)
    live_rows = live_clips[:, 0]
    cot_rows_all = cotangent[:, 0]

    def backward_tick(state_carry, tick_index):
        received, grads_in, weight_sum, vector_sum = state_carry
        batch_index = micro_count - tick_index - section_index
        is_valid = (batch_index >= 0) & (batch_index < micro_count)
        slot_index = jnp.clip(batch_index, 0, micro_count - 1)
        cot_rows = lax.dynamic_index_in_dim(cot_rows_all, slot_index, 0, keepdims=False).astype(
            jnp.float32
        )
        live_flag = lax.dynamic_index_in_dim(live_rows, slot_index, 0, keepdims=False).astype(
            jnp.float32
        )
        grad_out = jnp.where(
            section_index == 1, cot_rows * live_flag, received.astype(jnp.float32)
        ) * is_valid.astype(jnp.float32)
        stored_input = lax.dynamic_index_in_dim(layer_inputs, slot_index, 0, keepdims=False)
        kept = layer_forward(stored_input.astype(jnp.float32), weights, params)[1]
        grad_in, weight_grads, vector_grads = layer_backward(grad_out, kept, weights, params)
        passed = from_behind(grad_in.astype(jnp.bfloat16), "pipe", -1)
        grads_in = store_slot(grads_in, slot_index, is_valid, grad_in)
        weight_sum = jax.tree.map(jnp.add, weight_sum, weight_grads)
        vector_sum = jax.tree.map(jnp.add, vector_sum, vector_grads)
        return ((passed, grads_in, weight_sum, vector_sum), None)

    backward_out, unused_two = lax.scan(
        backward_tick, (zero_rows, grads_init, weight_acc, vector_acc), tick_range
    )
    unused_grad, grads_in, weight_acc, vector_acc = backward_out
    weight_out = reduce_end(weight_acc)
    split_out = lax.psum((vector_acc[2], vector_acc[3], vector_acc[7]), "row")
    whole_out = lax.psum(
        (vector_acc[0], vector_acc[1], vector_acc[4], vector_acc[5], vector_acc[6], vector_acc[8]),
        ("row", "col"),
    )
    return (
        outputs[None, :, None],
        grads_in[None, :, None],
        whole_out[0][None],
        whole_out[1][None],
        weight_out[0][None],
        split_out[0][None],
        split_out[1][None],
        weight_out[1][None],
        whole_out[2][None],
        whole_out[3][None],
        whole_out[4][None],
        weight_out[2][None],
        split_out[2][None],
        weight_out[3][None],
        whole_out[5][None],
    )


def contract(left, right, left_dim, right_dim):
    return lax.dot_general(
        left, right, (((left_dim,), (right_dim,)), ((), ())), preferred_element_type=jnp.float32
    )


TILE = 256
LANES = 2 * HD
VMEM_BYTES = 60 * 1024 * 1024
GROUP = ("pipe", "col")
EVERY = ("pipe", "col", "row")
ERFC_SCALE = 0.4
ERFC_TERMS = (
    0.23192221664065504,
    0.1618227850291895,
    0.4682761333792345,
    -0.37091039694171485,
    0.7091488547855423,
    -0.20025962054546065,
)


def gelu_and_slope(values):
    size = jnp.abs(values) * math.sqrt(0.5)
    turn = 1.0 / (1.0 + ERFC_SCALE * size)
    series = ERFC_TERMS[-1]
    for term in ERFC_TERMS[-2::-1]:
        series = series * turn + term
    bell = jnp.exp(-(size * size))
    tail = 0.5 * (series * turn * bell)
    below = jnp.where(values >= 0.0, 1.0 - tail, tail)
    return (values * below, below + values * bell * (1.0 / math.sqrt(2.0 * math.pi)))


def norm_rows(values):
    centered = values - jnp.mean(values, axis=-1, keepdims=True)
    inv_std = lax.rsqrt(jnp.mean(centered * centered, axis=-1, keepdims=True) + epsilon)
    return (centered * inv_std, inv_std)


def norm_rows_backward(grad, centered, inv_std, gain):
    scaled = grad * gain
    first = jnp.mean(scaled, axis=-1, keepdims=True)
    second = jnp.mean(scaled * centered, axis=-1, keepdims=True)
    return inv_std * (scaled - first - centered * second)


def tile_rows(index):
    return pl.ds(pl.multiple_of(index * TILE, TILE), TILE)


def lane_block(start):
    return pl.ds(pl.multiple_of(start, LANES), LANES)


class Sizes:
    def __init__(self, frames, features, width, hidden):
        self.frames = frames
        self.features = features
        self.width = width
        self.hidden = hidden
        self.tiles = frames // TILE
        self.pairs = 2 * width // LANES
        self.tails = 6 * features
        self.tail = 2 * width + hidden
        self.vector = self.tails + self.tail
        self.sums = self.tails + 2 * self.tail

    def pair_base(self, pair):
        per = self.width // LANES
        part = pair // per
        return part * (3 * self.width) + (pair % per) * LANES


def attention_forward(sizes, qkv, context, lse):
    width = sizes.width
    score_scale = 1.0 / math.sqrt(HD)

    def one_pair(pair, carry):
        base = sizes.pair_base(pair)
        for start in range(0, sizes.frames, TILE):
            rows = slice(start, start + TILE)
            query_pair = qkv[rows, lane_block(base)]
            key_pair = qkv[:, lane_block(base + width)]
            value_pair = qkv[:, lane_block(base + 2 * width)]
            parts = []
            for head in range(2):
                lanes = slice(head * HD, (head + 1) * HD)
                scaled = query_pair[:, lanes] * jnp.asarray(score_scale, jnp.bfloat16)
                scores = contract(key_pair[:, lanes], scaled, 1, 1)
                top = jnp.max(scores, axis=0, keepdims=True)
                weights = jnp.exp(scores - top)
                total = jnp.sum(weights, axis=0, keepdims=True)
                mixed = contract(value_pair[:, lanes], weights.astype(jnp.bfloat16), 0, 0)
                parts.append(mixed / total)
                lse[pair, head : head + 1, rows] = top + jnp.log(total)
            both = jnp.concatenate(parts, axis=0)
            context[rows, lane_block(pair * LANES)] = both.T.astype(jnp.bfloat16)
        return carry

    lax.fori_loop(0, sizes.pairs, one_pair, 0)


def attention_backward(sizes, qkv, grad_context, lse, add_query_bias, add_value_bias):
    width = sizes.width
    score_scale = 1.0 / math.sqrt(HD)

    def one_pair(pair, carry):
        base = sizes.pair_base(pair)
        key_pair = qkv[:, lane_block(base + width)]
        value_pair = qkv[:, lane_block(base + 2 * width)]
        grad_keys = [None, None]
        grad_values = [None, None]
        query_total = jnp.zeros((1, LANES), jnp.float32)
        for start in range(0, sizes.frames, TILE):
            rows = slice(start, start + TILE)
            query_pair = qkv[rows, lane_block(base)]
            grad_pair = grad_context[rows, lane_block(pair * LANES)]
            parts = []
            for head in range(2):
                lanes = slice(head * HD, (head + 1) * HD)
                keys = key_pair[:, lanes]
                grads = grad_pair[:, lanes]
                scaled = query_pair[:, lanes] * jnp.asarray(score_scale, jnp.bfloat16)
                scores = contract(keys, scaled, 1, 1)
                probs = jnp.exp(scores - lse[pair, head : head + 1, rows])
                grad_probs = contract(value_pair[:, lanes], grads, 1, 1)
                delta = jnp.sum(probs * grad_probs, axis=0, keepdims=True)
                low_scores = (probs * (grad_probs - delta)).astype(jnp.bfloat16)
                value_part = contract(probs.astype(jnp.bfloat16), grads, 1, 0)
                key_part = contract(low_scores, scaled, 1, 0)
                grad_values[head] = value_part if start == 0 else grad_values[head] + value_part
                grad_keys[head] = key_part if start == 0 else grad_keys[head] + key_part
                parts.append(contract(keys, low_scores, 0, 0))
            turned = jnp.concatenate(parts, axis=0).T * score_scale
            query_total = query_total + jnp.sum(turned, axis=0, keepdims=True)
            qkv[rows, lane_block(base)] = turned.astype(jnp.bfloat16)
        key_grad = jnp.concatenate(grad_keys, axis=1)
        value_grad = jnp.concatenate(grad_values, axis=1)
        qkv[:, lane_block(base + width)] = key_grad.astype(jnp.bfloat16)
        qkv[:, lane_block(base + 2 * width)] = value_grad.astype(jnp.bfloat16)
        add_query_bias(pair, query_total)
        add_value_bias(pair, jnp.sum(value_grad, axis=0, keepdims=True))
        return carry

    lax.fori_loop(0, sizes.pairs, one_pair, 0)


def vector_reader(sizes, vectors, layer):
    features, width = (sizes.features, sizes.width)

    def whole(index):
        return vectors[2 * layer : 2 * layer + 1, index * features : (index + 1) * features]

    def split(part, start, size):
        row = 2 * layer + part
        first = sizes.tails + start
        return vectors[row : row + 1, first : first + size]

    return (whole, split)


def forward_qkv(sizes, layer, values, early, vectors, qkv):
    features, width = (sizes.features, sizes.width)
    whole, split = vector_reader(sizes, vectors, layer)

    def one_tile(index, carry):
        rows = tile_rows(index)
        centered, unused = norm_rows(values[rows, :].astype(jnp.float32))
        normed = (centered * whole(0) + whole(1)).astype(jnp.bfloat16)
        for part in range(2):
            weights = early.at[2 * layer + part]
            for kind in range(3):
                result = contract(normed, weights[:, kind * width : (kind + 1) * width], 1, 0)
                if kind == 0:
                    result = result + split(part, 0, width)
                if kind == 2:
                    result = result + split(part, width, width)
                first = (3 * part + kind) * width
                qkv[rows, first : first + width] = result.astype(jnp.bfloat16)
        return carry

    lax.fori_loop(0, sizes.tiles, one_tile, 0)


def forward_rest(sizes, layer, values, early, late, vectors, context, hidden, active, slope, output):
    features, width, size = (sizes.features, sizes.width, sizes.hidden)
    whole, split = vector_reader(sizes, vectors, layer)

    def one_tile(index, carry):
        rows = tile_rows(index)
        total = values[rows, :].astype(jnp.float32) + whole(2)
        for part in range(2):
            total = total + contract(
                context[rows, part * width : (part + 1) * width],
                early[2 * layer + part, :, 3 * width : 4 * width],
                1,
                1,
            )
        hidden[rows, :] = total
        centered, unused = norm_rows(total)
        normed = (centered * whole(3) + whole(4)).astype(jnp.bfloat16)
        total = total + whole(5)
        for part in range(2):
            for start in range(0, size, 512):
                pre_act = contract(
                    normed, late[2 * layer + part, :, start : start + 512], 1, 0
                ) + split(part, 2 * width + start, 512)
                act, act_slope = gelu_and_slope(pre_act)
                act = act.astype(jnp.bfloat16)
                first = part * size + start
                active[rows, first : first + 512] = act
                slope[rows, first : first + 512] = act_slope.astype(jnp.bfloat16)
                total = total + contract(
                    act, late[2 * layer + part, :, size + start : size + start + 512], 1, 1
                )
        output[rows, :] = total.astype(jnp.bfloat16)
        return carry

    lax.fori_loop(0, sizes.tiles, one_tile, 0)


def forward_kernel(
    sizes,
    x_ref,
    early_ref,
    late_ref,
    vector_ref,
    sent_ref,
    final_ref,
    lse_ref,
    qkv_out,
    context_out,
    hidden_out,
    active_out,
    slope_out,
    qkv,
    context,
    hidden,
    active,
    slope,
    sems,
):
    copies = []

    def save(source, target, layer, number):
        copy = pltpu.make_async_copy(source.at[layer], target.at[layer], sems.at[layer, number])
        copy.start()
        copies.append(copy)

    for layer in range(2):
        values = (x_ref, sent_ref)[layer]
        output = (sent_ref, final_ref)[layer]
        forward_qkv(sizes, layer, values, early_ref, vector_ref, qkv.at[layer])
        save(qkv, qkv_out, layer, 0)
        attention_forward(sizes, qkv.at[layer], context.at[layer], lse_ref.at[layer])
        save(context, context_out, layer, 1)
        forward_rest(
            sizes,
            layer,
            values,
            early_ref,
            late_ref,
            vector_ref,
            context.at[layer],
            hidden.at[layer],
            active.at[layer],
            slope.at[layer],
            output,
        )
        save(hidden, hidden_out, layer, 2)
        save(active, active_out, layer, 3)
        save(slope, slope_out, layer, 4)
    for copy in copies:
        copy.wait()


def saved_shapes(sizes):
    frames, features = (sizes.frames, sizes.features)
    return [
        ((2, frames, 6 * sizes.width), jnp.bfloat16),
        ((2, frames, 2 * sizes.width), jnp.bfloat16),
        ((2, frames, features), jnp.float32),
        ((2, frames, 2 * sizes.hidden), jnp.bfloat16),
        ((2, frames, 2 * sizes.hidden), jnp.bfloat16),
    ]


def run_forward(sizes, values, early, late, vectors):
    frames, features = (sizes.frames, sizes.features)
    vmem = pl.BlockSpec(memory_space=pltpu.VMEM)
    hbm = pl.BlockSpec(memory_space=pl.ANY)
    saved = saved_shapes(sizes)
    return pl.pallas_call(
        functools.partial(forward_kernel, sizes),
        in_specs=[vmem] * 4,
        out_specs=[vmem] * 3 + [hbm] * 5,
        out_shape=[
            jax.ShapeDtypeStruct((frames, features), jnp.bfloat16),
            jax.ShapeDtypeStruct((frames, features), jnp.bfloat16),
            jax.ShapeDtypeStruct((2, sizes.pairs, 2, frames), jnp.float32),
        ]
        + [jax.ShapeDtypeStruct(shape, dtype) for shape, dtype in saved],
        scratch_shapes=[pltpu.VMEM(shape, dtype) for shape, dtype in saved]
        + [pltpu.SemaphoreType.DMA((2, 5))],
        compiler_params=pltpu.CompilerParams(vmem_limit_bytes=VMEM_BYTES),
        name="layers_forward",
    )(values, early, late, vectors)


def add_row(sums, layer, start, value):
    where = (slice(layer, layer + 1), slice(start, start + value.shape[1]))
    sums[where] = sums[where] + value


def column_sum(values):
    return jnp.sum(values, axis=0, keepdims=True)


def backward_mlp(
    sizes, layer, hidden, active, slope, early, late, vectors, grad, sums, normed_t, grad_t, grad_late
):
    features, width, size = (sizes.features, sizes.width, sizes.hidden)
    whole, split = vector_reader(sizes, vectors, layer)

    def one_tile(index, carry):
        rows = tile_rows(index)
        grad_out = grad[rows, :]
        add_row(sums, layer, 5 * features, column_sum(grad_out))
        grad_low = grad_out.astype(jnp.bfloat16)
        grad_t[:, rows] = grad_low.T
        centered, inv_std = norm_rows(hidden[rows, :])
        normed_t[:, rows] = (centered * whole(3) + whole(4)).astype(jnp.bfloat16).T
        grad_normed = jnp.zeros((TILE, features), jnp.float32)
        for part in range(2):
            for start in range(0, size, 512):
                first = part * size + start
                grad_act = contract(
                    grad_low, late[2 * layer + part, :, size + start : size + start + 512], 1, 0
                )
                grad_pre = grad_act * slope[rows, first : first + 512].astype(jnp.float32)
                add_row(
                    sums,
                    layer,
                    sizes.tails + part * sizes.tail + 2 * width + start,
                    column_sum(grad_pre),
                )
                low = grad_pre.astype(jnp.bfloat16)
                slope[rows, first : first + 512] = low
                grad_normed = grad_normed + contract(
                    low, late[2 * layer + part, :, start : start + 512], 1, 1
                )
        add_row(sums, layer, 3 * features, column_sum(grad_normed * centered))
        add_row(sums, layer, 4 * features, column_sum(grad_normed))
        grad_hidden = grad_out + norm_rows_backward(grad_normed, centered, inv_std, whole(3))
        add_row(sums, layer, 2 * features, column_sum(grad_hidden))
        grad[rows, :] = grad_hidden
        return carry

    lax.fori_loop(0, sizes.tiles, one_tile, 0)
    for part in range(2):
        for start in range(0, size, 256):
            first = part * size + start
            up = contract(normed_t[...], slope[:, first : first + 256], 1, 0)
            grad_late[part, :, start : start + 256] = up.astype(jnp.bfloat16)
            down = contract(grad_t[...], active[:, first : first + 256], 1, 0)
            grad_late[part, :, size + start : size + start + 256] = down.astype(jnp.bfloat16)


def backward_attention(
    sizes,
    layer,
    values,
    qkv,
    context,
    lse,
    early,
    vectors,
    grad,
    sums,
    normed_t,
    grad_t,
    grad_context,
    grad_early,
    grad_in,
):
    features, width = (sizes.features, sizes.width)
    whole, split = vector_reader(sizes, vectors, layer)

    def to_context(index, carry):
        rows = tile_rows(index)
        low = grad[rows, :].astype(jnp.bfloat16)
        grad_t[:, rows] = low.T
        for part in range(2):
            grad_context[rows, part * width : (part + 1) * width] = contract(
                low, early[2 * layer + part, :, 3 * width : 4 * width], 1, 0
            ).astype(jnp.bfloat16)
        return carry

    lax.fori_loop(0, sizes.tiles, to_context, 0)
    per = width // LANES

    def add_bias(offset):
        def add(pair, value):
            start = sizes.tails + (pair // per) * sizes.tail + offset + (pair % per) * LANES
            where = (slice(layer, layer + 1), lane_block(start))
            sums[where] = sums[where] + value

        return add

    attention_backward(sizes, qkv, grad_context, lse, add_bias(0), add_bias(width))

    def to_input(index, carry):
        rows = tile_rows(index)
        grad_normed = jnp.zeros((TILE, features), jnp.float32)
        for part in range(2):
            grad_normed = grad_normed + contract(
                qkv[rows, part * 3 * width : (part + 1) * 3 * width],
                early[2 * layer + part, :, : 3 * width],
                1,
                1,
            )
        centered, inv_std = norm_rows(values[rows, :].astype(jnp.float32))
        normed_t[:, rows] = (centered * whole(0) + whole(1)).astype(jnp.bfloat16).T
        add_row(sums, layer, 0, column_sum(grad_normed * centered))
        add_row(sums, layer, features, column_sum(grad_normed))
        low = (
            grad[rows, :] + norm_rows_backward(grad_normed, centered, inv_std, whole(0))
        ).astype(jnp.bfloat16)
        grad_in[rows, :] = low
        grad[rows, :] = low.astype(jnp.float32)
        return carry

    lax.fori_loop(0, sizes.tiles, to_input, 0)
    for part in range(2):
        for kind in range(3):
            first = (3 * part + kind) * width
            result = contract(normed_t[...], qkv[:, first : first + width], 1, 0)
            grad_early[part, :, kind * width : (kind + 1) * width] = result.astype(jnp.bfloat16)
        result = contract(grad_t[...], context[:, part * width : (part + 1) * width], 1, 0)
        grad_early[part, :, 3 * width :] = result.astype(jnp.bfloat16)


def backward_kernel(
    sizes,
    live_ref,
    cot_ref,
    x_ref,
    sent_ref,
    early_ref,
    late_ref,
    vector_ref,
    lse_ref,
    qkv_in,
    context_in,
    hidden_in,
    active_in,
    slope_in,
    mid_ref,
    start_ref,
    sums,
    grad_early_out,
    grad_late_out,
    qkv,
    context,
    hidden,
    active,
    slope,
    early,
    late,
    grad,
    normed_t,
    grad_t,
    grad_context,
    grad_early,
    grad_late,
    sems,
):
    def load(source, target, layer, number):
        copy = pltpu.make_async_copy(source.at[layer], target, sems.at[layer, number])
        copy.start()
        return copy

    def store(source, target, layer, number):
        copy = pltpu.make_async_copy(
            source, target.at[pl.ds(2 * layer, 2)], sems.at[layer, number]
        )
        copy.start()
        return copy

    def load_pair(source, target, layer, number):
        copy = pltpu.make_async_copy(
            source.at[pl.ds(2 * layer, 2)], target.at[pl.ds(2 * layer, 2)], sems.at[layer, number]
        )
        copy.start()
        return copy

    sums[...] = jnp.zeros_like(sums)
    late_copies = [load_pair(late_ref, late, layer, 5) for layer in (1, 0)]
    early_copies = [load_pair(early_ref, early, layer, 6) for layer in (1, 0)]
    grad[...] = cot_ref[...].astype(jnp.float32) * live_ref[0, 0]
    stores = []
    for step, layer in enumerate((1, 0)):
        mlp = [
            load(hidden_in, hidden, layer, 0),
            load(slope_in, slope, layer, 1),
            load(active_in, active, layer, 2),
        ]
        attention = [load(qkv_in, qkv, layer, 3), load(context_in, context, layer, 4)]
        late_copies[step].wait()
        for copy in mlp:
            copy.wait()
        backward_mlp(
            sizes,
            layer,
            hidden,
            active,
            slope,
            early,
            late,
            vector_ref,
            grad,
            sums,
            normed_t,
            grad_t,
            grad_late.at[pl.ds(2 * layer, 2)],
        )
        stores.append(
            store(grad_late.at[pl.ds(2 * layer, 2)], grad_late_out, layer, 7)
        )
        early_copies[step].wait()
        for copy in attention:
            copy.wait()
        backward_attention(
            sizes,
            layer,
            (x_ref, sent_ref)[layer],
            qkv,
            context,
            lse_ref.at[layer],
            early,
            vector_ref,
            grad,
            sums,
            normed_t,
            grad_t,
            grad_context,
            grad_early.at[pl.ds(2 * layer, 2)],
            (start_ref, mid_ref)[layer],
        )
        stores.append(
            store(grad_early.at[pl.ds(2 * layer, 2)], grad_early_out, layer, 8)
        )
    for copy in stores:
        copy.wait()


def run_backward(sizes, live, cot, values, sent, early, late, vectors, lse, saved):
    frames, features = (sizes.frames, sizes.features)
    vmem = pl.BlockSpec(memory_space=pltpu.VMEM)
    hbm = pl.BlockSpec(memory_space=pl.ANY)
    smem = pl.BlockSpec(memory_space=pltpu.SMEM)
    low = jnp.bfloat16
    return pl.pallas_call(
        functools.partial(backward_kernel, sizes),
        in_specs=[smem, vmem, vmem, vmem, hbm, hbm, vmem, vmem] + [hbm] * 5,
        out_specs=[vmem, vmem, vmem, hbm, hbm],
        out_shape=[
            jax.ShapeDtypeStruct((frames, features), low),
            jax.ShapeDtypeStruct((frames, features), low),
            jax.ShapeDtypeStruct((2, sizes.sums), jnp.float32),
            jax.ShapeDtypeStruct(early.shape, low),
            jax.ShapeDtypeStruct(late.shape, low),
        ],
        scratch_shapes=[pltpu.VMEM(shape[1:], dtype) for shape, dtype in saved_shapes(sizes)]
        + [
            pltpu.VMEM(early.shape, low),
            pltpu.VMEM(late.shape, low),
            pltpu.VMEM((frames, features), jnp.float32),
            pltpu.VMEM((features, frames), low),
            pltpu.VMEM((features, frames), low),
            pltpu.VMEM((frames, 2 * sizes.width), low),
            pltpu.VMEM(early.shape, low),
            pltpu.VMEM(late.shape, low),
            pltpu.SemaphoreType.DMA((2, 9)),
        ],
        compiler_params=pltpu.CompilerParams(vmem_limit_bytes=VMEM_BYTES),
        name="layers_backward",
    )(live, cot, values, sent, early, late, vectors, lse, *saved)


def trade(pieces, place):
    count = len(pieces)
    stacked = jnp.stack(pieces)
    taken = [lax.dynamic_index_in_dim(stacked, place, 0, keepdims=False)]
    for step in range(1, count):
        sent = lax.dynamic_index_in_dim(stacked, place ^ step, 0, keepdims=False)
        taken.append(
            lax.ppermute(sent, GROUP, [(here, here ^ step) for here in range(count)])
        )
    return taken


def in_order(taken, place):
    stacked = jnp.stack(taken)
    return jnp.stack(
        [
            lax.dynamic_index_in_dim(stacked, place ^ index, 0, keepdims=False)
            for index in range(len(taken))
        ]
    )


def swap_columns(own, other, col):
    got = lax.ppermute(other, "col", [(0, 1), (1, 0)])
    return jnp.where(col == 0, jnp.concatenate([own, got]), jnp.concatenate([got, own]))


def gather_blocks(block):
    full = lax.all_gather(block, EVERY, axis=0, tiled=True)
    return full.reshape(lax.axis_size(GROUP), -1, block.shape[1])


def on_device_clip(
    inputs,
    first_gain,
    first_shift,
    qkv_weight,
    query_bias,
    value_bias,
    proj_weight,
    proj_bias,
    second_gain,
    second_shift,
    up_weight,
    up_bias,
    down_weight,
    down_bias,
    cotangent,
    live_clips,
):
    section, col = (lax.axis_index("pipe"), lax.axis_index("col"))
    place = 2 * section + col
    width, hidden_width = (qkv_weight.shape[3], up_weight.shape[2])
    features = inputs.shape[3]
    half = inputs.shape[2]
    sizes = Sizes(2 * half, features, width, hidden_width)
    early_block = jnp.concatenate(
        [qkv_weight[0, 0], qkv_weight[0, 1], qkv_weight[0, 2], proj_weight[0].T], axis=1
    )
    late_block = jnp.concatenate([up_weight[0], down_weight[0].T], axis=1)
    early = gather_blocks(early_block)
    late = gather_blocks(late_block)
    vectors = lax.all_gather(
        jnp.concatenate(
            [
                first_gain[0],
                first_shift[0],
                proj_bias[0],
                second_gain[0],
                second_shift[0],
                down_bias[0],
                query_bias[0],
                value_bias[0],
                up_bias[0],
            ]
        ),
        GROUP,
        axis=0,
        tiled=False,
    )

    def own_clip(rows):
        own = lax.dynamic_index_in_dim(rows[:, 0], place, 0, keepdims=False)
        other = lax.dynamic_index_in_dim(rows[:, 0], place ^ 1, 0, keepdims=False)
        return swap_columns(own, other, col)

    values = own_clip(inputs)
    cot = own_clip(cotangent)
    live = lax.dynamic_slice(live_clips, (place, 0), (1, 1)).astype(jnp.float32)
    sent, final, lse, *saved = run_forward(sizes, values, early, late, vectors)
    mid, start, sums, grad_early, grad_late = run_backward(
        sizes, live, cot, values, sent, early, late, vectors, lse, saved
    )
    own_early, own_late = [
        lax.psum_scatter(
            grads.reshape(-1, grads.shape[2]), EVERY, scatter_dimension=0, tiled=True
        ).astype(jnp.float32)
        for grads in (grad_early, grad_late)
    ]
    states = in_order(
        trade([sent[:half], sent[half:], final[:half], final[half:]], place), place
    )
    grads_in = in_order(
        trade([start[:half], start[half:], mid[:half], mid[half:]], place), place
    ).astype(jnp.float32)
    sums_all = lax.dynamic_slice(lax.psum(sums, EVERY), (section, 0), (1, sizes.sums))
    split_out = lax.dynamic_slice(
        sums_all, (0, sizes.tails + col * sizes.tail), (1, sizes.tail)
    )
    whole_out = [sums_all[:, index * features : (index + 1) * features] for index in range(6)]
    return (
        states[None, :, None],
        grads_in[None, :, None],
        whole_out[0],
        whole_out[1],
        jnp.stack([own_early[:, part * width : (part + 1) * width] for part in range(3)])[None],
        split_out[:, :width],
        split_out[:, width : 2 * width],
        own_early[:, 3 * width :].T[None],
        whole_out[2],
        whole_out[3],
        whole_out[4],
        own_late[:, :hidden_width][None],
        split_out[:, 2 * width :],
        own_late[:, hidden_width:].T[None],
        whole_out[5],
    )


def one_clip_each(mesh):
    sizes = dict(mesh.shape)
    return sizes["pipe"] == 2 and sizes["col"] == 2


def choose(mesh):
    def body(*arrays):
        fits = one_clip_each(mesh) and arrays[0].shape[:2] == (4, 1)
        return (on_device_clip if fits else on_device)(*arrays)

    return body


def solution(mesh):
    placed = (
        P(None, "row", "col", None),
        P("pipe", None),
        P("pipe", None),
        P("pipe", None, "row", "col"),
        P("pipe", "col"),
        P("pipe", "col"),
        P("pipe", "col", "row"),
        P("pipe", None),
        P("pipe", None),
        P("pipe", None),
        P("pipe", "row", "col"),
        P("pipe", "col"),
        P("pipe", "col", "row"),
        P("pipe", None),
        P(None, "row", "col", None),
        P(None, "row"),
    )
    return jax.shard_map(
        choose(mesh),
        mesh=mesh,
        in_specs=placed,
        out_specs=(
            P("pipe", None, "row", "col", None),
            P("pipe", None, "row", "col", None),
            P("pipe", None),
            P("pipe", None),
            P("pipe", None, "row", "col"),
            P("pipe", "col"),
            P("pipe", "col"),
            P("pipe", "col", "row"),
            P("pipe", None),
            P("pipe", None),
            P("pipe", None),
            P("pipe", "row", "col"),
            P("pipe", "col"),
            P("pipe", "col", "row"),
            P("pipe", None),
        ),
        check_vma=False,
    )
```

```python
import functools
import math

import jax
import jax.numpy as jnp
from jax import lax
from jax.experimental import pallas as pl
from jax.experimental.pallas import tpu as pltpu
from jax.sharding import PartitionSpec as P

HD = 64


epsilon = 1e-05


def from_behind(value, axis, steps):
    count = lax.axis_size(axis)
    first, last = (max(0, -steps), min(count, count - steps))
    return lax.ppermute(value, axis, [(source, source + steps) for source in range(first, last)])


def exact_gelu(values):
    return jax.nn.gelu(values, approximate=False)


def spread_features(normed):
    return lax.all_gather(normed, "col", axis=0, tiled=True)


def sum_columns(partial_rows):
    return lax.psum_scatter(partial_rows, "col", scatter_dimension=0, tiled=True)


def spread_grads(grad_low):
    return lax.all_gather(grad_low, "col", axis=0, tiled=True)


def sum_grad_columns(partial_rows):
    return lax.psum_scatter(partial_rows, "col", scatter_dimension=0, tiled=True)


def norm_forward(values, gain, shift):
    row_mean = jnp.mean(values, axis=-1, keepdims=True)
    row_var = jnp.mean(jnp.square(values - row_mean), axis=-1, keepdims=True)
    inv_std = lax.rsqrt(row_var + epsilon)
    centered = (values - row_mean) * inv_std
    return (centered, inv_std[:, 0], (centered * gain + shift).astype(jnp.bfloat16))


def norm_backward(grad_norm, centered, inv_std, gain):
    grad_gain = jnp.sum(grad_norm * centered, axis=0)
    grad_shift = jnp.sum(grad_norm, axis=0)
    scaled = grad_norm * gain
    first = jnp.mean(scaled, axis=-1, keepdims=True)
    second = jnp.mean(scaled * centered, axis=-1, keepdims=True)
    grad_in = inv_std[:, None] * (scaled - first - centered * second)
    return (grad_in, grad_gain, grad_shift)


def attention_probs(query_heads, key_heads):
    score_scale = 1.0 / math.sqrt(HD)
    scores = (
        jnp.einsum("qhd,khd->hqk", query_heads, key_heads, preferred_element_type=jnp.float32)
        * score_scale
    )
    return jax.nn.softmax(scores, axis=-1)


def layer_forward(values, weights, params):
    qkv_full, proj_full, up_full, down_full = weights
    (
        gain_one,
        shift_one,
        query_bias,
        value_bias,
        proj_bias,
        gain_two,
        shift_two,
        up_bias,
        down_bias,
    ) = params
    head_count = qkv_full.shape[2] // HD
    centered_one, inv_one, normed_one = norm_forward(values, gain_one, shift_one)
    attn_input = spread_features(normed_one)
    frame_count = attn_input.shape[0]
    projected = jnp.einsum("sd,jde->jse", attn_input, qkv_full, preferred_element_type=jnp.float32)
    query_heads = (
        (projected[0] + query_bias).astype(jnp.bfloat16).reshape(frame_count, head_count, HD)
    )
    key_heads = projected[1].astype(jnp.bfloat16).reshape(frame_count, head_count, HD)
    value_heads = (
        (projected[2] + value_bias).astype(jnp.bfloat16).reshape(frame_count, head_count, HD)
    )
    softmax_out = attention_probs(query_heads, key_heads)
    context = jnp.einsum(
        "hqk,khd->qhd",
        softmax_out.astype(jnp.bfloat16),
        value_heads,
        preferred_element_type=jnp.float32,
    )
    context = context.reshape(frame_count, head_count * HD).astype(jnp.bfloat16)
    attended = (
        sum_columns(jnp.dot(context, proj_full, preferred_element_type=jnp.float32)) + proj_bias
    )
    hidden = values + attended
    centered_two, inv_two, normed_two = norm_forward(hidden, gain_two, shift_two)
    mlp_input = spread_features(normed_two)
    pre_act = jnp.dot(mlp_input, up_full, preferred_element_type=jnp.float32) + up_bias
    activated = exact_gelu(pre_act).astype(jnp.bfloat16)
    output = (
        hidden
        + sum_columns(jnp.dot(activated, down_full, preferred_element_type=jnp.float32))
        + down_bias
    )
    kept = (
        centered_one,
        inv_one,
        attn_input,
        query_heads,
        key_heads,
        value_heads,
        context,
        centered_two,
        inv_two,
        mlp_input,
        pre_act,
        activated,
    )
    return (output, kept)


def layer_backward(grad_out, kept, weights, params):
    qkv_full, proj_full, up_full, down_full = weights
    (
        gain_one,
        shift_one,
        query_bias,
        value_bias,
        proj_bias,
        gain_two,
        shift_two,
        up_bias,
        down_bias,
    ) = params
    (
        centered_one,
        inv_one,
        attn_input,
        query_heads,
        key_heads,
        value_heads,
        context,
        centered_two,
        inv_two,
        mlp_input,
        pre_act,
        activated,
    ) = kept
    frame_count = attn_input.shape[0]
    score_scale = 1.0 / math.sqrt(HD)
    grad_down_bias = jnp.sum(grad_out, axis=0)
    down_grad = spread_grads(grad_out.astype(jnp.bfloat16))
    grad_down = jnp.einsum("sf,sd->fd", activated, down_grad, preferred_element_type=jnp.float32)
    grad_act = jnp.einsum("sd,fd->sf", down_grad, down_full, preferred_element_type=jnp.float32)
    unused, gelu_pull = jax.vjp(exact_gelu, pre_act)
    grad_pre = gelu_pull(grad_act)[0]
    grad_up_bias = jnp.sum(grad_pre, axis=0)
    grad_pre_low = grad_pre.astype(jnp.bfloat16)
    grad_up = jnp.einsum("sd,sf->df", mlp_input, grad_pre_low, preferred_element_type=jnp.float32)
    grad_normed_two = sum_grad_columns(
        jnp.einsum("sf,df->sd", grad_pre_low, up_full, preferred_element_type=jnp.float32)
    )
    grad_hidden_norm, grad_gain_two, grad_shift_two = norm_backward(
        grad_normed_two, centered_two, inv_two, gain_two
    )
    grad_hidden = grad_out + grad_hidden_norm
    grad_proj_bias = jnp.sum(grad_hidden, axis=0)
    proj_grad = spread_grads(grad_hidden.astype(jnp.bfloat16))
    grad_proj = jnp.einsum("se,sd->ed", context, proj_grad, preferred_element_type=jnp.float32)
    grad_context = jnp.einsum("sd,ed->se", proj_grad, proj_full, preferred_element_type=jnp.float32)
    grad_context = grad_context.astype(jnp.bfloat16).reshape(query_heads.shape)
    softmax_out = attention_probs(query_heads, key_heads)
    grad_probs = jnp.einsum(
        "qhd,khd->hqk", grad_context, value_heads, preferred_element_type=jnp.float32
    )
    grad_value = jnp.einsum(
        "hqk,qhd->khd",
        softmax_out.astype(jnp.bfloat16),
        grad_context,
        preferred_element_type=jnp.float32,
    )
    grad_scores = softmax_out * (
        grad_probs - jnp.sum(softmax_out * grad_probs, axis=-1, keepdims=True)
    )
    scores_low = grad_scores.astype(jnp.bfloat16)
    grad_query = (
        jnp.einsum("hqk,khd->qhd", scores_low, key_heads, preferred_element_type=jnp.float32)
        * score_scale
    )
    grad_key = (
        jnp.einsum("hqk,qhd->khd", scores_low, query_heads, preferred_element_type=jnp.float32)
        * score_scale
    )
    grad_query = grad_query.reshape(frame_count, -1)
    grad_key = grad_key.reshape(frame_count, -1)
    grad_value = grad_value.reshape(frame_count, -1)
    grad_query_bias = jnp.sum(grad_query, axis=0)
    grad_value_bias = jnp.sum(grad_value, axis=0)
    grad_qkv_low = jnp.stack([grad_query, grad_key, grad_value]).astype(jnp.bfloat16)
    grad_qkv = jnp.einsum(
        "sd,jse->jde", attn_input, grad_qkv_low, preferred_element_type=jnp.float32
    )
    grad_normed_one = sum_grad_columns(
        jnp.einsum("jse,jde->sd", grad_qkv_low, qkv_full, preferred_element_type=jnp.float32)
    )
    grad_in_norm, grad_gain_one, grad_shift_one = norm_backward(
        grad_normed_one, centered_one, inv_one, gain_one
    )
    grad_in = grad_hidden + grad_in_norm
    weight_grads = (grad_qkv, grad_proj, grad_up, grad_down)
    vector_grads = (
        grad_gain_one,
        grad_shift_one,
        grad_query_bias,
        grad_value_bias,
        grad_proj_bias,
        grad_gain_two,
        grad_shift_two,
        grad_up_bias,
        grad_down_bias,
    )
    return (grad_in, weight_grads, vector_grads)


def store_slot(buffer, slot_index, is_valid, value):
    current = lax.dynamic_index_in_dim(buffer, slot_index, 0, keepdims=False)
    return lax.dynamic_update_index_in_dim(
        buffer, jnp.where(is_valid, value, current), slot_index, 0
    )


def reduce_end(weight_acc):
    return (
        lax.psum_scatter(
            weight_acc[0].astype(jnp.bfloat16), "row", scatter_dimension=1, tiled=True
        ).astype(jnp.float32),
        lax.psum_scatter(
            weight_acc[1].astype(jnp.bfloat16), "row", scatter_dimension=1, tiled=True
        ).astype(jnp.float32),
        lax.psum_scatter(
            weight_acc[2].astype(jnp.bfloat16), "row", scatter_dimension=0, tiled=True
        ).astype(jnp.float32),
        lax.psum_scatter(
            weight_acc[3].astype(jnp.bfloat16), "row", scatter_dimension=1, tiled=True
        ).astype(jnp.float32),
    )


def on_device(
    inputs,
    first_gain,
    first_shift,
    qkv_weight,
    query_bias,
    value_bias,
    proj_weight,
    proj_bias,
    second_gain,
    second_shift,
    up_weight,
    up_bias,
    down_weight,
    down_bias,
    cotangent,
    live_clips,
):
    micro_count = inputs.shape[0]
    row_count = inputs.shape[2]
    feature_count = inputs.shape[3]
    section_index = lax.axis_index("pipe")
    weights = (
        lax.all_gather(qkv_weight[0], "row", axis=1, tiled=True),
        lax.all_gather(proj_weight[0], "row", axis=1, tiled=True),
        lax.all_gather(up_weight[0], "row", axis=0, tiled=True),
        lax.all_gather(down_weight[0], "row", axis=1, tiled=True),
    )
    params = (
        first_gain[0],
        first_shift[0],
        query_bias[0],
        value_bias[0],
        proj_bias[0],
        second_gain[0],
        second_shift[0],
        up_bias[0],
        down_bias[0],
    )
    kept_buffers = ()
    zero_rows = jnp.zeros((row_count, feature_count), jnp.bfloat16)
    zero_stack = jnp.zeros((micro_count, row_count, feature_count), jnp.bfloat16)
    own_inputs = inputs[:, 0]

    def forward_tick(state_carry, tick_index):
        received, outputs, layer_inputs, buffers = state_carry
        batch_index = tick_index - section_index
        is_valid = (batch_index >= 0) & (batch_index < micro_count)
        slot_index = jnp.clip(batch_index, 0, micro_count - 1)
        own_input = lax.dynamic_index_in_dim(
            own_inputs, jnp.minimum(tick_index, micro_count - 1), 0, keepdims=False
        )
        layer_input = jnp.where(section_index == 0, own_input, received)
        output, kept = layer_forward(layer_input.astype(jnp.float32), weights, params)
        output_low = output.astype(jnp.bfloat16)
        passed = from_behind(output_low, "pipe", 1)
        outputs = store_slot(outputs, slot_index, is_valid, output_low)
        layer_inputs = store_slot(layer_inputs, slot_index, is_valid, layer_input)
        return ((passed, outputs, layer_inputs, buffers), None)

    tick_range = jnp.arange(micro_count + 1)
    forward_out, unused = lax.scan(
        forward_tick, (zero_rows, zero_stack, zero_stack, kept_buffers), tick_range
    )
    unused_rows, outputs, layer_inputs, kept_buffers = forward_out
    weight_acc = tuple((jnp.zeros(part.shape, jnp.float32) for part in weights))
    vector_acc = tuple((jnp.zeros(part.shape, jnp.float32) for part in params))
    grads_init = jnp.zeros((micro_count, row_count, feature_count), jnp.float32)
    live_rows = live_clips[:, 0]
    cot_rows_all = cotangent[:, 0]

    def backward_tick(state_carry, tick_index):
        received, grads_in, weight_sum, vector_sum = state_carry
        batch_index = micro_count - tick_index - section_index
        is_valid = (batch_index >= 0) & (batch_index < micro_count)
        slot_index = jnp.clip(batch_index, 0, micro_count - 1)
        cot_rows = lax.dynamic_index_in_dim(cot_rows_all, slot_index, 0, keepdims=False).astype(
            jnp.float32
        )
        live_flag = lax.dynamic_index_in_dim(live_rows, slot_index, 0, keepdims=False).astype(
            jnp.float32
        )
        grad_out = jnp.where(
            section_index == 1, cot_rows * live_flag, received.astype(jnp.float32)
        ) * is_valid.astype(jnp.float32)
        stored_input = lax.dynamic_index_in_dim(layer_inputs, slot_index, 0, keepdims=False)
        kept = layer_forward(stored_input.astype(jnp.float32), weights, params)[1]
        grad_in, weight_grads, vector_grads = layer_backward(grad_out, kept, weights, params)
        passed = from_behind(grad_in.astype(jnp.bfloat16), "pipe", -1)
        grads_in = store_slot(grads_in, slot_index, is_valid, grad_in)
        weight_sum = jax.tree.map(jnp.add, weight_sum, weight_grads)
        vector_sum = jax.tree.map(jnp.add, vector_sum, vector_grads)
        return ((passed, grads_in, weight_sum, vector_sum), None)

    backward_out, unused_two = lax.scan(
        backward_tick, (zero_rows, grads_init, weight_acc, vector_acc), tick_range
    )
    unused_grad, grads_in, weight_acc, vector_acc = backward_out
    weight_out = reduce_end(weight_acc)
    split_out = lax.psum((vector_acc[2], vector_acc[3], vector_acc[7]), "row")
    whole_out = lax.psum(
        (vector_acc[0], vector_acc[1], vector_acc[4], vector_acc[5], vector_acc[6], vector_acc[8]),
        ("row", "col"),
    )
    return (
        outputs[None, :, None],
        grads_in[None, :, None],
        whole_out[0][None],
        whole_out[1][None],
        weight_out[0][None],
        split_out[0][None],
        split_out[1][None],
        weight_out[1][None],
        whole_out[2][None],
        whole_out[3][None],
        whole_out[4][None],
        weight_out[2][None],
        split_out[2][None],
        weight_out[3][None],
        whole_out[5][None],
    )


def contract(left, right, left_dim, right_dim):
    return lax.dot_general(
        left, right, (((left_dim,), (right_dim,)), ((), ())), preferred_element_type=jnp.float32
    )


TILE = 256
CHUNK = 512
LANES = 2 * HD
VMEM_BYTES = 60 * 1024 * 1024
ERFC_SCALE = 0.4
ERFC_TERMS = (
    0.23192221664065504,
    0.1618227850291895,
    0.4682761333792345,
    -0.37091039694171485,
    0.7091488547855423,
    -0.20025962054546065,
)


def gelu_and_slope(values):
    size = jnp.abs(values) * math.sqrt(0.5)
    turn = 1.0 / (1.0 + ERFC_SCALE * size)
    series = ERFC_TERMS[-1]
    for term in ERFC_TERMS[-2::-1]:
        series = series * turn + term
    bell = jnp.exp(-(size * size))
    tail = 0.5 * (series * turn * bell)
    below = jnp.where(values >= 0.0, 1.0 - tail, tail)
    return (values * below, below + values * bell * (1.0 / math.sqrt(2.0 * math.pi)))


def norm_rows(values):
    centered = values - jnp.mean(values, axis=-1, keepdims=True)
    inv_std = lax.rsqrt(jnp.mean(centered * centered, axis=-1, keepdims=True) + epsilon)
    return (centered * inv_std, inv_std)


def norm_rows_backward(grad, centered, inv_std, gain):
    scaled = grad * gain
    first = jnp.mean(scaled, axis=-1, keepdims=True)
    second = jnp.mean(scaled * centered, axis=-1, keepdims=True)
    return inv_std * (scaled - first - centered * second)


def tile_rows(index):
    return pl.ds(pl.multiple_of(index * TILE, TILE), TILE)


def lane_block(start):
    return pl.ds(pl.multiple_of(start, LANES), LANES)


class Sizes:
    def __init__(self, frames, features, width, hidden, depth):
        self.frames = frames
        self.half = frames // 2
        self.features = features
        self.width = width
        self.hidden = hidden
        self.depth = depth
        self.block = features // (2 * depth)
        self.tiles = frames // TILE
        self.per = width // LANES
        self.tails = 6 * features
        self.tail = 2 * width + hidden
        self.vector = self.tails + self.tail
        self.sums = self.tails + 2 * self.tail
        self.early = (2 * depth, self.block, 4 * width)
        self.late = (2 * depth, self.block, 2 * hidden)


class Wires:
    def __init__(self, sizes, send, recv):
        self.depth = sizes.depth
        self.send, self.recv = (send, recv)
        self.used = 0
        self.pipe = lax.axis_index("pipe")
        self.row = lax.axis_index("row")
        self.col = lax.axis_index("col")
        self.plane = lax.div(self.row, 2)
        self.core = lax.rem(self.row, 2)
        self.place = 2 * self.pipe + self.col
        self.across_x = (1 - self.pipe, self.row, self.col)
        self.across_y = (self.pipe, self.row, 1 - self.col)
        self.across_both = (1 - self.pipe, self.row, 1 - self.col)
        self.across_core = (self.pipe, 2 * self.plane + 1 - self.core, self.col)

    def plane_at(self, step):
        return lax.rem(self.plane + step, self.depth)

    def along_z(self, step):
        return (self.pipe, 2 * self.plane_at(step) + self.core, self.col)

    def greet(self):
        barrier = pltpu.get_barrier_semaphore()
        partners = [self.across_x, self.across_y, self.across_both, self.across_core]
        partners += [self.along_z(step) for step in range(1, self.depth)]
        for partner in partners:
            pl.semaphore_signal(
                barrier, inc=1, device_id=partner, device_id_type=pl.DeviceIdType.MESH
            )
        pl.semaphore_wait(barrier, len(partners))

    def copy(self, source, target, partner):
        number = self.used
        self.used += 1
        return pltpu.make_async_remote_copy(
            src_ref=source,
            dst_ref=target,
            send_sem=self.send.at[number],
            recv_sem=self.recv.at[number],
            device_id=partner,
            device_id_type=pl.DeviceIdType.MESH,
        )


class Local:
    def __init__(self, sems):
        self.sems = sems
        self.used = 0
        self.open = []

    def start(self, source, target):
        copy = pltpu.make_async_copy(source, target, self.sems.at[self.used])
        self.used += 1
        copy.start()
        return copy

    def keep(self, source, target):
        self.open.append(self.start(source, target))

    def finish(self):
        for copy in self.open:
            copy.wait()


def whole_weight(weights, index, start, size):
    depth = weights.shape[1] // 2
    columns = slice(start, start + size)
    return jnp.concatenate(
        [
            weights[index, core * depth + plane, :, columns]
            for plane in range(depth)
            for core in range(2)
        ],
        axis=0,
    )


def attention_forward(sizes, part, qkv, context, lse, between):
    width = sizes.width
    score_scale = 1.0 / math.sqrt(HD)

    def one_pair(index, carry):
        pair = part * sizes.per + index
        base = part * (3 * width) + index * LANES
        for start in range(0, sizes.frames, TILE):
            rows = slice(start, start + TILE)
            query_pair = qkv[rows, lane_block(base)]
            key_pair = qkv[:, lane_block(base + width)]
            value_pair = qkv[:, lane_block(base + 2 * width)]
            parts = []
            for head in range(2):
                lanes = slice(head * HD, (head + 1) * HD)
                scaled = query_pair[:, lanes] * jnp.asarray(score_scale, jnp.bfloat16)
                scores = contract(key_pair[:, lanes], scaled, 1, 1)
                top = jnp.max(scores, axis=0, keepdims=True)
                weights = jnp.exp(scores - top)
                total = jnp.sum(weights, axis=0, keepdims=True)
                mixed = contract(value_pair[:, lanes], weights.astype(jnp.bfloat16), 0, 0)
                parts.append(mixed / total)
                lse[pair, head : head + 1, rows] = top + jnp.log(total)
            both = jnp.concatenate(parts, axis=0)
            context[rows, lane_block(pair * LANES)] = both.T.astype(jnp.bfloat16)
        pl.when(index == 0)(between)
        return carry

    lax.fori_loop(0, sizes.per, one_pair, 0)


def attention_backward(
    sizes, part, qkv, grad_context, lse, add_query_bias, add_value_bias, between
):
    width = sizes.width
    score_scale = 1.0 / math.sqrt(HD)

    def one_pair(index, carry):
        pair = part * sizes.per + index
        base = part * (3 * width) + index * LANES
        key_pair = qkv[:, lane_block(base + width)]
        value_pair = qkv[:, lane_block(base + 2 * width)]
        grad_keys = [None, None]
        grad_values = [None, None]
        query_total = jnp.zeros((1, LANES), jnp.float32)
        for start in range(0, sizes.frames, TILE):
            rows = slice(start, start + TILE)
            query_pair = qkv[rows, lane_block(base)]
            grad_pair = grad_context[rows, lane_block(pair * LANES)]
            parts = []
            for head in range(2):
                lanes = slice(head * HD, (head + 1) * HD)
                keys = key_pair[:, lanes]
                grads = grad_pair[:, lanes]
                scaled = query_pair[:, lanes] * jnp.asarray(score_scale, jnp.bfloat16)
                scores = contract(keys, scaled, 1, 1)
                probs = jnp.exp(scores - lse[pair, head : head + 1, rows])
                grad_probs = contract(value_pair[:, lanes], grads, 1, 1)
                delta = jnp.sum(probs * grad_probs, axis=0, keepdims=True)
                low_scores = (probs * (grad_probs - delta)).astype(jnp.bfloat16)
                value_part = contract(probs.astype(jnp.bfloat16), grads, 1, 0)
                key_part = contract(low_scores, scaled, 1, 0)
                grad_values[head] = value_part if start == 0 else grad_values[head] + value_part
                grad_keys[head] = key_part if start == 0 else grad_keys[head] + key_part
                parts.append(contract(keys, low_scores, 0, 0))
            turned = jnp.concatenate(parts, axis=0).T * score_scale
            query_total = query_total + jnp.sum(turned, axis=0, keepdims=True)
            qkv[rows, lane_block(base)] = turned.astype(jnp.bfloat16)
        key_grad = jnp.concatenate(grad_keys, axis=1)
        value_grad = jnp.concatenate(grad_values, axis=1)
        qkv[:, lane_block(base + width)] = key_grad.astype(jnp.bfloat16)
        qkv[:, lane_block(base + 2 * width)] = value_grad.astype(jnp.bfloat16)
        add_query_bias(part, index, query_total)
        add_value_bias(part, index, jnp.sum(value_grad, axis=0, keepdims=True))
        pl.when(index == 0)(between)
        return carry

    lax.fori_loop(0, sizes.per, one_pair, 0)


def vector_reader(sizes, vectors, layer):
    features = sizes.features

    def whole(index):
        return vectors[2 * layer, :, index * features : (index + 1) * features]

    def split(part, start, size):
        first = sizes.tails + start
        return vectors[2 * layer + part, :, first : first + size]

    return (whole, split)


def forward_norm(sizes, layer, values, vectors, normed):
    whole, split = vector_reader(sizes, vectors, layer)

    def one_tile(index, carry):
        rows = tile_rows(index)
        centered, unused = norm_rows(values[rows, :].astype(jnp.float32))
        normed[rows, :] = (centered * whole(0) + whole(1)).astype(jnp.bfloat16)
        return carry

    lax.fori_loop(0, sizes.tiles, one_tile, 0)


def forward_qkv(sizes, layer, part, normed, early, vectors, qkv):
    width = sizes.width
    whole, split = vector_reader(sizes, vectors, layer)

    def one_tile(index, carry):
        rows = tile_rows(index)
        for kind in range(3):
            result = contract(
                normed[rows, :], whole_weight(early, 2 * layer + part, kind * width, width), 1, 0
            )
            if kind == 0:
                result = result + split(part, 0, width)
            if kind == 2:
                result = result + split(part, width, width)
            columns = pl.ds(pl.multiple_of((3 * part + kind) * width, width), width)
            qkv[rows, columns] = result.astype(jnp.bfloat16)
        return carry

    lax.fori_loop(0, sizes.tiles, one_tile, 0)


def forward_rest(
    sizes, layer, values, early, late, vectors, context, hidden, active, slope, output, between
):
    width, size = (sizes.width, sizes.hidden)
    whole, split = vector_reader(sizes, vectors, layer)

    def one_tile(index, carry):
        rows = tile_rows(index)
        total = values[rows, :].astype(jnp.float32) + whole(2)
        for part in range(2):
            total = total + contract(
                context[rows, part * width : (part + 1) * width],
                whole_weight(early, 2 * layer + part, 3 * width, width),
                1,
                1,
            )
        hidden[rows, :] = total
        centered, unused = norm_rows(total)
        normed = (centered * whole(3) + whole(4)).astype(jnp.bfloat16)
        total = total + whole(5)
        for part in range(2):
            for start in range(0, size, CHUNK):
                weights = late.at[2 * layer + part]
                pre_act = contract(
                    normed, whole_weight(late, 2 * layer + part, start, CHUNK), 1, 0
                ) + split(part, 2 * width + start, CHUNK)
                act, act_slope = gelu_and_slope(pre_act)
                act = act.astype(jnp.bfloat16)
                first = part * size + start
                active[rows, first : first + CHUNK] = act
                slope[rows, first : first + CHUNK] = act_slope.astype(jnp.bfloat16)
                total = total + contract(
                    act, whole_weight(late, 2 * layer + part, size + start, CHUNK), 1, 1
                )
        output[rows, :] = total.astype(jnp.bfloat16)
        pl.when(index == 1)(between)
        return carry

    lax.fori_loop(0, sizes.tiles, one_tile, 0)


class Gather:
    def __init__(self, wires, block, full):
        self.wires, self.block, self.full = (wires, block, full)
        depth = wires.depth
        slot = wires.core * depth + wires.plane

        def one(layer):
            return full.at[2 * layer + wires.col, slot]

        def send(rows, partner):
            return wires.copy(rows, rows, partner)

        self.own = (2 * wires.pipe + wires.col, slot)
        self.x = wires.copy(block, one(wires.pipe), wires.across_x)
        self.z, self.k, self.y, self.k2 = ([], [], [], [])
        core_rows = pl.ds(wires.core * depth, depth)
        for layer in range(2):
            self.z.append(
                [send(one(layer), wires.along_z(step)) for step in range(1, depth)]
            )
            rows = full.at[2 * layer + wires.col, core_rows]
            self.k.append(send(rows, wires.across_core))
            self.y.append(send(rows, wires.across_y))
            rows = full.at[2 * layer + 1 - wires.col, core_rows]
            self.k2.append(send(rows, wires.across_core))

    def place_own(self):
        self.full[self.own] = self.block[...]

    def start_z(self, layer):
        for copy in self.z[layer]:
            copy.start()

    def end_z(self, layer):
        for copy in self.z[layer]:
            copy.wait_recv()
        self.k[layer].start()
        self.y[layer].start()

    def end_y(self, layer):
        self.y[layer].wait_recv()
        self.k2[layer].start()

    def finish(self):
        for copy in [self.x] + self.z[0] + self.z[1] + self.k + self.y + self.k2:
            copy.wait_send()


def forward_kernel(
    sizes,
    inputs_ref,
    cot_ref,
    early_block,
    late_block,
    vector_block,
    sent_ref,
    final_ref,
    lse_ref,
    x_out,
    cot_out,
    early_out,
    late_out,
    vector_out,
    qkv_out,
    context_out,
    hidden_out,
    active_out,
    slope_out,
    qkv,
    context,
    hidden,
    active,
    slope,
    x,
    cot,
    early,
    late,
    vectors,
    normed,
    send,
    recv,
    sems,
):
    half = sizes.half
    wires = Wires(sizes, send, recv)
    local = Local(sems)
    own_rows = pl.ds(pl.multiple_of(wires.col * half, half), half)
    other_place = 2 * wires.pipe + 1 - wires.col
    own_x = local.start(inputs_ref.at[wires.place, 0], x.at[own_rows])
    own_cot = local.start(cot_ref.at[wires.place, 0], cot.at[own_rows])
    early_gather = Gather(wires, early_block, early)
    late_gather = Gather(wires, late_block, late)
    early_gather.place_own()
    late_gather.place_own()
    vectors[wires.place] = vector_block[...]
    wires.greet()
    early_gather.x.start()
    vector_copies = [
        wires.copy(vector_block, vectors.at[wires.place], partner)
        for partner in (wires.across_x, wires.across_y, wires.across_both)
    ]
    for copy in vector_copies:
        copy.start()
    x_copy = wires.copy(inputs_ref.at[other_place, 0], x.at[own_rows], wires.across_y)
    x_copy.start()
    late_gather.x.start()
    early_gather.x.wait_recv()
    early_gather.start_z(0)
    cot_copy = wires.copy(cot_ref.at[other_place, 0], cot.at[own_rows], wires.across_y)
    cot_copy.start()
    own_x.wait()
    x_copy.wait_recv()
    for copy in vector_copies:
        copy.wait_recv()
    forward_norm(sizes, 0, x, vectors, normed)
    early_gather.end_z(0)
    late_gather.x.wait_recv()
    late_gather.start_z(0)
    local.keep(x, x_out)

    def no_wait():
        pass

    for layer in range(2):
        values = (x, sent_ref)[layer]
        output = (sent_ref, final_ref)[layer]
        if layer == 1:
            forward_norm(sizes, 1, values, vectors, normed)
        early_gather.k[layer].wait_recv()
        forward_qkv(sizes, layer, wires.col, normed, early, vectors, qkv.at[layer])
        between = [functools.partial(early_gather.end_y, 0), functools.partial(late_gather.end_y, 0)]
        if layer == 1:
            between = [functools.partial(late_gather.end_y, 1), no_wait]
        attention_forward(
            sizes, wires.col, qkv.at[layer], context.at[layer], lse_ref.at[layer], between[0]
        )
        if layer == 0:
            late_gather.end_z(0)
            early_gather.start_z(1)
        early_gather.k2[layer].wait_recv()
        forward_qkv(sizes, layer, 1 - wires.col, normed, early, vectors, qkv.at[layer])
        local.keep(qkv.at[layer], qkv_out.at[layer])
        attention_forward(
            sizes, 1 - wires.col, qkv.at[layer], context.at[layer], lse_ref.at[layer], between[1]
        )
        local.keep(context.at[layer], context_out.at[layer])
        if layer == 0:
            early_gather.end_z(1)
            late_gather.start_z(1)
        late_gather.k[layer].wait_recv()
        late_gather.k2[layer].wait_recv()
        forward_rest(
            sizes,
            layer,
            values,
            early,
            late,
            vectors,
            context.at[layer],
            hidden.at[layer],
            active.at[layer],
            slope.at[layer],
            output,
            functools.partial(early_gather.end_y, 1) if layer == 0 else no_wait,
        )
        local.keep(hidden.at[layer], hidden_out.at[layer])
        local.keep(active.at[layer], active_out.at[layer])
        local.keep(slope.at[layer], slope_out.at[layer])
        both = pl.ds(2 * layer, 2)
        local.keep(early.at[both], early_out.at[both])
        local.keep(late.at[both], late_out.at[both])
        if layer == 0:
            late_gather.end_z(1)
            own_cot.wait()
            cot_copy.wait_recv()
            local.keep(cot, cot_out)
    vector_out[...] = vectors[...]
    for copy in vector_copies + [x_copy, cot_copy]:
        copy.wait_send()
    early_gather.finish()
    late_gather.finish()
    local.finish()


def saved_shapes(sizes):
    frames, features = (sizes.frames, sizes.features)
    return [
        ((2, frames, 6 * sizes.width), jnp.bfloat16),
        ((2, frames, 2 * sizes.width), jnp.bfloat16),
        ((2, frames, features), jnp.float32),
        ((2, frames, 2 * sizes.hidden), jnp.bfloat16),
        ((2, frames, 2 * sizes.hidden), jnp.bfloat16),
    ]


def run_forward(sizes, inputs, cot, early_block, late_block, vector_block):
    frames, features = (sizes.frames, sizes.features)
    vmem = pl.BlockSpec(memory_space=pltpu.VMEM)
    hbm = pl.BlockSpec(memory_space=pl.ANY)
    saved = saved_shapes(sizes)
    low = jnp.bfloat16
    rows = ((frames, features), low)
    early, late = (((4,) + sizes.early, low), ((4,) + sizes.late, low))
    vectors = ((4, 1, sizes.vector), jnp.float32)
    outs = [rows, rows, ((2, 2 * sizes.per, 2, frames), jnp.float32)]
    outs += [rows, rows, early, late, vectors] + saved
    count = 2 * (1 + 2 * (sizes.depth - 1) + 6) + 5
    return pl.pallas_call(
        functools.partial(forward_kernel, sizes),
        in_specs=[hbm, hbm, vmem, vmem, vmem],
        out_specs=[vmem] * 3 + [hbm] * 4 + [vmem] + [hbm] * 5,
        out_shape=[jax.ShapeDtypeStruct(shape, dtype) for shape, dtype in outs],
        scratch_shapes=[
            pltpu.VMEM(shape, dtype)
            for shape, dtype in saved + [rows, rows, early, late, vectors, rows]
        ]
        + [
            pltpu.SemaphoreType.DMA((count,)),
            pltpu.SemaphoreType.DMA((count,)),
            pltpu.SemaphoreType.DMA((18,)),
        ],
        compiler_params=pltpu.CompilerParams(
            vmem_limit_bytes=VMEM_BYTES, collective_id=0, has_side_effects=True
        ),
        name="layers_forward",
    )(inputs, cot, early_block, late_block, vector_block)


def add_row(sums, layer, start, value):
    where = (layer, slice(None), slice(start, start + value.shape[1]))
    sums[where] = sums[where] + value


def column_sum(values):
    return jnp.sum(values, axis=0, keepdims=True)


def put_block(target, part, start, value):
    depth, block = (target.shape[1] // 2, target.shape[2])
    low = value.astype(jnp.bfloat16)
    for row in range(2 * depth):
        target[part, (row % 2) * depth + row // 2, :, start : start + value.shape[1]] = low[
            row * block : (row + 1) * block
        ]


def backward_mlp(
    sizes,
    layer,
    hidden,
    active,
    slope,
    late,
    vectors,
    grad,
    sums,
    normed_t,
    grad_t,
    grad_late,
    between,
    after_rows,
):
    features, width, size = (sizes.features, sizes.width, sizes.hidden)
    whole, split = vector_reader(sizes, vectors, layer)

    def one_tile(index, carry):
        rows = tile_rows(index)
        grad_out = grad[rows, :]
        add_row(sums, layer, 5 * features, column_sum(grad_out))
        grad_low = grad_out.astype(jnp.bfloat16)
        grad_t[:, rows] = grad_low.T
        centered, inv_std = norm_rows(hidden[rows, :])
        normed_t[:, rows] = (centered * whole(3) + whole(4)).astype(jnp.bfloat16).T
        grad_normed = jnp.zeros((TILE, features), jnp.float32)
        for part in range(2):
            for start in range(0, size, CHUNK):
                first = part * size + start
                grad_act = contract(grad_low, whole_weight(late, part, size + start, CHUNK), 1, 0)
                grad_pre = grad_act * slope[rows, first : first + CHUNK].astype(jnp.float32)
                add_row(
                    sums,
                    layer,
                    sizes.tails + part * sizes.tail + 2 * width + start,
                    column_sum(grad_pre),
                )
                low = grad_pre.astype(jnp.bfloat16)
                slope[rows, first : first + CHUNK] = low
                grad_normed = grad_normed + contract(
                    low, whole_weight(late, part, start, CHUNK), 1, 1
                )
        add_row(sums, layer, 3 * features, column_sum(grad_normed * centered))
        add_row(sums, layer, 4 * features, column_sum(grad_normed))
        grad_hidden = grad_out + norm_rows_backward(grad_normed, centered, inv_std, whole(3))
        add_row(sums, layer, 2 * features, column_sum(grad_hidden))
        grad[rows, :] = grad_hidden
        pl.when(index == 1)(between)
        return carry

    lax.fori_loop(0, sizes.tiles, one_tile, 0)
    after_rows()
    for part in range(2):
        for start in range(0, size, 256):
            first = part * size + start
            up = contract(normed_t[...], slope[:, first : first + 256], 1, 0)
            put_block(grad_late, part, start, up)
            down = contract(grad_t[...], active[:, first : first + 256], 1, 0)
            put_block(grad_late, part, size + start, down)


def backward_context(
    sizes, layer, values, early, vectors, grad, normed_t, grad_t, grad_context
):
    width = sizes.width
    whole, split = vector_reader(sizes, vectors, layer)

    def to_context(index, carry):
        rows = tile_rows(index)
        low = grad[rows, :].astype(jnp.bfloat16)
        grad_t[:, rows] = low.T
        for part in range(2):
            grad_context[rows, part * width : (part + 1) * width] = contract(
                low, whole_weight(early, part, 3 * width, width), 1, 0
            ).astype(jnp.bfloat16)
        centered, unused = norm_rows(values[rows, :].astype(jnp.float32))
        normed_t[:, rows] = (centered * whole(0) + whole(1)).astype(jnp.bfloat16).T
        return carry

    lax.fori_loop(0, sizes.tiles, to_context, 0)


def backward_early_weights(sizes, qkv, context, normed_t, grad_t, grad_early):
    width = sizes.width
    for part in range(2):
        for kind in range(3):
            first = (3 * part + kind) * width
            result = contract(normed_t[...], qkv[:, first : first + width], 1, 0)
            put_block(grad_early, part, kind * width, result)
        result = contract(grad_t[...], context[:, part * width : (part + 1) * width], 1, 0)
        put_block(grad_early, part, 3 * width, result)


def backward_input(sizes, layer, values, qkv, early, vectors, grad, sums, grad_in):
    features, width = (sizes.features, sizes.width)
    whole, split = vector_reader(sizes, vectors, layer)

    def to_input(index, carry):
        rows = tile_rows(index)
        grad_normed = jnp.zeros((TILE, features), jnp.float32)
        for part in range(2):
            grad_normed = grad_normed + contract(
                qkv[rows, part * 3 * width : (part + 1) * 3 * width],
                whole_weight(early, part, 0, 3 * width),
                1,
                1,
            )
        centered, inv_std = norm_rows(values[rows, :].astype(jnp.float32))
        add_row(sums, layer, 0, column_sum(grad_normed * centered))
        add_row(sums, layer, features, column_sum(grad_normed))
        low = (
            grad[rows, :] + norm_rows_backward(grad_normed, centered, inv_std, whole(0))
        ).astype(jnp.bfloat16)
        grad_in[rows, :] = low
        grad[rows, :] = low.astype(jnp.float32)
        return carry

    lax.fori_loop(0, sizes.tiles, to_input, 0)


def add_low(left, right):
    return (left.astype(jnp.float32) + right.astype(jnp.float32)).astype(jnp.bfloat16)


class Reduce:
    def __init__(self, wires, grads, from_core, from_y, from_z, total, low, from_x):
        self.wires, self.grads = (wires, grads)
        self.from_core, self.from_y, self.from_z = (from_core, from_y, from_z)
        self.total, self.from_x, self.low = (total, from_x, low)
        depth = wires.depth
        rows = pl.ds((1 - wires.core) * depth, depth)
        self.core, self.y, self.z = ([], [], [])
        for layer in range(2):
            self.core.append(
                wires.copy(grads.at[:, rows], from_core.at[layer], wires.across_core)
            )
            self.y.append(
                wires.copy(from_core.at[layer, 1 - wires.col], from_y.at[layer], wires.across_y)
            )
            self.z.append(
                [
                    wires.copy(
                        from_y.at[layer, wires.plane_at(step)],
                        from_z.at[layer, wires.plane],
                        wires.along_z(step),
                    )
                    for step in range(1, depth)
                ]
            )
        self.x = wires.copy(low.at[1 - wires.pipe], from_x, wires.across_x)

    def end_core(self, layer):
        wires, held = (self.wires, self.from_core)
        self.core[layer].wait()

        def add(part):
            def one(plane, carry):
                held[layer, part, plane] = add_low(
                    held[layer, part, plane],
                    self.grads[part, wires.core * wires.depth + plane],
                )
                return carry

            lax.fori_loop(0, wires.depth, one, 0)

        add(1 - wires.col)
        self.y[layer].start()
        add(wires.col)

    def end_y(self, layer):
        wires, held = (self.wires, self.from_y)
        self.y[layer].wait_recv()

        def one(plane, carry):
            held[layer, plane] = add_low(
                held[layer, plane], self.from_core[layer, wires.col, plane]
            )
            return carry

        lax.fori_loop(0, wires.depth, one, 0)
        for copy in self.z[layer]:
            copy.start()

    def end_z(self, layer):
        wires = self.wires
        for copy in self.z[layer]:
            copy.wait_recv()
        total = self.from_y[layer, wires.plane].astype(jnp.float32)
        for step in range(1, wires.depth):
            total = total + self.from_z[layer, wires.plane_at(step)].astype(jnp.float32)
        self.total[layer] = total
        self.low[layer] = total.astype(jnp.bfloat16)

    def end_x(self, target):
        self.x.wait()
        target[...] = self.total[self.wires.pipe] + self.from_x[...].astype(jnp.float32)
        for layer in range(2):
            for copy in [self.y[layer]] + self.z[layer]:
                copy.wait_send()


class ReduceSums:
    def __init__(self, wires, sums, second, third, from_all, from_x):
        self.wires = wires
        self.stages = (sums, second, third)
        self.from_all, self.from_x = (from_all, from_x)
        self.core, self.y, self.z = ([], [], [])
        for layer in range(2):
            self.core.append(
                wires.copy(sums.at[layer], from_all.at[layer, 0], wires.across_core)
            )
            self.y.append(wires.copy(second.at[layer], from_all.at[layer, 1], wires.across_y))
            self.z.append(
                [
                    wires.copy(
                        third.at[layer], from_all.at[layer, 2 + wires.plane], wires.along_z(step)
                    )
                    for step in range(1, wires.depth)
                ]
            )
        self.x = wires.copy(sums.at[1 - wires.pipe], from_x, wires.across_x)

    def end_core(self, layer):
        self.core[layer].wait()
        self.stages[1][layer] = self.stages[0][layer] + self.from_all[layer, 0]
        self.y[layer].start()

    def end_y(self, layer):
        self.y[layer].wait()
        self.stages[2][layer] = self.stages[1][layer] + self.from_all[layer, 1]
        for copy in self.z[layer]:
            copy.start()

    def end_z(self, layer):
        wires = self.wires
        for copy in self.z[layer]:
            copy.wait()
        self.from_all[layer, 2 + wires.plane] = self.stages[2][layer]
        total = self.from_all[layer, 2]
        for plane in range(1, wires.depth):
            total = total + self.from_all[layer, 2 + plane]
        self.stages[0][layer] = total

    def end_x(self, target):
        self.x.wait()
        target[...] = self.stages[0][self.wires.pipe] + self.from_x[...]


class Trade:
    def __init__(self, sizes, wires, local, layer, source, target):
        half = sizes.half
        self.wires, self.layer = (wires, layer)
        self.copies = []
        for step in range(1, 4):
            pipe = wires.pipe if step < 2 else 1 - wires.pipe
            col = wires.col if step == 2 else 1 - wires.col
            rows = pl.ds(pl.multiple_of(col * half, half), half)
            copy = wires.copy(
                source.at[rows], target.at[wires.place], (pipe, wires.row, col)
            )
            self.copies.append((pipe == layer, copy))
        rows = pl.ds(pl.multiple_of(wires.col * half, half), half)
        self.own = pltpu.make_async_copy(
            source.at[rows], target.at[wires.place], local.sems.at[local.used]
        )
        local.used += 1

    def start(self):
        for wanted, copy in self.copies:
            pl.when(wanted)(copy.start)
        pl.when(self.wires.pipe == self.layer)(self.own.start)

    def finish(self):
        for wanted, copy in self.copies:
            pl.when(wanted)(copy.wait_send)

        def arrive():
            self.own.wait()
            for wanted, copy in self.copies:
                copy.wait_recv()

        pl.when(self.wires.pipe == self.layer)(arrive)


def backward_kernel(
    sizes,
    live_ref,
    cot_ref,
    x_ref,
    sent_ref,
    final_ref,
    vectors,
    lse_ref,
    early_in,
    late_in,
    qkv_in,
    context_in,
    hidden_in,
    active_in,
    slope_in,
    states_out,
    grads_out,
    sums_out,
    early_out,
    late_out,
    qkv,
    context,
    hidden,
    active,
    slope,
    early,
    late,
    mid,
    first,
    values,
    grad,
    normed_t,
    grad_t,
    grad_context,
    grad_early,
    grad_late,
    early_core,
    early_y,
    early_z,
    early_total,
    early_low,
    early_x,
    late_core,
    late_y,
    late_z,
    late_total,
    late_low,
    late_x,
    sums,
    sums_second,
    sums_third,
    sums_all,
    sums_x,
    send,
    recv,
    sems,
):
    wires = Wires(sizes, send, recv)
    local = Local(sems)

    def load(source, target, layer):
        return local.start(source.at[layer], target)

    def load_pair(source, target, layer):
        return local.start(source.at[pl.ds(2 * layer, 2)], target)

    cot_copy = local.start(cot_ref, first)
    late_copy = load_pair(late_in, late, 1)
    slope_copy = load(slope_in, slope, 1)
    hidden_copy = load(hidden_in, hidden, 1)
    active_copy = load(active_in, active, 1)
    early_copy = load_pair(early_in, early, 1)
    attention_copies = [
        load(qkv_in, qkv, 1),
        load(context_in, context, 1),
        local.start(sent_ref, values),
    ]
    sums[...] = jnp.zeros_like(sums)
    wires.greet()
    trades = [
        Trade(sizes, wires, local, layer, source, states_out)
        for layer, source in enumerate((sent_ref, final_ref))
    ]
    for trade in trades:
        trade.start()
    cot_copy.wait()
    grad[...] = first[...].astype(jnp.float32) * live_ref[0, 0]
    early_sum = Reduce(
        wires, grad_early, early_core, early_y, early_z, early_total, early_low, early_x
    )
    late_sum = Reduce(wires, grad_late, late_core, late_y, late_z, late_total, late_low, late_x)
    small_sum = ReduceSums(wires, sums, sums_second, sums_third, sums_all, sums_x)

    def no_wait():
        pass

    def after_mlp_rows():
        late_sum.end_z(1)
        early_sum.end_y(1)
        small_sum.end_y(1)

    for layer in (1, 0):
        late_copy.wait()
        slope_copy.wait()
        hidden_copy.wait()
        active_copy.wait()
        backward_mlp(
            sizes,
            layer,
            hidden,
            active,
            slope,
            late,
            vectors,
            grad,
            sums,
            normed_t,
            grad_t,
            grad_late,
            no_wait,
            no_wait if layer == 1 else after_mlp_rows,
        )
        late_sum.core[layer].start()
        if layer == 1:
            late_copy = load_pair(late_in, late, 0)
            slope_copy = load(slope_in, slope, 0)
            hidden_copy = load(hidden_in, hidden, 0)
            active_copy = load(active_in, active, 0)
        early_copy.wait()
        for copy in attention_copies:
            copy.wait()
        backward_context(
            sizes, layer, values, early, vectors, grad, normed_t, grad_t, grad_context
        )

        def add_bias(offset):
            def add(part, index, value):
                start = sizes.tails + part * sizes.tail + offset + index * LANES
                where = (layer, slice(None), lane_block(start))
                sums[where] = sums[where] + value

            return add

        attention_backward(
            sizes,
            1 - wires.col,
            qkv,
            grad_context,
            lse_ref.at[layer],
            add_bias(0),
            add_bias(sizes.width),
            functools.partial(late_sum.end_core, layer),
        )
        if layer == 0:
            early_sum.end_z(1)
            small_sum.end_z(1)
        attention_backward(
            sizes,
            wires.col,
            qkv,
            grad_context,
            lse_ref.at[layer],
            add_bias(0),
            add_bias(sizes.width),
            no_wait,
        )
        late_sum.end_y(layer)
        backward_early_weights(sizes, qkv, context, normed_t, grad_t, grad_early)
        early_sum.core[layer].start()
        grad_in = (first, mid)[layer]
        backward_input(sizes, layer, values, qkv, early, vectors, grad, sums, grad_in)
        small_sum.core[layer].start()
        trades.append(Trade(sizes, wires, local, layer, grad_in, grads_out))
        trades[-1].start()
        early_sum.end_core(layer)
        small_sum.end_core(layer)
        if layer == 1:
            early_copy = load_pair(early_in, early, 0)
            attention_copies = [
                load(qkv_in, qkv, 0),
                load(context_in, context, 0),
                local.start(x_ref, values),
            ]
    early_sum.end_y(0)
    small_sum.end_y(0)
    late_sum.end_z(0)
    late_sum.x.start()
    early_sum.end_z(0)
    early_sum.x.start()
    small_sum.end_z(0)
    small_sum.x.start()
    late_sum.end_x(late_out)
    early_sum.end_x(early_out)
    small_sum.end_x(sums_out)
    for trade in trades:
        trade.finish()


def run_backward(sizes, live, cot, values, sent, final, vectors, lse, early, late, saved):
    frames, features, depth = (sizes.frames, sizes.features, sizes.depth)
    vmem = pl.BlockSpec(memory_space=pltpu.VMEM)
    hbm = pl.BlockSpec(memory_space=pl.ANY)
    smem = pl.BlockSpec(memory_space=pltpu.SMEM)
    low, high = (jnp.bfloat16, jnp.float32)

    def reduce_shapes(block):
        one = block[1:]
        return [
            ((2, 2, depth) + one, low),
            ((2, depth) + one, low),
            ((2, depth) + one, low),
            ((2,) + one, high),
            ((2,) + one, low),
            (one, low),
        ]

    row = (1, sizes.sums)
    scratch = [(shape[1:], dtype) for shape, dtype in saved_shapes(sizes)]
    scratch += [((2,) + sizes.early, low), ((2,) + sizes.late, low)]
    scratch += [((frames, features), low)] * 3 + [((frames, features), high)]
    scratch += [((features, frames), low)] * 2 + [((frames, 2 * sizes.width), low)]
    scratch += [((2,) + sizes.early, low), ((2,) + sizes.late, low)]
    scratch += reduce_shapes(sizes.early) + reduce_shapes(sizes.late)
    scratch += [((2,) + row, high)] * 3 + [((2, 2 + depth) + row, high), (row, high)]
    count = 12 + 2 * 3 * (2 + depth - 1) + 3
    return pl.pallas_call(
        functools.partial(backward_kernel, sizes),
        in_specs=[smem] + [hbm] * 4 + [vmem] * 2 + [hbm] * 7,
        out_specs=[hbm, hbm, vmem, vmem, vmem],
        out_shape=[
            jax.ShapeDtypeStruct((4, sizes.half, features), low),
            jax.ShapeDtypeStruct((4, sizes.half, features), low),
            jax.ShapeDtypeStruct(row, high),
            jax.ShapeDtypeStruct(sizes.early[1:], high),
            jax.ShapeDtypeStruct(sizes.late[1:], high),
        ],
        scratch_shapes=[pltpu.VMEM(shape, dtype) for shape, dtype in scratch]
        + [
            pltpu.SemaphoreType.DMA((count,)),
            pltpu.SemaphoreType.DMA((count,)),
            pltpu.SemaphoreType.DMA((21,)),
        ],
        compiler_params=pltpu.CompilerParams(
            vmem_limit_bytes=VMEM_BYTES, collective_id=1, has_side_effects=True
        ),
        name="layers_backward",
    )(live, cot, values, sent, final, vectors, lse, early, late, *saved)


def on_device_clip(
    inputs,
    first_gain,
    first_shift,
    qkv_weight,
    query_bias,
    value_bias,
    proj_weight,
    proj_bias,
    second_gain,
    second_shift,
    up_weight,
    up_bias,
    down_weight,
    down_bias,
    cotangent,
    live_clips,
):
    section, col = (lax.axis_index("pipe"), lax.axis_index("col"))
    place = 2 * section + col
    width, hidden_width = (qkv_weight.shape[3], up_weight.shape[2])
    features = inputs.shape[3]
    sizes = Sizes(
        2 * inputs.shape[2], features, width, hidden_width, lax.axis_size("row") // 2
    )
    early_block = jnp.concatenate(
        [qkv_weight[0, 0], qkv_weight[0, 1], qkv_weight[0, 2], proj_weight[0].T], axis=1
    )
    late_block = jnp.concatenate([up_weight[0], down_weight[0].T], axis=1)
    vector_block = jnp.concatenate(
        [
            first_gain[0],
            first_shift[0],
            proj_bias[0],
            second_gain[0],
            second_shift[0],
            down_bias[0],
            query_bias[0],
            value_bias[0],
            up_bias[0],
        ]
    )[None]
    live = lax.dynamic_slice(live_clips, (place, 0), (1, 1)).astype(jnp.float32)
    sent, final, lse, values, cot, early, late, vectors, *saved = run_forward(
        sizes, inputs, cotangent, early_block, late_block, vector_block
    )
    states, grads_in, sums, own_early, own_late = run_backward(
        sizes, live, cot, values, sent, final, vectors, lse, early, late, saved
    )
    split_out = lax.dynamic_slice(sums, (0, sizes.tails + col * sizes.tail), (1, sizes.tail))
    whole_out = [sums[:, index * features : (index + 1) * features] for index in range(6)]
    return (
        states[None, :, None],
        grads_in.astype(jnp.float32)[None, :, None],
        whole_out[0],
        whole_out[1],
        jnp.stack([own_early[:, part * width : (part + 1) * width] for part in range(3)])[None],
        split_out[:, :width],
        split_out[:, width : 2 * width],
        own_early[:, 3 * width :].T[None],
        whole_out[2],
        whole_out[3],
        whole_out[4],
        own_late[:, :hidden_width][None],
        split_out[:, 2 * width :],
        own_late[:, hidden_width:].T[None],
        whole_out[5],
    )


def one_clip_each(mesh):
    sizes = dict(mesh.shape)
    return sizes["pipe"] == 2 and sizes["col"] == 2


def choose(mesh):
    def body(*arrays):
        fits = one_clip_each(mesh) and arrays[0].shape[:2] == (4, 1)
        return (on_device_clip if fits else on_device)(*arrays)

    return body


def solution(mesh):
    placed = (
        P(None, "row", "col", None),
        P("pipe", None),
        P("pipe", None),
        P("pipe", None, "row", "col"),
        P("pipe", "col"),
        P("pipe", "col"),
        P("pipe", "col", "row"),
        P("pipe", None),
        P("pipe", None),
        P("pipe", None),
        P("pipe", "row", "col"),
        P("pipe", "col"),
        P("pipe", "col", "row"),
        P("pipe", None),
        P(None, "row", "col", None),
        P(None, "row"),
    )
    return jax.shard_map(
        choose(mesh),
        mesh=mesh,
        in_specs=placed,
        out_specs=(
            P("pipe", None, "row", "col", None),
            P("pipe", None, "row", "col", None),
            P("pipe", None),
            P("pipe", None),
            P("pipe", None, "row", "col"),
            P("pipe", "col"),
            P("pipe", "col"),
            P("pipe", "col", "row"),
            P("pipe", None),
            P("pipe", None),
            P("pipe", None),
            P("pipe", "row", "col"),
            P("pipe", "col"),
            P("pipe", "col", "row"),
            P("pipe", None),
        ),
        check_vma=False,
    )
```

```python
import functools
import math

import jax
import jax.numpy as jnp
from jax import lax
from jax.experimental import pallas as pl
from jax.experimental.pallas import tpu as pltpu
from jax.sharding import PartitionSpec as P

HD = 64


epsilon = 1e-05


def from_behind(value, axis, steps):
    count = lax.axis_size(axis)
    first, last = (max(0, -steps), min(count, count - steps))
    return lax.ppermute(value, axis, [(source, source + steps) for source in range(first, last)])


def exact_gelu(values):
    return jax.nn.gelu(values, approximate=False)


def spread_features(normed):
    return lax.all_gather(normed, "col", axis=0, tiled=True)


def sum_columns(partial_rows):
    return lax.psum_scatter(partial_rows, "col", scatter_dimension=0, tiled=True)


def spread_grads(grad_low):
    return lax.all_gather(grad_low, "col", axis=0, tiled=True)


def sum_grad_columns(partial_rows):
    return lax.psum_scatter(partial_rows, "col", scatter_dimension=0, tiled=True)


def norm_forward(values, gain, shift):
    row_mean = jnp.mean(values, axis=-1, keepdims=True)
    row_var = jnp.mean(jnp.square(values - row_mean), axis=-1, keepdims=True)
    inv_std = lax.rsqrt(row_var + epsilon)
    centered = (values - row_mean) * inv_std
    return (centered, inv_std[:, 0], (centered * gain + shift).astype(jnp.bfloat16))


def norm_backward(grad_norm, centered, inv_std, gain):
    grad_gain = jnp.sum(grad_norm * centered, axis=0)
    grad_shift = jnp.sum(grad_norm, axis=0)
    scaled = grad_norm * gain
    first = jnp.mean(scaled, axis=-1, keepdims=True)
    second = jnp.mean(scaled * centered, axis=-1, keepdims=True)
    grad_in = inv_std[:, None] * (scaled - first - centered * second)
    return (grad_in, grad_gain, grad_shift)


def attention_probs(query_heads, key_heads):
    score_scale = 1.0 / math.sqrt(HD)
    scores = (
        jnp.einsum("qhd,khd->hqk", query_heads, key_heads, preferred_element_type=jnp.float32)
        * score_scale
    )
    return jax.nn.softmax(scores, axis=-1)


def layer_forward(values, weights, params):
    qkv_full, proj_full, up_full, down_full = weights
    (
        gain_one,
        shift_one,
        query_bias,
        value_bias,
        proj_bias,
        gain_two,
        shift_two,
        up_bias,
        down_bias,
    ) = params
    head_count = qkv_full.shape[2] // HD
    centered_one, inv_one, normed_one = norm_forward(values, gain_one, shift_one)
    attn_input = spread_features(normed_one)
    frame_count = attn_input.shape[0]
    projected = jnp.einsum("sd,jde->jse", attn_input, qkv_full, preferred_element_type=jnp.float32)
    query_heads = (
        (projected[0] + query_bias).astype(jnp.bfloat16).reshape(frame_count, head_count, HD)
    )
    key_heads = projected[1].astype(jnp.bfloat16).reshape(frame_count, head_count, HD)
    value_heads = (
        (projected[2] + value_bias).astype(jnp.bfloat16).reshape(frame_count, head_count, HD)
    )
    softmax_out = attention_probs(query_heads, key_heads)
    context = jnp.einsum(
        "hqk,khd->qhd",
        softmax_out.astype(jnp.bfloat16),
        value_heads,
        preferred_element_type=jnp.float32,
    )
    context = context.reshape(frame_count, head_count * HD).astype(jnp.bfloat16)
    attended = (
        sum_columns(jnp.dot(context, proj_full, preferred_element_type=jnp.float32)) + proj_bias
    )
    hidden = values + attended
    centered_two, inv_two, normed_two = norm_forward(hidden, gain_two, shift_two)
    mlp_input = spread_features(normed_two)
    pre_act = jnp.dot(mlp_input, up_full, preferred_element_type=jnp.float32) + up_bias
    activated = exact_gelu(pre_act).astype(jnp.bfloat16)
    output = (
        hidden
        + sum_columns(jnp.dot(activated, down_full, preferred_element_type=jnp.float32))
        + down_bias
    )
    kept = (
        centered_one,
        inv_one,
        attn_input,
        query_heads,
        key_heads,
        value_heads,
        context,
        centered_two,
        inv_two,
        mlp_input,
        pre_act,
        activated,
    )
    return (output, kept)


def layer_backward(grad_out, kept, weights, params):
    qkv_full, proj_full, up_full, down_full = weights
    (
        gain_one,
        shift_one,
        query_bias,
        value_bias,
        proj_bias,
        gain_two,
        shift_two,
        up_bias,
        down_bias,
    ) = params
    (
        centered_one,
        inv_one,
        attn_input,
        query_heads,
        key_heads,
        value_heads,
        context,
        centered_two,
        inv_two,
        mlp_input,
        pre_act,
        activated,
    ) = kept
    frame_count = attn_input.shape[0]
    score_scale = 1.0 / math.sqrt(HD)
    grad_down_bias = jnp.sum(grad_out, axis=0)
    down_grad = spread_grads(grad_out.astype(jnp.bfloat16))
    grad_down = jnp.einsum("sf,sd->fd", activated, down_grad, preferred_element_type=jnp.float32)
    grad_act = jnp.einsum("sd,fd->sf", down_grad, down_full, preferred_element_type=jnp.float32)
    unused, gelu_pull = jax.vjp(exact_gelu, pre_act)
    grad_pre = gelu_pull(grad_act)[0]
    grad_up_bias = jnp.sum(grad_pre, axis=0)
    grad_pre_low = grad_pre.astype(jnp.bfloat16)
    grad_up = jnp.einsum("sd,sf->df", mlp_input, grad_pre_low, preferred_element_type=jnp.float32)
    grad_normed_two = sum_grad_columns(
        jnp.einsum("sf,df->sd", grad_pre_low, up_full, preferred_element_type=jnp.float32)
    )
    grad_hidden_norm, grad_gain_two, grad_shift_two = norm_backward(
        grad_normed_two, centered_two, inv_two, gain_two
    )
    grad_hidden = grad_out + grad_hidden_norm
    grad_proj_bias = jnp.sum(grad_hidden, axis=0)
    proj_grad = spread_grads(grad_hidden.astype(jnp.bfloat16))
    grad_proj = jnp.einsum("se,sd->ed", context, proj_grad, preferred_element_type=jnp.float32)
    grad_context = jnp.einsum("sd,ed->se", proj_grad, proj_full, preferred_element_type=jnp.float32)
    grad_context = grad_context.astype(jnp.bfloat16).reshape(query_heads.shape)
    softmax_out = attention_probs(query_heads, key_heads)
    grad_probs = jnp.einsum(
        "qhd,khd->hqk", grad_context, value_heads, preferred_element_type=jnp.float32
    )
    grad_value = jnp.einsum(
        "hqk,qhd->khd",
        softmax_out.astype(jnp.bfloat16),
        grad_context,
        preferred_element_type=jnp.float32,
    )
    grad_scores = softmax_out * (
        grad_probs - jnp.sum(softmax_out * grad_probs, axis=-1, keepdims=True)
    )
    scores_low = grad_scores.astype(jnp.bfloat16)
    grad_query = (
        jnp.einsum("hqk,khd->qhd", scores_low, key_heads, preferred_element_type=jnp.float32)
        * score_scale
    )
    grad_key = (
        jnp.einsum("hqk,qhd->khd", scores_low, query_heads, preferred_element_type=jnp.float32)
        * score_scale
    )
    grad_query = grad_query.reshape(frame_count, -1)
    grad_key = grad_key.reshape(frame_count, -1)
    grad_value = grad_value.reshape(frame_count, -1)
    grad_query_bias = jnp.sum(grad_query, axis=0)
    grad_value_bias = jnp.sum(grad_value, axis=0)
    grad_qkv_low = jnp.stack([grad_query, grad_key, grad_value]).astype(jnp.bfloat16)
    grad_qkv = jnp.einsum(
        "sd,jse->jde", attn_input, grad_qkv_low, preferred_element_type=jnp.float32
    )
    grad_normed_one = sum_grad_columns(
        jnp.einsum("jse,jde->sd", grad_qkv_low, qkv_full, preferred_element_type=jnp.float32)
    )
    grad_in_norm, grad_gain_one, grad_shift_one = norm_backward(
        grad_normed_one, centered_one, inv_one, gain_one
    )
    grad_in = grad_hidden + grad_in_norm
    weight_grads = (grad_qkv, grad_proj, grad_up, grad_down)
    vector_grads = (
        grad_gain_one,
        grad_shift_one,
        grad_query_bias,
        grad_value_bias,
        grad_proj_bias,
        grad_gain_two,
        grad_shift_two,
        grad_up_bias,
        grad_down_bias,
    )
    return (grad_in, weight_grads, vector_grads)


def store_slot(buffer, slot_index, is_valid, value):
    current = lax.dynamic_index_in_dim(buffer, slot_index, 0, keepdims=False)
    return lax.dynamic_update_index_in_dim(
        buffer, jnp.where(is_valid, value, current), slot_index, 0
    )


def reduce_end(weight_acc):
    return (
        lax.psum_scatter(
            weight_acc[0].astype(jnp.bfloat16), "row", scatter_dimension=1, tiled=True
        ).astype(jnp.float32),
        lax.psum_scatter(
            weight_acc[1].astype(jnp.bfloat16), "row", scatter_dimension=1, tiled=True
        ).astype(jnp.float32),
        lax.psum_scatter(
            weight_acc[2].astype(jnp.bfloat16), "row", scatter_dimension=0, tiled=True
        ).astype(jnp.float32),
        lax.psum_scatter(
            weight_acc[3].astype(jnp.bfloat16), "row", scatter_dimension=1, tiled=True
        ).astype(jnp.float32),
    )


def on_device(
    inputs,
    first_gain,
    first_shift,
    qkv_weight,
    query_bias,
    value_bias,
    proj_weight,
    proj_bias,
    second_gain,
    second_shift,
    up_weight,
    up_bias,
    down_weight,
    down_bias,
    cotangent,
    live_clips,
):
    micro_count = inputs.shape[0]
    row_count = inputs.shape[2]
    feature_count = inputs.shape[3]
    section_index = lax.axis_index("pipe")
    weights = (
        lax.all_gather(qkv_weight[0], "row", axis=1, tiled=True),
        lax.all_gather(proj_weight[0], "row", axis=1, tiled=True),
        lax.all_gather(up_weight[0], "row", axis=0, tiled=True),
        lax.all_gather(down_weight[0], "row", axis=1, tiled=True),
    )
    params = (
        first_gain[0],
        first_shift[0],
        query_bias[0],
        value_bias[0],
        proj_bias[0],
        second_gain[0],
        second_shift[0],
        up_bias[0],
        down_bias[0],
    )
    kept_buffers = ()
    zero_rows = jnp.zeros((row_count, feature_count), jnp.bfloat16)
    zero_stack = jnp.zeros((micro_count, row_count, feature_count), jnp.bfloat16)
    own_inputs = inputs[:, 0]

    def forward_tick(state_carry, tick_index):
        received, outputs, layer_inputs, buffers = state_carry
        batch_index = tick_index - section_index
        is_valid = (batch_index >= 0) & (batch_index < micro_count)
        slot_index = jnp.clip(batch_index, 0, micro_count - 1)
        own_input = lax.dynamic_index_in_dim(
            own_inputs, jnp.minimum(tick_index, micro_count - 1), 0, keepdims=False
        )
        layer_input = jnp.where(section_index == 0, own_input, received)
        output, kept = layer_forward(layer_input.astype(jnp.float32), weights, params)
        output_low = output.astype(jnp.bfloat16)
        passed = from_behind(output_low, "pipe", 1)
        outputs = store_slot(outputs, slot_index, is_valid, output_low)
        layer_inputs = store_slot(layer_inputs, slot_index, is_valid, layer_input)
        return ((passed, outputs, layer_inputs, buffers), None)

    tick_range = jnp.arange(micro_count + 1)
    forward_out, unused = lax.scan(
        forward_tick, (zero_rows, zero_stack, zero_stack, kept_buffers), tick_range
    )
    unused_rows, outputs, layer_inputs, kept_buffers = forward_out
    weight_acc = tuple((jnp.zeros(part.shape, jnp.float32) for part in weights))
    vector_acc = tuple((jnp.zeros(part.shape, jnp.float32) for part in params))
    grads_init = jnp.zeros((micro_count, row_count, feature_count), jnp.float32)
    live_rows = live_clips[:, 0]
    cot_rows_all = cotangent[:, 0]

    def backward_tick(state_carry, tick_index):
        received, grads_in, weight_sum, vector_sum = state_carry
        batch_index = micro_count - tick_index - section_index
        is_valid = (batch_index >= 0) & (batch_index < micro_count)
        slot_index = jnp.clip(batch_index, 0, micro_count - 1)
        cot_rows = lax.dynamic_index_in_dim(cot_rows_all, slot_index, 0, keepdims=False).astype(
            jnp.float32
        )
        live_flag = lax.dynamic_index_in_dim(live_rows, slot_index, 0, keepdims=False).astype(
            jnp.float32
        )
        grad_out = jnp.where(
            section_index == 1, cot_rows * live_flag, received.astype(jnp.float32)
        ) * is_valid.astype(jnp.float32)
        stored_input = lax.dynamic_index_in_dim(layer_inputs, slot_index, 0, keepdims=False)
        kept = layer_forward(stored_input.astype(jnp.float32), weights, params)[1]
        grad_in, weight_grads, vector_grads = layer_backward(grad_out, kept, weights, params)
        passed = from_behind(grad_in.astype(jnp.bfloat16), "pipe", -1)
        grads_in = store_slot(grads_in, slot_index, is_valid, grad_in)
        weight_sum = jax.tree.map(jnp.add, weight_sum, weight_grads)
        vector_sum = jax.tree.map(jnp.add, vector_sum, vector_grads)
        return ((passed, grads_in, weight_sum, vector_sum), None)

    backward_out, unused_two = lax.scan(
        backward_tick, (zero_rows, grads_init, weight_acc, vector_acc), tick_range
    )
    unused_grad, grads_in, weight_acc, vector_acc = backward_out
    weight_out = reduce_end(weight_acc)
    split_out = lax.psum((vector_acc[2], vector_acc[3], vector_acc[7]), "row")
    whole_out = lax.psum(
        (vector_acc[0], vector_acc[1], vector_acc[4], vector_acc[5], vector_acc[6], vector_acc[8]),
        ("row", "col"),
    )
    return (
        outputs[None, :, None],
        grads_in[None, :, None],
        whole_out[0][None],
        whole_out[1][None],
        weight_out[0][None],
        split_out[0][None],
        split_out[1][None],
        weight_out[1][None],
        whole_out[2][None],
        whole_out[3][None],
        whole_out[4][None],
        weight_out[2][None],
        split_out[2][None],
        weight_out[3][None],
        whole_out[5][None],
    )


def contract(left, right, left_dim, right_dim):
    return lax.dot_general(
        left, right, (((left_dim,), (right_dim,)), ((), ())), preferred_element_type=jnp.float32
    )


TILE = 256
QUERY_TILE = 512
CHUNK = 512
LANES = 2 * HD
VMEM_BYTES = 60 * 1024 * 1024
ERFC_SCALE = 0.4
ERFC_TERMS = (
    0.23192221664065504,
    0.1618227850291895,
    0.4682761333792345,
    -0.37091039694171485,
    0.7091488547855423,
    -0.20025962054546065,
)


def gelu_and_slope(values):
    size = jnp.abs(values) * math.sqrt(0.5)
    turn = 1.0 / (1.0 + ERFC_SCALE * size)
    series = ERFC_TERMS[-1]
    for term in ERFC_TERMS[-2::-1]:
        series = series * turn + term
    bell = jnp.exp(-(size * size))
    tail = 0.5 * (series * turn * bell)
    below = jnp.where(values >= 0.0, 1.0 - tail, tail)
    return (values * below, below + values * bell * (1.0 / math.sqrt(2.0 * math.pi)))


def norm_rows(values):
    centered = values - jnp.mean(values, axis=-1, keepdims=True)
    inv_std = lax.rsqrt(jnp.mean(centered * centered, axis=-1, keepdims=True) + epsilon)
    return (centered * inv_std, inv_std)


def norm_rows_backward(grad, centered, inv_std, gain):
    scaled = grad * gain
    first = jnp.mean(scaled, axis=-1, keepdims=True)
    second = jnp.mean(scaled * centered, axis=-1, keepdims=True)
    return inv_std * (scaled - first - centered * second)


def tile_rows(index):
    return pl.ds(pl.multiple_of(index * TILE, TILE), TILE)


def lane_block(start):
    return pl.ds(pl.multiple_of(start, LANES), LANES)


def run_hooks(hooks, index):
    for when, hook in hooks.items():
        pl.when(index == when)(hook)


class Sizes:
    def __init__(self, frames, features, width, hidden, depth):
        self.frames = frames
        self.half = frames // 2
        self.features = features
        self.width = width
        self.hidden = hidden
        self.depth = depth
        self.block = features // (2 * depth)
        self.tiles = frames // TILE
        self.per = width // LANES
        self.tails = 6 * features
        self.tail = 2 * width + hidden
        self.vector = self.tails + self.tail
        self.sums = self.tails + 2 * self.tail
        self.early = (2 * depth, self.block, 4 * width)
        self.late = (2 * depth, self.block, 2 * hidden)


class Wires:
    def __init__(self, sizes, send, recv):
        self.depth = sizes.depth
        self.send, self.recv = (send, recv)
        self.used = 0
        self.pipe = lax.axis_index("pipe")
        self.row = lax.axis_index("row")
        self.col = lax.axis_index("col")
        self.plane = lax.div(self.row, 2)
        self.core = lax.rem(self.row, 2)
        self.place = 2 * self.pipe + self.col
        self.across_x = (1 - self.pipe, self.row, self.col)
        self.across_y = (self.pipe, self.row, 1 - self.col)
        self.across_both = (1 - self.pipe, self.row, 1 - self.col)
        self.across_core = (self.pipe, 2 * self.plane + 1 - self.core, self.col)

    def plane_at(self, step):
        return lax.rem(self.plane + step, self.depth)

    def along_z(self, step):
        return (self.pipe, 2 * self.plane_at(step) + self.core, self.col)

    def greet(self):
        barrier = pltpu.get_barrier_semaphore()
        partners = [self.across_x, self.across_y, self.across_both, self.across_core]
        partners += [self.along_z(step) for step in range(1, self.depth)]
        for partner in partners:
            pl.semaphore_signal(
                barrier, inc=1, device_id=partner, device_id_type=pl.DeviceIdType.MESH
            )
        pl.semaphore_wait(barrier, len(partners))

    def copy(self, source, target, partner):
        number = self.used
        self.used += 1
        return pltpu.make_async_remote_copy(
            src_ref=source,
            dst_ref=target,
            send_sem=self.send.at[number],
            recv_sem=self.recv.at[number],
            device_id=partner,
            device_id_type=pl.DeviceIdType.MESH,
        )


class Local:
    def __init__(self, sems):
        self.sems = sems
        self.used = 0
        self.open = []

    def start(self, source, target):
        copy = pltpu.make_async_copy(source, target, self.sems.at[self.used])
        self.used += 1
        copy.start()
        return copy

    def keep(self, source, target):
        self.open.append(self.start(source, target))

    def finish(self):
        for copy in self.open:
            copy.wait()


def whole_weight(weights, index, start, size):
    depth = weights.shape[1] // 2
    columns = slice(start, start + size)
    return jnp.concatenate(
        [
            weights[index, core * depth + plane, :, columns]
            for plane in range(depth)
            for core in range(2)
        ],
        axis=0,
    )


def attention_forward(sizes, qkv, context, lse, hooks):
    width = sizes.width
    score_scale = 1.0 / math.sqrt(HD)

    def one_pair(pair, carry):
        part, index = (lax.div(pair, sizes.per), lax.rem(pair, sizes.per))
        base = part * (3 * width) + index * LANES
        for start in range(0, sizes.frames, QUERY_TILE):
            rows = slice(start, start + QUERY_TILE)
            query_pair = qkv[rows, lane_block(base)]
            key_pair = qkv[:, lane_block(base + width)]
            value_pair = qkv[:, lane_block(base + 2 * width)]
            parts = []
            for head in range(2):
                lanes = slice(head * HD, (head + 1) * HD)
                scaled = query_pair[:, lanes] * jnp.asarray(score_scale, jnp.bfloat16)
                scores = contract(scaled, key_pair[:, lanes], 1, 1)
                top = jnp.max(scores, axis=1, keepdims=True)
                weights = jnp.exp(scores - top).astype(jnp.bfloat16)
                extended = jnp.concatenate(
                    [value_pair[:, lanes], jnp.ones((sizes.frames, HD), jnp.bfloat16)], axis=1
                )
                mixed = contract(weights, extended, 1, 0)
                total = mixed[:, HD : HD + 1]
                parts.append(mixed[:, :HD] / total)
                lse[pair, head : head + 1, rows] = (top + jnp.log(total)).reshape(1, QUERY_TILE)
            context[rows, lane_block(pair * LANES)] = jnp.concatenate(parts, axis=1).astype(
                jnp.bfloat16
            )
        run_hooks(hooks, pair)
        return carry

    lax.fori_loop(0, 2 * sizes.per, one_pair, 0)


def attention_backward(
    sizes, qkv, context, grad_context, lse, add_query_bias, add_value_bias, hooks
):
    width = sizes.width
    score_scale = 1.0 / math.sqrt(HD)

    def one_pair(pair, carry):
        part, index = (lax.div(pair, sizes.per), lax.rem(pair, sizes.per))
        base = part * (3 * width) + index * LANES
        key_pair = qkv[:, lane_block(base + width)]
        value_pair = qkv[:, lane_block(base + 2 * width)]
        grad_keys = [None, None]
        grad_values = [None, None]
        query_total = jnp.zeros((1, LANES), jnp.float32)
        for start in range(0, sizes.frames, TILE):
            rows = slice(start, start + TILE)
            query_pair = qkv[rows, lane_block(base)]
            grad_pair = grad_context[rows, lane_block(pair * LANES)]
            context_pair = context[rows, lane_block(pair * LANES)]
            products = (grad_pair.astype(jnp.float32) * context_pair.astype(jnp.float32)).T
            parts = []
            for head in range(2):
                lanes = slice(head * HD, (head + 1) * HD)
                keys = key_pair[:, lanes]
                grads = grad_pair[:, lanes]
                scaled = query_pair[:, lanes] * jnp.asarray(score_scale, jnp.bfloat16)
                scores = contract(keys, scaled, 1, 1)
                probs = jnp.exp(scores - lse[pair, head : head + 1, rows])
                grad_probs = contract(value_pair[:, lanes], grads, 1, 1)
                delta = jnp.sum(products[lanes, :], axis=0, keepdims=True)
                low_scores = (probs * (grad_probs - delta)).astype(jnp.bfloat16)
                value_part = contract(probs.astype(jnp.bfloat16), grads, 1, 0)
                key_part = contract(low_scores, scaled, 1, 0)
                grad_values[head] = value_part if start == 0 else grad_values[head] + value_part
                grad_keys[head] = key_part if start == 0 else grad_keys[head] + key_part
                parts.append(contract(keys, low_scores, 0, 0))
            turned = jnp.concatenate(parts, axis=0).T * score_scale
            query_total = query_total + jnp.sum(turned, axis=0, keepdims=True)
            qkv[rows, lane_block(base)] = turned.astype(jnp.bfloat16)
        key_grad = jnp.concatenate(grad_keys, axis=1)
        value_grad = jnp.concatenate(grad_values, axis=1)
        qkv[:, lane_block(base + width)] = key_grad.astype(jnp.bfloat16)
        qkv[:, lane_block(base + 2 * width)] = value_grad.astype(jnp.bfloat16)
        add_query_bias(part, index, query_total)
        add_value_bias(part, index, jnp.sum(value_grad, axis=0, keepdims=True))
        run_hooks(hooks, pair)
        return carry

    lax.fori_loop(0, 2 * sizes.per, one_pair, 0)


def vector_reader(sizes, vectors, layer):
    features = sizes.features

    def whole(index):
        return vectors[2 * layer, :, index * features : (index + 1) * features]

    def split(part, start, size):
        first = sizes.tails + start
        return vectors[2 * layer + part, :, first : first + size]

    return (whole, split)


def forward_norm(sizes, layer, values, vectors, normed):
    whole, split = vector_reader(sizes, vectors, layer)

    def one_tile(index, carry):
        rows = tile_rows(index)
        centered, unused = norm_rows(values[rows, :].astype(jnp.float32))
        normed[rows, :] = (centered * whole(0) + whole(1)).astype(jnp.bfloat16)
        return carry

    lax.fori_loop(0, sizes.tiles, one_tile, 0)


def forward_qkv(sizes, layer, normed, early, vectors, qkv):
    width = sizes.width
    whole, split = vector_reader(sizes, vectors, layer)

    def one_tile(index, carry):
        rows = tile_rows(index)
        for part in range(2):
            for kind in range(3):
                result = contract(
                    normed[rows, :],
                    whole_weight(early, 2 * layer + part, kind * width, width),
                    1,
                    0,
                )
                if kind == 0:
                    result = result + split(part, 0, width)
                if kind == 2:
                    result = result + split(part, width, width)
                first = (3 * part + kind) * width
                qkv[rows, first : first + width] = result.astype(jnp.bfloat16)
        return carry

    lax.fori_loop(0, sizes.tiles, one_tile, 0)


def forward_rest(
    sizes, layer, values, early, late, vectors, context, hidden, active, slope, output, hooks
):
    width, size = (sizes.width, sizes.hidden)
    whole, split = vector_reader(sizes, vectors, layer)

    def one_tile(index, carry):
        rows = tile_rows(index)
        total = values[rows, :].astype(jnp.float32) + whole(2)
        for part in range(2):
            total = total + contract(
                context[rows, part * width : (part + 1) * width],
                whole_weight(early, 2 * layer + part, 3 * width, width),
                1,
                1,
            )
        hidden[rows, :] = total
        centered, unused = norm_rows(total)
        normed = (centered * whole(3) + whole(4)).astype(jnp.bfloat16)
        total = total + whole(5)
        for part in range(2):
            for start in range(0, size, CHUNK):
                weights = late.at[2 * layer + part]
                pre_act = contract(
                    normed, whole_weight(late, 2 * layer + part, start, CHUNK), 1, 0
                ) + split(part, 2 * width + start, CHUNK)
                act, act_slope = gelu_and_slope(pre_act)
                act = act.astype(jnp.bfloat16)
                first = part * size + start
                active[rows, first : first + CHUNK] = act
                slope[rows, first : first + CHUNK] = act_slope.astype(jnp.bfloat16)
                total = total + contract(
                    act, whole_weight(late, 2 * layer + part, size + start, CHUNK), 1, 1
                )
        output[rows, :] = total.astype(jnp.bfloat16)
        run_hooks(hooks, index)
        return carry

    lax.fori_loop(0, sizes.tiles, one_tile, 0)


class Gather:
    def __init__(self, wires, block, full):
        self.block, self.full = (block, full)
        depth, half = (wires.depth, block.shape[0] // 2)
        middle = block.shape[1] // 2
        left, right, every = (pl.ds(0, middle), pl.ds(middle, middle), pl.ds(0, 2 * middle))
        slot = wires.core * depth + wires.plane
        slots = pl.ds(wires.core * depth, depth)
        mine = pl.ds(pl.multiple_of(wires.pipe * half, half), half)
        theirs = pl.ds(pl.multiple_of((1 - wires.pipe) * half, half), half)
        both = pl.ds(0, 2 * half)

        def send(where, partner):
            return wires.copy(full.at[where], full.at[where], partner)

        own = 2 * wires.pipe + wires.col
        self.own, self.mine = ((own, slot, mine), mine)
        self.x = wires.copy(block.at[theirs], full.at[own, slot, theirs], wires.across_x)
        self.z, self.first, self.second, self.core = ([], [], [], [])
        for layer in range(2):
            index = 2 * layer + wires.col
            pair = pl.ds(2 * layer, 2)
            self.z.append(
                [
                    send((index, slot, mine, every), wires.along_z(step))
                    for step in range(1, depth)
                ]
            )
            self.first.append(
                [
                    send((index, slots, mine, left), wires.across_x),
                    send((index, slots, mine, right), wires.across_y),
                ]
            )
            self.second.append(
                [
                    send((index, slots, both, left), wires.across_y),
                    send((pair, slots, mine, right), wires.across_x),
                ]
            )
            self.core.append([send((pair, slots, both, every), wires.across_core)])

    def place_own(self):
        self.full[self.own] = self.block[self.mine, :]

    def move(self, arriving, leaving):
        for copy in arriving:
            copy.wait_recv()
        for copy in leaving:
            copy.start()

    def start_z(self, layer):
        self.move([], self.z[layer])

    def end_z(self, layer):
        self.move(self.z[layer], self.first[layer])

    def end_first(self, layer):
        self.move(self.first[layer], self.second[layer])

    def end_second(self, layer):
        self.move(self.second[layer], self.core[layer])

    def arrive(self, layer):
        self.move(self.core[layer], [])

    def finish(self):
        self.x.wait_send()
        for layer in range(2):
            for copies in (self.z, self.first, self.second, self.core):
                for copy in copies[layer]:
                    copy.wait_send()


def forward_kernel(
    sizes,
    inputs_ref,
    cot_ref,
    qkv_weight,
    proj_weight,
    up_weight,
    down_weight,
    *rest,
):
    vector_parts = rest[:9]
    forward_body(
        sizes,
        inputs_ref,
        cot_ref,
        (qkv_weight, proj_weight, up_weight, down_weight),
        vector_parts,
        *rest[9:],
    )


def forward_body(
    sizes,
    inputs_ref,
    cot_ref,
    own_weights,
    vector_parts,
    sent_ref,
    final_ref,
    lse_ref,
    states_out,
    x_out,
    cot_out,
    early_out,
    late_out,
    vector_out,
    qkv_out,
    context_out,
    hidden_out,
    active_out,
    slope_out,
    qkv,
    context,
    hidden,
    active,
    slope,
    x,
    cot,
    early,
    late,
    vectors,
    normed,
    early_block,
    late_block,
    vector_block,
    send,
    recv,
    sems,
):
    half = sizes.half
    qkv_weight, proj_weight, up_weight, down_weight = own_weights
    wires = Wires(sizes, send, recv)
    local = Local(sems)
    own_rows = pl.ds(pl.multiple_of(wires.col * half, half), half)
    other_place = 2 * wires.pipe + 1 - wires.col
    own_x = local.start(inputs_ref.at[wires.place, 0], x.at[own_rows])
    own_cot = local.start(cot_ref.at[wires.place, 0], cot.at[own_rows])
    width, size = (sizes.width, sizes.hidden)
    for kind in range(3):
        early_block[:, kind * width : (kind + 1) * width] = qkv_weight[0, kind]
    early_block[:, 3 * width :] = proj_weight[0].T
    start = 0
    for part in vector_parts:
        vector_block[:, start : start + part.shape[1]] = part[...]
        start += part.shape[1]
    early_gather = Gather(wires, early_block, early)
    late_gather = Gather(wires, late_block, late)
    early_gather.place_own()
    vectors[wires.place] = vector_block[...]
    wires.greet()
    early_gather.x.start()
    vector_copies = [
        wires.copy(vector_block, vectors.at[wires.place], partner)
        for partner in (wires.across_x, wires.across_y, wires.across_both)
    ]
    for copy in vector_copies:
        copy.start()
    x_copy = wires.copy(inputs_ref.at[other_place, 0], x.at[own_rows], wires.across_y)
    x_copy.start()
    late_block[:, :size] = up_weight[0]
    late_block[:, size:] = down_weight[0].T
    late_gather.place_own()
    late_gather.x.start()
    trade = Trade(sizes, wires, local, 0, sent_ref, states_out)
    cot_copy = wires.copy(cot_ref.at[other_place, 0], cot.at[own_rows], wires.across_y)
    early_gather.x.wait_recv()
    early_gather.start_z(0)
    own_x.wait()
    x_copy.wait_recv()
    for copy in vector_copies:
        copy.wait_recv()
    early_gather.end_z(0)
    late_gather.x.wait_recv()
    late_gather.start_z(0)
    forward_norm(sizes, 0, x, vectors, normed)
    early_gather.end_first(0)
    local.keep(x, x_out)
    early_gather.end_second(0)

    def second_pair():
        late_gather.end_first(0)

    def third_pair():
        late_gather.end_second(0)
        early_gather.end_z(1)
        late_gather.start_z(1)

    def later_second_pair():
        late_gather.end_second(1)
        cot_copy.start()
        trade.start()

    attention_hooks = [{0: second_pair, 2: third_pair}, {1: later_second_pair}]
    rest_hooks = [
        {
            0: functools.partial(early_gather.end_first, 1),
            1: functools.partial(late_gather.end_z, 1),
            2: functools.partial(early_gather.end_second, 1),
            3: functools.partial(late_gather.end_first, 1),
        },
        {},
    ]
    for layer in range(2):
        values = (x, sent_ref)[layer]
        output = (sent_ref, final_ref)[layer]
        if layer == 1:
            forward_norm(sizes, 1, values, vectors, normed)
        early_gather.arrive(layer)
        if layer == 0:
            late_gather.end_z(0)
            early_gather.start_z(1)
        forward_qkv(sizes, layer, normed, early, vectors, qkv.at[layer])
        local.keep(qkv.at[layer], qkv_out.at[layer])
        attention_forward(
            sizes, qkv.at[layer], context.at[layer], lse_ref.at[layer], attention_hooks[layer]
        )
        local.keep(context.at[layer], context_out.at[layer])
        late_gather.arrive(layer)
        forward_rest(
            sizes,
            layer,
            values,
            early,
            late,
            vectors,
            context.at[layer],
            hidden.at[layer],
            active.at[layer],
            slope.at[layer],
            output,
            rest_hooks[layer],
        )
        local.keep(hidden.at[layer], hidden_out.at[layer])
        local.keep(active.at[layer], active_out.at[layer])
        local.keep(slope.at[layer], slope_out.at[layer])
        both = pl.ds(2 * layer, 2)
        local.keep(early.at[both], early_out.at[both])
        local.keep(late.at[both], late_out.at[both])
    own_cot.wait()
    cot_copy.wait_recv()
    local.keep(cot, cot_out)
    vector_out[...] = vectors[...]
    for copy in vector_copies + [x_copy, cot_copy]:
        copy.wait_send()
    early_gather.finish()
    late_gather.finish()
    trade.finish()
    local.finish()


def saved_shapes(sizes):
    frames, features = (sizes.frames, sizes.features)
    return [
        ((2, frames, 6 * sizes.width), jnp.bfloat16),
        ((2, frames, 2 * sizes.width), jnp.bfloat16),
        ((2, frames, features), jnp.float32),
        ((2, frames, 2 * sizes.hidden), jnp.bfloat16),
        ((2, frames, 2 * sizes.hidden), jnp.bfloat16),
    ]


def run_forward(sizes, inputs, cot, weights, vector_parts):
    frames, features = (sizes.frames, sizes.features)
    vmem = pl.BlockSpec(memory_space=pltpu.VMEM)
    hbm = pl.BlockSpec(memory_space=pl.ANY)
    saved = saved_shapes(sizes)
    low = jnp.bfloat16
    rows = ((frames, features), low)
    early, late = (((4,) + sizes.early, low), ((4,) + sizes.late, low))
    vectors = ((4, 1, sizes.vector), jnp.float32)
    states = ((4, sizes.half, features), low)
    blocks = [(sizes.early[1:], low), (sizes.late[1:], low), (vectors[0][1:], jnp.float32)]
    outs = [rows, rows, ((2, 2 * sizes.per, 2, frames), jnp.float32)]
    outs += [states, rows, rows, early, late, vectors] + saved
    count = 2 * (1 + 2 * (sizes.depth - 1 + 5)) + 5 + 3
    return pl.pallas_call(
        functools.partial(forward_kernel, sizes),
        in_specs=[hbm, hbm] + [vmem] * 13,
        out_specs=[vmem] * 3 + [hbm] * 5 + [vmem] + [hbm] * 5,
        out_shape=[jax.ShapeDtypeStruct(shape, dtype) for shape, dtype in outs],
        scratch_shapes=[
            pltpu.VMEM(shape, dtype)
            for shape, dtype in saved + [rows, rows, early, late, vectors, rows] + blocks
        ]
        + [
            pltpu.SemaphoreType.DMA((count,)),
            pltpu.SemaphoreType.DMA((count,)),
            pltpu.SemaphoreType.DMA((19,)),
        ],
        compiler_params=pltpu.CompilerParams(
            vmem_limit_bytes=VMEM_BYTES, collective_id=0, has_side_effects=True
        ),
        name="layers_forward",
    )(inputs, cot, *weights, *vector_parts)


def add_row(sums, layer, start, value):
    where = (layer, slice(None), slice(start, start + value.shape[1]))
    sums[where] = sums[where] + value


def column_sum(values):
    return jnp.sum(values, axis=0, keepdims=True)


def put_block(target, part, start, value):
    depth, block = (target.shape[1] // 2, target.shape[2])
    low = value.astype(jnp.bfloat16)
    for row in range(2 * depth):
        target[part, (row % 2) * depth + row // 2, :, start : start + value.shape[1]] = low[
            row * block : (row + 1) * block
        ]


def backward_mlp(
    sizes,
    layer,
    hidden,
    active,
    slope,
    late,
    vectors,
    grad,
    sums,
    normed_t,
    grad_t,
    grad_late,
    hooks,
    after_rows,
):
    features, width, size = (sizes.features, sizes.width, sizes.hidden)
    whole, split = vector_reader(sizes, vectors, layer)

    def one_tile(index, carry):
        rows = tile_rows(index)
        grad_out = grad[rows, :]
        add_row(sums, layer, 5 * features, column_sum(grad_out))
        grad_low = grad_out.astype(jnp.bfloat16)
        grad_t[:, rows] = grad_low.T
        centered, inv_std = norm_rows(hidden[rows, :])
        normed_t[:, rows] = (centered * whole(3) + whole(4)).astype(jnp.bfloat16).T
        grad_normed = jnp.zeros((TILE, features), jnp.float32)
        for part in range(2):
            for start in range(0, size, CHUNK):
                first = part * size + start
                grad_act = contract(grad_low, whole_weight(late, part, size + start, CHUNK), 1, 0)
                grad_pre = grad_act * slope[rows, first : first + CHUNK].astype(jnp.float32)
                add_row(
                    sums,
                    layer,
                    sizes.tails + part * sizes.tail + 2 * width + start,
                    column_sum(grad_pre),
                )
                low = grad_pre.astype(jnp.bfloat16)
                slope[rows, first : first + CHUNK] = low
                grad_normed = grad_normed + contract(
                    low, whole_weight(late, part, start, CHUNK), 1, 1
                )
        add_row(sums, layer, 3 * features, column_sum(grad_normed * centered))
        add_row(sums, layer, 4 * features, column_sum(grad_normed))
        grad_hidden = grad_out + norm_rows_backward(grad_normed, centered, inv_std, whole(3))
        add_row(sums, layer, 2 * features, column_sum(grad_hidden))
        grad[rows, :] = grad_hidden
        run_hooks(hooks, index)
        return carry

    lax.fori_loop(0, sizes.tiles, one_tile, 0)
    after_rows()
    for part in range(2):
        for start in range(0, size, 256):
            first = part * size + start
            up = contract(normed_t[...], slope[:, first : first + 256], 1, 0)
            put_block(grad_late, part, start, up)
            down = contract(grad_t[...], active[:, first : first + 256], 1, 0)
            put_block(grad_late, part, size + start, down)


def backward_context(
    sizes, layer, values, early, vectors, grad, normed_t, grad_t, grad_context
):
    width = sizes.width
    whole, split = vector_reader(sizes, vectors, layer)

    def to_context(index, carry):
        rows = tile_rows(index)
        low = grad[rows, :].astype(jnp.bfloat16)
        grad_t[:, rows] = low.T
        for part in range(2):
            grad_context[rows, part * width : (part + 1) * width] = contract(
                low, whole_weight(early, part, 3 * width, width), 1, 0
            ).astype(jnp.bfloat16)
        centered, unused = norm_rows(values[rows, :].astype(jnp.float32))
        normed_t[:, rows] = (centered * whole(0) + whole(1)).astype(jnp.bfloat16).T
        return carry

    lax.fori_loop(0, sizes.tiles, to_context, 0)


def backward_early_weights(sizes, qkv, context, normed_t, grad_t, grad_early):
    width = sizes.width
    for part in range(2):
        for kind in range(3):
            first = (3 * part + kind) * width
            result = contract(normed_t[...], qkv[:, first : first + width], 1, 0)
            put_block(grad_early, part, kind * width, result)
        result = contract(grad_t[...], context[:, part * width : (part + 1) * width], 1, 0)
        put_block(grad_early, part, 3 * width, result)


def backward_input(sizes, layer, values, qkv, early, vectors, grad, sums, grad_in):
    features, width = (sizes.features, sizes.width)
    whole, split = vector_reader(sizes, vectors, layer)

    def to_input(index, carry):
        rows = tile_rows(index)
        grad_normed = jnp.zeros((TILE, features), jnp.float32)
        for part in range(2):
            grad_normed = grad_normed + contract(
                qkv[rows, part * 3 * width : (part + 1) * 3 * width],
                whole_weight(early, part, 0, 3 * width),
                1,
                1,
            )
        centered, inv_std = norm_rows(values[rows, :].astype(jnp.float32))
        add_row(sums, layer, 0, column_sum(grad_normed * centered))
        add_row(sums, layer, features, column_sum(grad_normed))
        low = (
            grad[rows, :] + norm_rows_backward(grad_normed, centered, inv_std, whole(0))
        ).astype(jnp.bfloat16)
        grad_in[rows, :] = low
        grad[rows, :] = low.astype(jnp.float32)
        return carry

    lax.fori_loop(0, sizes.tiles, to_input, 0)


def add_low(left, right):
    return (left.astype(jnp.float32) + right.astype(jnp.float32)).astype(jnp.bfloat16)


class Reduce:
    def __init__(self, wires, grads, from_core, x_one, y_one, y_two, x_two, joined, from_z, total, low, from_x):
        self.wires, self.grads, self.from_core = (wires, grads, from_core)
        self.x_one, self.y_one, self.y_two, self.x_two = (x_one, y_one, y_two, x_two)
        self.joined, self.from_z = (joined, from_z)
        self.total, self.from_x, self.low = (total, from_x, low)
        depth, half = (wires.depth, grads.shape[2] // 2)
        middle = grads.shape[3] // 2
        self.half, self.middle = (half, middle)
        left, right = (pl.ds(0, middle), pl.ds(middle, middle))
        self.left, self.right = (slice(0, middle), slice(middle, 2 * middle))
        slots = pl.ds((1 - wires.core) * depth, depth)
        self.mine = pl.ds(pl.multiple_of(wires.pipe * half, half), half)
        self.theirs = pl.ds(pl.multiple_of((1 - wires.pipe) * half, half), half)
        col, planes, rows = (1 - wires.col, pl.ds(0, depth), pl.ds(0, 2 * half))
        self.core, self.first, self.second, self.z = ([], [], [], [])
        for layer in range(2):
            self.core.append(
                wires.copy(grads.at[:, slots], from_core.at[layer], wires.across_core)
            )
            held = from_core.at[layer]
            self.first.append(
                [
                    wires.copy(
                        held.at[pl.ds(0, 2), planes, self.theirs, left],
                        x_one.at[layer],
                        wires.across_x,
                    ),
                    wires.copy(
                        held.at[col, planes, rows, right], y_one.at[layer], wires.across_y
                    ),
                ]
            )
            self.second.append(
                [
                    wires.copy(x_one.at[layer, col], y_two.at[layer], wires.across_y),
                    wires.copy(
                        y_one.at[layer, planes, self.theirs], x_two.at[layer], wires.across_x
                    ),
                ]
            )
            self.z.append(
                [
                    wires.copy(
                        joined.at[layer, wires.plane_at(step)],
                        from_z.at[layer, wires.plane],
                        wires.along_z(step),
                    )
                    for step in range(1, depth)
                ]
            )
        self.x = wires.copy(low.at[1 - wires.pipe], from_x, wires.across_x)

    def each_plane(self, body):
        def one(plane, carry):
            body(plane)
            return carry

        lax.fori_loop(0, self.wires.depth, one, 0)

    def end_core(self, layer):
        wires, held = (self.wires, self.from_core)
        self.core[layer].wait()

        def add(plane):
            for part in range(2):
                held[layer, part, plane] = add_low(
                    held[layer, part, plane],
                    self.grads[part, wires.core * wires.depth + plane],
                )

        self.each_plane(add)
        for copy in self.first[layer]:
            copy.start()

    def end_first(self, layer):
        held, x_one, y_one = (self.from_core, self.x_one, self.y_one)
        for copy in self.first[layer]:
            copy.wait_recv()

        def add(plane):
            for part in range(2):
                x_one[layer, part, plane] = add_low(
                    x_one[layer, part, plane], held[layer, part, plane, self.mine, self.left]
                )
            y_one[layer, plane] = add_low(
                y_one[layer, plane], held[layer, self.wires.col, plane, :, self.right]
            )

        self.each_plane(add)
        for copy in self.second[layer]:
            copy.start()

    def end_second(self, layer):
        joined = self.joined
        for copy in self.second[layer]:
            copy.wait_recv()

        def add(plane):
            joined[layer, plane, :, self.left] = add_low(
                self.y_two[layer, plane], self.x_one[layer, self.wires.col, plane]
            )
            joined[layer, plane, :, self.right] = add_low(
                self.x_two[layer, plane], self.y_one[layer, plane, self.mine, :]
            )

        self.each_plane(add)
        for copy in self.z[layer]:
            copy.start()

    def end_z(self, layer):
        wires = self.wires
        for copy in self.z[layer]:
            copy.wait_recv()
        total = self.joined[layer, wires.plane].astype(jnp.float32)
        for step in range(1, wires.depth):
            total = total + self.from_z[layer, wires.plane_at(step)].astype(jnp.float32)
        self.total[layer] = total
        self.low[layer] = total.astype(jnp.bfloat16)

    def end_x(self, target):
        self.x.wait()
        target[self.mine, :] = self.total[self.wires.pipe]
        target[self.theirs, :] = self.from_x[...].astype(jnp.float32)
        for layer in range(2):
            for copy in self.first[layer] + self.second[layer] + self.z[layer]:
                copy.wait_send()


class ReduceSums:
    def __init__(self, wires, sums, second, third, from_all, from_x):
        self.wires = wires
        self.stages = (sums, second, third)
        self.from_all, self.from_x = (from_all, from_x)
        self.core, self.y, self.z = ([], [], [])
        for layer in range(2):
            self.core.append(
                wires.copy(sums.at[layer], from_all.at[layer, 0], wires.across_core)
            )
            self.y.append(wires.copy(second.at[layer], from_all.at[layer, 1], wires.across_y))
            self.z.append(
                [
                    wires.copy(
                        third.at[layer], from_all.at[layer, 2 + wires.plane], wires.along_z(step)
                    )
                    for step in range(1, wires.depth)
                ]
            )
        self.x = wires.copy(sums.at[1 - wires.pipe], from_x, wires.across_x)

    def end_core(self, layer):
        self.core[layer].wait()
        self.stages[1][layer] = self.stages[0][layer] + self.from_all[layer, 0]
        self.y[layer].start()

    def end_y(self, layer):
        self.y[layer].wait()
        self.stages[2][layer] = self.stages[1][layer] + self.from_all[layer, 1]
        for copy in self.z[layer]:
            copy.start()

    def end_z(self, layer):
        wires = self.wires
        for copy in self.z[layer]:
            copy.wait()
        self.from_all[layer, 2 + wires.plane] = self.stages[2][layer]
        total = self.from_all[layer, 2]
        for plane in range(1, wires.depth):
            total = total + self.from_all[layer, 2 + plane]
        self.stages[0][layer] = total

    def end_x(self, target):
        self.x.wait()
        target[...] = self.stages[0][self.wires.pipe] + self.from_x[...]


class Trade:
    def __init__(self, sizes, wires, local, layer, source, target):
        half = sizes.half
        self.wires, self.layer = (wires, layer)
        self.copies = []
        for step in range(1, 4):
            pipe = wires.pipe if step < 2 else 1 - wires.pipe
            col = wires.col if step == 2 else 1 - wires.col
            rows = pl.ds(pl.multiple_of(col * half, half), half)
            copy = wires.copy(
                source.at[rows], target.at[wires.place], (pipe, wires.row, col)
            )
            self.copies.append((pipe == layer, copy))
        rows = pl.ds(pl.multiple_of(wires.col * half, half), half)
        self.own = pltpu.make_async_copy(
            source.at[rows], target.at[wires.place], local.sems.at[local.used]
        )
        local.used += 1

    def start(self):
        for wanted, copy in self.copies:
            pl.when(wanted)(copy.start)
        pl.when(self.wires.pipe == self.layer)(self.own.start)

    def finish(self):
        for wanted, copy in self.copies:
            pl.when(wanted)(copy.wait_send)

        def arrive():
            self.own.wait()
            for wanted, copy in self.copies:
                copy.wait_recv()

        pl.when(self.wires.pipe == self.layer)(arrive)


def backward_kernel(
    sizes,
    live_ref,
    cot_ref,
    x_ref,
    sent_ref,
    final_ref,
    vectors,
    lse_ref,
    early_in,
    late_in,
    qkv_in,
    context_in,
    hidden_in,
    active_in,
    slope_in,
    states_in,
    states_out,
    grads_out,
    sums_out,
    early_out,
    late_out,
    qkv,
    context,
    hidden,
    active,
    slope,
    early,
    late,
    mid,
    first,
    values,
    grad,
    normed_t,
    grad_t,
    grad_context,
    grad_early,
    grad_late,
    early_core,
    early_x_one,
    early_y_one,
    early_y_two,
    early_x_two,
    early_joined,
    early_z,
    early_total,
    early_low,
    early_x,
    late_core,
    late_x_one,
    late_y_one,
    late_y_two,
    late_x_two,
    late_joined,
    late_z,
    late_total,
    late_low,
    late_x,
    sums,
    sums_second,
    sums_third,
    sums_all,
    sums_x,
    send,
    recv,
    sems,
):
    wires = Wires(sizes, send, recv)
    local = Local(sems)

    def load(source, target, layer):
        return local.start(source.at[layer], target)

    def load_pair(source, target, layer):
        return local.start(source.at[pl.ds(2 * layer, 2)], target)

    cot_copy = local.start(cot_ref, first)
    late_copy = load_pair(late_in, late, 1)
    slope_copy = load(slope_in, slope, 1)
    hidden_copy = load(hidden_in, hidden, 1)
    active_copy = load(active_in, active, 1)
    early_copy = load_pair(early_in, early, 1)
    attention_copies = [
        load(qkv_in, qkv, 1),
        load(context_in, context, 1),
        local.start(sent_ref, values),
    ]
    sums[...] = jnp.zeros_like(sums)
    wires.greet()
    trades = [Trade(sizes, wires, local, 1, final_ref, states_out)]
    trades[0].start()
    cot_copy.wait()
    grad[...] = first[...].astype(jnp.float32) * live_ref[wires.place, 0].astype(jnp.float32)
    early_sum = Reduce(
        wires,
        grad_early,
        early_core,
        early_x_one,
        early_y_one,
        early_y_two,
        early_x_two,
        early_joined,
        early_z,
        early_total,
        early_low,
        early_x,
    )
    late_sum = Reduce(
        wires,
        grad_late,
        late_core,
        late_x_one,
        late_y_one,
        late_y_two,
        late_x_two,
        late_joined,
        late_z,
        late_total,
        late_low,
        late_x,
    )
    small_sum = ReduceSums(wires, sums, sums_second, sums_third, sums_all, sums_x)

    def no_wait():
        pass

    def mlp_one():
        late_sum.end_second(1)

    def mlp_two():
        early_sum.end_first(1)
        small_sum.end_y(1)

    def after_mlp_rows():
        late_sum.end_z(1)
        early_sum.end_second(1)
        small_sum.end_z(1)

    def pair_zero():
        late_sum.end_core(0)
        early_sum.end_z(1)

    for layer in (1, 0):
        late_copy.wait()
        slope_copy.wait()
        hidden_copy.wait()
        active_copy.wait()
        backward_mlp(
            sizes,
            layer,
            hidden,
            active,
            slope,
            late,
            vectors,
            grad,
            sums,
            normed_t,
            grad_t,
            grad_late,
            {} if layer == 1 else {1: mlp_one, 2: mlp_two},
            no_wait if layer == 1 else after_mlp_rows,
        )
        late_sum.core[layer].start()
        if layer == 1:
            late_copy = load_pair(late_in, late, 0)
            slope_copy = load(slope_in, slope, 0)
            hidden_copy = load(hidden_in, hidden, 0)
            active_copy = load(active_in, active, 0)
        early_copy.wait()
        for copy in attention_copies:
            copy.wait()
        backward_context(
            sizes, layer, values, early, vectors, grad, normed_t, grad_t, grad_context
        )

        def add_bias(offset):
            def add(part, index, value):
                start = sizes.tails + part * sizes.tail + offset + index * LANES
                where = (layer, slice(None), lane_block(start))
                sums[where] = sums[where] + value

            return add

        if layer == 1:
            hooks = {0: functools.partial(late_sum.end_core, 1)}
        else:
            hooks = {0: pair_zero, 1: functools.partial(late_sum.end_first, 0)}
        attention_backward(
            sizes,
            qkv,
            context,
            grad_context,
            lse_ref.at[layer],
            add_bias(0),
            add_bias(sizes.width),
            hooks,
        )
        if layer == 1:
            late_sum.end_first(1)
        else:
            late_sum.end_second(0)
        grad_in = (first, mid)[layer]
        backward_input(sizes, layer, values, qkv, early, vectors, grad, sums, grad_in)
        trades.append(Trade(sizes, wires, local, layer, grad_in, grads_out))
        if layer == 0:
            for trade in trades[-2:]:
                trade.start()
        small_sum.core[layer].start()
        backward_early_weights(sizes, qkv, context, normed_t, grad_t, grad_early)
        early_sum.core[layer].start()
        small_sum.end_core(layer)
        early_sum.end_core(layer)
        if layer == 1:
            early_copy = load_pair(early_in, early, 0)
            attention_copies = [
                load(qkv_in, qkv, 0),
                load(context_in, context, 0),
                local.start(x_ref, values),
            ]
    early_sum.end_first(0)
    small_sum.end_y(0)
    late_sum.end_z(0)
    late_sum.x.start()
    early_sum.end_second(0)
    small_sum.end_z(0)
    small_sum.x.start()
    early_sum.end_z(0)
    early_sum.x.start()
    late_sum.end_x(late_out)
    early_sum.end_x(early_out)
    small_sum.end_x(sums_out)
    for trade in trades:
        trade.finish()


def run_backward(sizes, live, cot, values, sent, final, vectors, lse, early, late, states, saved):
    frames, features, depth = (sizes.frames, sizes.features, sizes.depth)
    vmem = pl.BlockSpec(memory_space=pltpu.VMEM)
    hbm = pl.BlockSpec(memory_space=pl.ANY)
    smem = pl.BlockSpec(memory_space=pltpu.SMEM)
    low, high = (jnp.bfloat16, jnp.float32)

    def reduce_shapes(block):
        rows, columns = block[1:]
        half, middle = (rows // 2, columns // 2)
        return [
            ((2, 2, depth, rows, columns), low),
            ((2, 2, depth, half, middle), low),
            ((2, depth, rows, middle), low),
            ((2, depth, half, middle), low),
            ((2, depth, half, middle), low),
            ((2, depth, half, columns), low),
            ((2, depth, half, columns), low),
            ((2, half, columns), high),
            ((2, half, columns), low),
            ((half, columns), low),
        ]

    row = (1, sizes.sums)
    scratch = [(shape[1:], dtype) for shape, dtype in saved_shapes(sizes)]
    scratch += [((2,) + sizes.early, low), ((2,) + sizes.late, low)]
    scratch += [((frames, features), low)] * 3 + [((frames, features), high)]
    scratch += [((features, frames), low)] * 2 + [((frames, 2 * sizes.width), low)]
    scratch += [((2,) + sizes.early, low), ((2,) + sizes.late, low)]
    scratch += reduce_shapes(sizes.early) + reduce_shapes(sizes.late)
    scratch += [((2,) + row, high)] * 3 + [((2, 2 + depth) + row, high), (row, high)]
    count = 9 + 2 * (2 * (5 + depth - 1) + 2 + depth - 1) + 3
    return pl.pallas_call(
        functools.partial(backward_kernel, sizes),
        in_specs=[smem] + [hbm] * 4 + [vmem] * 2 + [hbm] * 8,
        out_specs=[hbm, hbm, vmem, vmem, vmem],
        out_shape=[
            jax.ShapeDtypeStruct((4, sizes.half, features), low),
            jax.ShapeDtypeStruct((4, sizes.half, features), low),
            jax.ShapeDtypeStruct(row, high),
            jax.ShapeDtypeStruct(sizes.early[1:], high),
            jax.ShapeDtypeStruct(sizes.late[1:], high),
        ],
        scratch_shapes=[pltpu.VMEM(shape, dtype) for shape, dtype in scratch]
        + [
            pltpu.SemaphoreType.DMA((count,)),
            pltpu.SemaphoreType.DMA((count,)),
            pltpu.SemaphoreType.DMA((21,)),
        ],
        compiler_params=pltpu.CompilerParams(
            vmem_limit_bytes=VMEM_BYTES, collective_id=1, has_side_effects=True
        ),
        input_output_aliases={14: 0},
        name="layers_backward",
    )(live, cot, values, sent, final, vectors, lse, early, late, *saved, states)


def on_device_clip(
    inputs,
    first_gain,
    first_shift,
    qkv_weight,
    query_bias,
    value_bias,
    proj_weight,
    proj_bias,
    second_gain,
    second_shift,
    up_weight,
    up_bias,
    down_weight,
    down_bias,
    cotangent,
    live_clips,
):
    col = lax.axis_index("col")
    width, hidden_width = (qkv_weight.shape[3], up_weight.shape[2])
    features = inputs.shape[3]
    sizes = Sizes(
        2 * inputs.shape[2], features, width, hidden_width, lax.axis_size("row") // 2
    )
    vector_parts = (
        first_gain,
        first_shift,
        proj_bias,
        second_gain,
        second_shift,
        down_bias,
        query_bias,
        value_bias,
        up_bias,
    )
    sent, final, lse, states, values, cot, early, late, vectors, *saved = run_forward(
        sizes,
        inputs,
        cotangent,
        (qkv_weight, proj_weight, up_weight, down_weight),
        vector_parts,
    )
    states, grads_in, sums, own_early, own_late = run_backward(
        sizes, live_clips, cot, values, sent, final, vectors, lse, early, late, states, saved
    )
    split_out = lax.dynamic_slice(sums, (0, sizes.tails + col * sizes.tail), (1, sizes.tail))
    whole_out = [sums[:, index * features : (index + 1) * features] for index in range(6)]
    return (
        states[None, :, None],
        grads_in.astype(jnp.float32)[None, :, None],
        whole_out[0],
        whole_out[1],
        jnp.stack([own_early[:, part * width : (part + 1) * width] for part in range(3)])[None],
        split_out[:, :width],
        split_out[:, width : 2 * width],
        own_early[:, 3 * width :].T[None],
        whole_out[2],
        whole_out[3],
        whole_out[4],
        own_late[:, :hidden_width][None],
        split_out[:, 2 * width :],
        own_late[:, hidden_width:].T[None],
        whole_out[5],
    )


def one_clip_each(mesh):
    sizes = dict(mesh.shape)
    return sizes["pipe"] == 2 and sizes["col"] == 2


def choose(mesh):
    def body(*arrays):
        fits = one_clip_each(mesh) and arrays[0].shape[:2] == (4, 1)
        return (on_device_clip if fits else on_device)(*arrays)

    return body


def solution(mesh):
    placed = (
        P(None, "row", "col", None),
        P("pipe", None),
        P("pipe", None),
        P("pipe", None, "row", "col"),
        P("pipe", "col"),
        P("pipe", "col"),
        P("pipe", "col", "row"),
        P("pipe", None),
        P("pipe", None),
        P("pipe", None),
        P("pipe", "row", "col"),
        P("pipe", "col"),
        P("pipe", "col", "row"),
        P("pipe", None),
        P(None, "row", "col", None),
        P(None, "row"),
    )
    return jax.shard_map(
        choose(mesh),
        mesh=mesh,
        in_specs=placed,
        out_specs=(
            P("pipe", None, "row", "col", None),
            P("pipe", None, "row", "col", None),
            P("pipe", None),
            P("pipe", None),
            P("pipe", None, "row", "col"),
            P("pipe", "col"),
            P("pipe", "col"),
            P("pipe", "col", "row"),
            P("pipe", None),
            P("pipe", None),
            P("pipe", None),
            P("pipe", "row", "col"),
            P("pipe", "col"),
            P("pipe", "col", "row"),
            P("pipe", None),
        ),
        check_vma=False,
    )
```

```python
import functools
import math

import jax
import jax.numpy as jnp
from jax import lax
from jax.experimental import pallas as pl
from jax.experimental.pallas import tpu as pltpu
from jax.sharding import PartitionSpec as P

HD = 64


epsilon = 1e-05


def from_behind(value, axis, steps):
    count = lax.axis_size(axis)
    first, last = (max(0, -steps), min(count, count - steps))
    return lax.ppermute(value, axis, [(source, source + steps) for source in range(first, last)])


def exact_gelu(values):
    return jax.nn.gelu(values, approximate=False)


def spread_features(normed):
    return lax.all_gather(normed, "col", axis=0, tiled=True)


def sum_columns(partial_rows):
    return lax.psum_scatter(partial_rows, "col", scatter_dimension=0, tiled=True)


def spread_grads(grad_low):
    return lax.all_gather(grad_low, "col", axis=0, tiled=True)


def sum_grad_columns(partial_rows):
    return lax.psum_scatter(partial_rows, "col", scatter_dimension=0, tiled=True)


def norm_forward(values, gain, shift):
    row_mean = jnp.mean(values, axis=-1, keepdims=True)
    row_var = jnp.mean(jnp.square(values - row_mean), axis=-1, keepdims=True)
    inv_std = lax.rsqrt(row_var + epsilon)
    centered = (values - row_mean) * inv_std
    return (centered, inv_std[:, 0], (centered * gain + shift).astype(jnp.bfloat16))


def norm_backward(grad_norm, centered, inv_std, gain):
    grad_gain = jnp.sum(grad_norm * centered, axis=0)
    grad_shift = jnp.sum(grad_norm, axis=0)
    scaled = grad_norm * gain
    first = jnp.mean(scaled, axis=-1, keepdims=True)
    second = jnp.mean(scaled * centered, axis=-1, keepdims=True)
    grad_in = inv_std[:, None] * (scaled - first - centered * second)
    return (grad_in, grad_gain, grad_shift)


def attention_probs(query_heads, key_heads):
    score_scale = 1.0 / math.sqrt(HD)
    scores = (
        jnp.einsum("qhd,khd->hqk", query_heads, key_heads, preferred_element_type=jnp.float32)
        * score_scale
    )
    return jax.nn.softmax(scores, axis=-1)


def layer_forward(values, weights, params):
    qkv_full, proj_full, up_full, down_full = weights
    (
        gain_one,
        shift_one,
        query_bias,
        value_bias,
        proj_bias,
        gain_two,
        shift_two,
        up_bias,
        down_bias,
    ) = params
    head_count = qkv_full.shape[2] // HD
    centered_one, inv_one, normed_one = norm_forward(values, gain_one, shift_one)
    attn_input = spread_features(normed_one)
    frame_count = attn_input.shape[0]
    projected = jnp.einsum("sd,jde->jse", attn_input, qkv_full, preferred_element_type=jnp.float32)
    query_heads = (
        (projected[0] + query_bias).astype(jnp.bfloat16).reshape(frame_count, head_count, HD)
    )
    key_heads = projected[1].astype(jnp.bfloat16).reshape(frame_count, head_count, HD)
    value_heads = (
        (projected[2] + value_bias).astype(jnp.bfloat16).reshape(frame_count, head_count, HD)
    )
    softmax_out = attention_probs(query_heads, key_heads)
    context = jnp.einsum(
        "hqk,khd->qhd",
        softmax_out.astype(jnp.bfloat16),
        value_heads,
        preferred_element_type=jnp.float32,
    )
    context = context.reshape(frame_count, head_count * HD).astype(jnp.bfloat16)
    attended = (
        sum_columns(jnp.dot(context, proj_full, preferred_element_type=jnp.float32)) + proj_bias
    )
    hidden = values + attended
    centered_two, inv_two, normed_two = norm_forward(hidden, gain_two, shift_two)
    mlp_input = spread_features(normed_two)
    pre_act = jnp.dot(mlp_input, up_full, preferred_element_type=jnp.float32) + up_bias
    activated = exact_gelu(pre_act).astype(jnp.bfloat16)
    output = (
        hidden
        + sum_columns(jnp.dot(activated, down_full, preferred_element_type=jnp.float32))
        + down_bias
    )
    kept = (
        centered_one,
        inv_one,
        attn_input,
        query_heads,
        key_heads,
        value_heads,
        context,
        centered_two,
        inv_two,
        mlp_input,
        pre_act,
        activated,
    )
    return (output, kept)


def layer_backward(grad_out, kept, weights, params):
    qkv_full, proj_full, up_full, down_full = weights
    (
        gain_one,
        shift_one,
        query_bias,
        value_bias,
        proj_bias,
        gain_two,
        shift_two,
        up_bias,
        down_bias,
    ) = params
    (
        centered_one,
        inv_one,
        attn_input,
        query_heads,
        key_heads,
        value_heads,
        context,
        centered_two,
        inv_two,
        mlp_input,
        pre_act,
        activated,
    ) = kept
    frame_count = attn_input.shape[0]
    score_scale = 1.0 / math.sqrt(HD)
    grad_down_bias = jnp.sum(grad_out, axis=0)
    down_grad = spread_grads(grad_out.astype(jnp.bfloat16))
    grad_down = jnp.einsum("sf,sd->fd", activated, down_grad, preferred_element_type=jnp.float32)
    grad_act = jnp.einsum("sd,fd->sf", down_grad, down_full, preferred_element_type=jnp.float32)
    unused, gelu_pull = jax.vjp(exact_gelu, pre_act)
    grad_pre = gelu_pull(grad_act)[0]
    grad_up_bias = jnp.sum(grad_pre, axis=0)
    grad_pre_low = grad_pre.astype(jnp.bfloat16)
    grad_up = jnp.einsum("sd,sf->df", mlp_input, grad_pre_low, preferred_element_type=jnp.float32)
    grad_normed_two = sum_grad_columns(
        jnp.einsum("sf,df->sd", grad_pre_low, up_full, preferred_element_type=jnp.float32)
    )
    grad_hidden_norm, grad_gain_two, grad_shift_two = norm_backward(
        grad_normed_two, centered_two, inv_two, gain_two
    )
    grad_hidden = grad_out + grad_hidden_norm
    grad_proj_bias = jnp.sum(grad_hidden, axis=0)
    proj_grad = spread_grads(grad_hidden.astype(jnp.bfloat16))
    grad_proj = jnp.einsum("se,sd->ed", context, proj_grad, preferred_element_type=jnp.float32)
    grad_context = jnp.einsum("sd,ed->se", proj_grad, proj_full, preferred_element_type=jnp.float32)
    grad_context = grad_context.astype(jnp.bfloat16).reshape(query_heads.shape)
    softmax_out = attention_probs(query_heads, key_heads)
    grad_probs = jnp.einsum(
        "qhd,khd->hqk", grad_context, value_heads, preferred_element_type=jnp.float32
    )
    grad_value = jnp.einsum(
        "hqk,qhd->khd",
        softmax_out.astype(jnp.bfloat16),
        grad_context,
        preferred_element_type=jnp.float32,
    )
    grad_scores = softmax_out * (
        grad_probs - jnp.sum(softmax_out * grad_probs, axis=-1, keepdims=True)
    )
    scores_low = grad_scores.astype(jnp.bfloat16)
    grad_query = (
        jnp.einsum("hqk,khd->qhd", scores_low, key_heads, preferred_element_type=jnp.float32)
        * score_scale
    )
    grad_key = (
        jnp.einsum("hqk,qhd->khd", scores_low, query_heads, preferred_element_type=jnp.float32)
        * score_scale
    )
    grad_query = grad_query.reshape(frame_count, -1)
    grad_key = grad_key.reshape(frame_count, -1)
    grad_value = grad_value.reshape(frame_count, -1)
    grad_query_bias = jnp.sum(grad_query, axis=0)
    grad_value_bias = jnp.sum(grad_value, axis=0)
    grad_qkv_low = jnp.stack([grad_query, grad_key, grad_value]).astype(jnp.bfloat16)
    grad_qkv = jnp.einsum(
        "sd,jse->jde", attn_input, grad_qkv_low, preferred_element_type=jnp.float32
    )
    grad_normed_one = sum_grad_columns(
        jnp.einsum("jse,jde->sd", grad_qkv_low, qkv_full, preferred_element_type=jnp.float32)
    )
    grad_in_norm, grad_gain_one, grad_shift_one = norm_backward(
        grad_normed_one, centered_one, inv_one, gain_one
    )
    grad_in = grad_hidden + grad_in_norm
    weight_grads = (grad_qkv, grad_proj, grad_up, grad_down)
    vector_grads = (
        grad_gain_one,
        grad_shift_one,
        grad_query_bias,
        grad_value_bias,
        grad_proj_bias,
        grad_gain_two,
        grad_shift_two,
        grad_up_bias,
        grad_down_bias,
    )
    return (grad_in, weight_grads, vector_grads)


def store_slot(buffer, slot_index, is_valid, value):
    current = lax.dynamic_index_in_dim(buffer, slot_index, 0, keepdims=False)
    return lax.dynamic_update_index_in_dim(
        buffer, jnp.where(is_valid, value, current), slot_index, 0
    )


def reduce_end(weight_acc):
    return (
        lax.psum_scatter(
            weight_acc[0].astype(jnp.bfloat16), "row", scatter_dimension=1, tiled=True
        ).astype(jnp.float32),
        lax.psum_scatter(
            weight_acc[1].astype(jnp.bfloat16), "row", scatter_dimension=1, tiled=True
        ).astype(jnp.float32),
        lax.psum_scatter(
            weight_acc[2].astype(jnp.bfloat16), "row", scatter_dimension=0, tiled=True
        ).astype(jnp.float32),
        lax.psum_scatter(
            weight_acc[3].astype(jnp.bfloat16), "row", scatter_dimension=1, tiled=True
        ).astype(jnp.float32),
    )


def on_device(
    inputs,
    first_gain,
    first_shift,
    qkv_weight,
    query_bias,
    value_bias,
    proj_weight,
    proj_bias,
    second_gain,
    second_shift,
    up_weight,
    up_bias,
    down_weight,
    down_bias,
    cotangent,
    live_clips,
):
    micro_count = inputs.shape[0]
    row_count = inputs.shape[2]
    feature_count = inputs.shape[3]
    section_index = lax.axis_index("pipe")
    weights = (
        lax.all_gather(qkv_weight[0], "row", axis=1, tiled=True),
        lax.all_gather(proj_weight[0], "row", axis=1, tiled=True),
        lax.all_gather(up_weight[0], "row", axis=0, tiled=True),
        lax.all_gather(down_weight[0], "row", axis=1, tiled=True),
    )
    params = (
        first_gain[0],
        first_shift[0],
        query_bias[0],
        value_bias[0],
        proj_bias[0],
        second_gain[0],
        second_shift[0],
        up_bias[0],
        down_bias[0],
    )
    kept_buffers = ()
    zero_rows = jnp.zeros((row_count, feature_count), jnp.bfloat16)
    zero_stack = jnp.zeros((micro_count, row_count, feature_count), jnp.bfloat16)
    own_inputs = inputs[:, 0]

    def forward_tick(state_carry, tick_index):
        received, outputs, layer_inputs, buffers = state_carry
        batch_index = tick_index - section_index
        is_valid = (batch_index >= 0) & (batch_index < micro_count)
        slot_index = jnp.clip(batch_index, 0, micro_count - 1)
        own_input = lax.dynamic_index_in_dim(
            own_inputs, jnp.minimum(tick_index, micro_count - 1), 0, keepdims=False
        )
        layer_input = jnp.where(section_index == 0, own_input, received)
        output, kept = layer_forward(layer_input.astype(jnp.float32), weights, params)
        output_low = output.astype(jnp.bfloat16)
        passed = from_behind(output_low, "pipe", 1)
        outputs = store_slot(outputs, slot_index, is_valid, output_low)
        layer_inputs = store_slot(layer_inputs, slot_index, is_valid, layer_input)
        return ((passed, outputs, layer_inputs, buffers), None)

    tick_range = jnp.arange(micro_count + 1)
    forward_out, unused = lax.scan(
        forward_tick, (zero_rows, zero_stack, zero_stack, kept_buffers), tick_range
    )
    unused_rows, outputs, layer_inputs, kept_buffers = forward_out
    weight_acc = tuple((jnp.zeros(part.shape, jnp.float32) for part in weights))
    vector_acc = tuple((jnp.zeros(part.shape, jnp.float32) for part in params))
    grads_init = jnp.zeros((micro_count, row_count, feature_count), jnp.float32)
    live_rows = live_clips[:, 0]
    cot_rows_all = cotangent[:, 0]

    def backward_tick(state_carry, tick_index):
        received, grads_in, weight_sum, vector_sum = state_carry
        batch_index = micro_count - tick_index - section_index
        is_valid = (batch_index >= 0) & (batch_index < micro_count)
        slot_index = jnp.clip(batch_index, 0, micro_count - 1)
        cot_rows = lax.dynamic_index_in_dim(cot_rows_all, slot_index, 0, keepdims=False).astype(
            jnp.float32
        )
        live_flag = lax.dynamic_index_in_dim(live_rows, slot_index, 0, keepdims=False).astype(
            jnp.float32
        )
        grad_out = jnp.where(
            section_index == 1, cot_rows * live_flag, received.astype(jnp.float32)
        ) * is_valid.astype(jnp.float32)
        stored_input = lax.dynamic_index_in_dim(layer_inputs, slot_index, 0, keepdims=False)
        kept = layer_forward(stored_input.astype(jnp.float32), weights, params)[1]
        grad_in, weight_grads, vector_grads = layer_backward(grad_out, kept, weights, params)
        passed = from_behind(grad_in.astype(jnp.bfloat16), "pipe", -1)
        grads_in = store_slot(grads_in, slot_index, is_valid, grad_in)
        weight_sum = jax.tree.map(jnp.add, weight_sum, weight_grads)
        vector_sum = jax.tree.map(jnp.add, vector_sum, vector_grads)
        return ((passed, grads_in, weight_sum, vector_sum), None)

    backward_out, unused_two = lax.scan(
        backward_tick, (zero_rows, grads_init, weight_acc, vector_acc), tick_range
    )
    unused_grad, grads_in, weight_acc, vector_acc = backward_out
    weight_out = reduce_end(weight_acc)
    split_out = lax.psum((vector_acc[2], vector_acc[3], vector_acc[7]), "row")
    whole_out = lax.psum(
        (vector_acc[0], vector_acc[1], vector_acc[4], vector_acc[5], vector_acc[6], vector_acc[8]),
        ("row", "col"),
    )
    return (
        outputs[None, :, None],
        grads_in[None, :, None],
        whole_out[0][None],
        whole_out[1][None],
        weight_out[0][None],
        split_out[0][None],
        split_out[1][None],
        weight_out[1][None],
        whole_out[2][None],
        whole_out[3][None],
        whole_out[4][None],
        weight_out[2][None],
        split_out[2][None],
        weight_out[3][None],
        whole_out[5][None],
    )


def contract(left, right, left_dim, right_dim):
    return lax.dot_general(
        left, right, (((left_dim,), (right_dim,)), ((), ())), preferred_element_type=jnp.float32
    )


TILE = 256
QUERY_TILE = 512
CHUNK = 512
LANES = 2 * HD
VMEM_BYTES = 60 * 1024 * 1024
ERFC_SCALE = 0.4
ERFC_TERMS = (
    0.23192221664065504,
    0.1618227850291895,
    0.4682761333792345,
    -0.37091039694171485,
    0.7091488547855423,
    -0.20025962054546065,
)


def gelu_and_slope(values):
    size = jnp.abs(values) * math.sqrt(0.5)
    turn = 1.0 / (1.0 + ERFC_SCALE * size)
    series = ERFC_TERMS[-1]
    for term in ERFC_TERMS[-2::-1]:
        series = series * turn + term
    bell = jnp.exp(-(size * size))
    tail = 0.5 * (series * turn * bell)
    below = jnp.where(values >= 0.0, 1.0 - tail, tail)
    return (values * below, below + values * bell * (1.0 / math.sqrt(2.0 * math.pi)))


def norm_rows(values):
    centered = values - jnp.mean(values, axis=-1, keepdims=True)
    inv_std = lax.rsqrt(jnp.mean(centered * centered, axis=-1, keepdims=True) + epsilon)
    return (centered * inv_std, inv_std)


def norm_rows_backward(grad, centered, inv_std, gain):
    scaled = grad * gain
    first = jnp.mean(scaled, axis=-1, keepdims=True)
    second = jnp.mean(scaled * centered, axis=-1, keepdims=True)
    return inv_std * (scaled - first - centered * second)


def tile_rows(index):
    return pl.ds(pl.multiple_of(index * TILE, TILE), TILE)


def lane_block(start):
    return pl.ds(pl.multiple_of(start, LANES), LANES)


def run_hooks(hooks, index):
    for when, hook in hooks.items():
        pl.when(index == when)(hook)


class Sizes:
    def __init__(self, frames, features, width, hidden, depth):
        self.frames = frames
        self.half = frames // 2
        self.features = features
        self.width = width
        self.hidden = hidden
        self.depth = depth
        self.block = features // (2 * depth)
        self.tiles = frames // TILE
        self.per = width // LANES
        self.tails = 6 * features
        self.tail = 2 * width + hidden
        self.vector = self.tails + self.tail
        self.sums = self.tails + 2 * self.tail
        self.early = (2 * depth, self.block, 4 * width)
        self.late = (2 * depth, self.block, 2 * hidden)


class Wires:
    def __init__(self, sizes, send, recv):
        self.depth = sizes.depth
        self.send, self.recv = (send, recv)
        self.used = 0
        self.pipe = lax.axis_index("pipe")
        self.row = lax.axis_index("row")
        self.col = lax.axis_index("col")
        self.plane = lax.div(self.row, 2)
        self.core = lax.rem(self.row, 2)
        self.place = 2 * self.pipe + self.col
        self.across_x = (1 - self.pipe, self.row, self.col)
        self.across_y = (self.pipe, self.row, 1 - self.col)
        self.across_both = (1 - self.pipe, self.row, 1 - self.col)
        self.across_core = (self.pipe, 2 * self.plane + 1 - self.core, self.col)

    def plane_at(self, step):
        return lax.rem(self.plane + step, self.depth)

    def along_z(self, step):
        return (self.pipe, 2 * self.plane_at(step) + self.core, self.col)

    def greet(self):
        barrier = pltpu.get_barrier_semaphore()
        partners = [self.across_x, self.across_y, self.across_both, self.across_core]
        partners += [self.along_z(step) for step in range(1, self.depth)]
        for partner in partners:
            pl.semaphore_signal(
                barrier, inc=1, device_id=partner, device_id_type=pl.DeviceIdType.MESH
            )
        pl.semaphore_wait(barrier, len(partners))

    def copy(self, source, target, partner):
        number = self.used
        self.used += 1
        return pltpu.make_async_remote_copy(
            src_ref=source,
            dst_ref=target,
            send_sem=self.send.at[number],
            recv_sem=self.recv.at[number],
            device_id=partner,
            device_id_type=pl.DeviceIdType.MESH,
        )


class Local:
    def __init__(self, sems):
        self.sems = sems
        self.used = 0
        self.open = []

    def start(self, source, target):
        copy = pltpu.make_async_copy(source, target, self.sems.at[self.used])
        self.used += 1
        copy.start()
        return copy

    def keep(self, source, target):
        self.open.append(self.start(source, target))

    def later(self, source, target):
        copy = pltpu.make_async_copy(source, target, self.sems.at[self.used])
        self.used += 1
        self.open.append(copy)
        return copy

    def finish(self):
        for copy in self.open:
            copy.wait()


def whole_weight(weights, index, start, size):
    depth = weights.shape[1] // 2
    columns = slice(start, start + size)
    return jnp.concatenate(
        [
            weights[index, core * depth + plane, :, columns]
            for plane in range(depth)
            for core in range(2)
        ],
        axis=0,
    )


def attention_forward(sizes, qkv, context, lse, hooks):
    width = sizes.width
    score_scale = 1.0 / math.sqrt(HD)

    def one_pair(pair, carry):
        part, index = (lax.div(pair, sizes.per), lax.rem(pair, sizes.per))
        base = part * (3 * width) + index * LANES
        for start in range(0, sizes.frames, QUERY_TILE):
            rows = slice(start, start + QUERY_TILE)
            query_pair = qkv[rows, lane_block(base)]
            key_pair = qkv[:, lane_block(base + width)]
            value_pair = qkv[:, lane_block(base + 2 * width)]
            parts = []
            for head in range(2):
                lanes = slice(head * HD, (head + 1) * HD)
                scaled = query_pair[:, lanes] * jnp.asarray(score_scale, jnp.bfloat16)
                scores = contract(scaled, key_pair[:, lanes], 1, 1)
                top = jnp.max(scores, axis=1, keepdims=True)
                weights = jnp.exp(scores - top)
                total = jnp.sum(weights, axis=1, keepdims=True)
                mixed = contract(weights.astype(jnp.bfloat16), value_pair[:, lanes], 1, 0)
                parts.append(mixed / total)
                lse[pair, head : head + 1, rows] = (top + jnp.log(total)).reshape(1, QUERY_TILE)
            context[rows, lane_block(pair * LANES)] = jnp.concatenate(parts, axis=1).astype(
                jnp.bfloat16
            )
        run_hooks(hooks, pair)
        return carry

    lax.fori_loop(0, 2 * sizes.per, one_pair, 0)


def attention_backward(
    sizes, qkv, context, grad_context, lse, add_query_bias, add_value_bias, hooks
):
    width = sizes.width
    score_scale = 1.0 / math.sqrt(HD)

    def one_pair(pair, carry):
        part, index = (lax.div(pair, sizes.per), lax.rem(pair, sizes.per))
        base = part * (3 * width) + index * LANES
        key_pair = qkv[:, lane_block(base + width)]
        value_pair = qkv[:, lane_block(base + 2 * width)]
        grad_keys = [None, None]
        grad_values = [None, None]
        query_total = jnp.zeros((1, LANES), jnp.float32)
        for start in range(0, sizes.frames, TILE):
            rows = slice(start, start + TILE)
            query_pair = qkv[rows, lane_block(base)]
            grad_pair = grad_context[rows, lane_block(pair * LANES)]
            context_pair = context[rows, lane_block(pair * LANES)]
            products = (grad_pair.astype(jnp.float32) * context_pair.astype(jnp.float32)).T
            parts = []
            for head in range(2):
                lanes = slice(head * HD, (head + 1) * HD)
                keys = key_pair[:, lanes]
                grads = grad_pair[:, lanes]
                scaled = query_pair[:, lanes] * jnp.asarray(score_scale, jnp.bfloat16)
                scores = contract(keys, scaled, 1, 1)
                probs = jnp.exp(scores - lse[pair, head : head + 1, rows])
                grad_probs = contract(value_pair[:, lanes], grads, 1, 1)
                delta = jnp.sum(products[lanes, :], axis=0, keepdims=True)
                low_scores = (probs * (grad_probs - delta)).astype(jnp.bfloat16)
                value_part = contract(probs.astype(jnp.bfloat16), grads, 1, 0)
                key_part = contract(low_scores, scaled, 1, 0)
                grad_values[head] = value_part if start == 0 else grad_values[head] + value_part
                grad_keys[head] = key_part if start == 0 else grad_keys[head] + key_part
                parts.append(contract(keys, low_scores, 0, 0))
            turned = jnp.concatenate(parts, axis=0).T * score_scale
            query_total = query_total + jnp.sum(turned, axis=0, keepdims=True)
            qkv[rows, lane_block(base)] = turned.astype(jnp.bfloat16)
        key_grad = jnp.concatenate(grad_keys, axis=1)
        value_grad = jnp.concatenate(grad_values, axis=1)
        qkv[:, lane_block(base + width)] = key_grad.astype(jnp.bfloat16)
        qkv[:, lane_block(base + 2 * width)] = value_grad.astype(jnp.bfloat16)
        add_query_bias(part, index, query_total)
        add_value_bias(part, index, jnp.sum(value_grad, axis=0, keepdims=True))
        run_hooks(hooks, pair)
        return carry

    lax.fori_loop(0, 2 * sizes.per, one_pair, 0)


def vector_reader(sizes, vectors, layer):
    features = sizes.features

    def whole(index):
        return vectors[2 * layer, :, index * features : (index + 1) * features]

    def split(part, start, size):
        first = sizes.tails + start
        return vectors[2 * layer + part, :, first : first + size]

    return (whole, split)


def forward_norm(sizes, layer, values, vectors, normed):
    whole, split = vector_reader(sizes, vectors, layer)

    def one_tile(index, carry):
        rows = tile_rows(index)
        centered, unused = norm_rows(values[rows, :].astype(jnp.float32))
        normed[rows, :] = (centered * whole(0) + whole(1)).astype(jnp.bfloat16)
        return carry

    lax.fori_loop(0, sizes.tiles, one_tile, 0)


def forward_qkv(sizes, layer, normed, early, vectors, qkv):
    width = sizes.width
    whole, split = vector_reader(sizes, vectors, layer)

    def one_tile(index, carry):
        rows = tile_rows(index)
        for part in range(2):
            for kind in range(3):
                result = contract(
                    normed[rows, :],
                    whole_weight(early, 2 * layer + part, kind * width, width),
                    1,
                    0,
                )
                if kind == 0:
                    result = result + split(part, 0, width)
                if kind == 2:
                    result = result + split(part, width, width)
                first = (3 * part + kind) * width
                qkv[rows, first : first + width] = result.astype(jnp.bfloat16)
        return carry

    lax.fori_loop(0, sizes.tiles, one_tile, 0)


def forward_rest(
    sizes, layer, values, early, late, vectors, context, hidden, active, slope, output, hooks
):
    width, size = (sizes.width, sizes.hidden)
    whole, split = vector_reader(sizes, vectors, layer)

    def one_tile(index, carry):
        rows = tile_rows(index)
        total = values[rows, :].astype(jnp.float32) + whole(2)
        for part in range(2):
            total = total + contract(
                context[rows, part * width : (part + 1) * width],
                whole_weight(early, 2 * layer + part, 3 * width, width),
                1,
                1,
            )
        hidden[rows, :] = total
        centered, unused = norm_rows(total)
        normed = (centered * whole(3) + whole(4)).astype(jnp.bfloat16)
        total = total + whole(5)
        for part in range(2):
            for start in range(0, size, CHUNK):
                weights = late.at[2 * layer + part]
                pre_act = contract(
                    normed, whole_weight(late, 2 * layer + part, start, CHUNK), 1, 0
                ) + split(part, 2 * width + start, CHUNK)
                act, act_slope = gelu_and_slope(pre_act)
                act = act.astype(jnp.bfloat16)
                first = part * size + start
                active[rows, first : first + CHUNK] = act
                slope[rows, first : first + CHUNK] = act_slope.astype(jnp.bfloat16)
                total = total + contract(
                    act, whole_weight(late, 2 * layer + part, size + start, CHUNK), 1, 1
                )
        output[rows, :] = total.astype(jnp.bfloat16)
        run_hooks(hooks, index)
        return carry

    lax.fori_loop(0, sizes.tiles, one_tile, 0)


class Gather:
    def __init__(self, wires, block, full):
        self.block, self.full = (block, full)
        depth, half = (wires.depth, block.shape[0] // 2)
        middle = block.shape[1] // 2
        left, right, every = (pl.ds(0, middle), pl.ds(middle, middle), pl.ds(0, 2 * middle))
        slot = wires.core * depth + wires.plane
        slots = pl.ds(wires.core * depth, depth)
        mine = pl.ds(pl.multiple_of(wires.pipe * half, half), half)
        theirs = pl.ds(pl.multiple_of((1 - wires.pipe) * half, half), half)
        both = pl.ds(0, 2 * half)

        def send(where, partner):
            return wires.copy(full.at[where], full.at[where], partner)

        own = 2 * wires.pipe + wires.col
        self.own, self.mine = ((own, slot, mine), mine)
        self.x = wires.copy(block.at[theirs], full.at[own, slot, theirs], wires.across_x)
        self.z, self.first, self.second, self.core = ([], [], [], [])
        for layer in range(2):
            index = 2 * layer + wires.col
            pair = pl.ds(2 * layer, 2)
            self.z.append(
                [
                    send((index, slot, mine, every), wires.along_z(step))
                    for step in range(1, depth)
                ]
            )
            self.first.append(
                [
                    send((index, slots, mine, left), wires.across_x),
                    send((index, slots, mine, right), wires.across_y),
                ]
            )
            self.second.append(
                [
                    send((index, slots, both, left), wires.across_y),
                    send((pair, slots, mine, right), wires.across_x),
                ]
            )
            self.core.append([send((pair, slots, both, every), wires.across_core)])

    def place_own(self):
        self.full[self.own] = self.block[self.mine, :]

    def move(self, arriving, leaving):
        for copy in arriving:
            copy.wait_recv()
        for copy in leaving:
            copy.start()

    def start_z(self, layer):
        self.move([], self.z[layer])

    def end_z(self, layer):
        self.move(self.z[layer], self.first[layer])

    def end_first(self, layer):
        self.move(self.first[layer], self.second[layer])

    def end_second(self, layer):
        self.move(self.second[layer], self.core[layer])

    def arrive(self, layer):
        self.move(self.core[layer], [])

    def finish(self):
        self.x.wait_send()
        for layer in range(2):
            for copies in (self.z, self.first, self.second, self.core):
                for copy in copies[layer]:
                    copy.wait_send()


def forward_kernel(
    sizes,
    inputs_ref,
    cot_ref,
    qkv_weight,
    proj_weight,
    up_weight,
    down_weight,
    *rest,
):
    vector_parts = rest[:9]
    forward_body(
        sizes,
        inputs_ref,
        cot_ref,
        (qkv_weight, proj_weight, up_weight, down_weight),
        vector_parts,
        *rest[9:],
    )


def forward_body(
    sizes,
    inputs_ref,
    cot_ref,
    own_weights,
    vector_parts,
    sent_ref,
    final_ref,
    lse_ref,
    states_out,
    x_out,
    cot_out,
    early_out,
    late_out,
    vector_out,
    qkv_out,
    context_out,
    hidden_out,
    active_out,
    slope_out,
    qkv,
    context,
    hidden,
    active,
    slope,
    x,
    cot,
    early,
    late,
    vectors,
    normed,
    early_block,
    late_block,
    vector_block,
    send,
    recv,
    sems,
):
    half = sizes.half
    qkv_weight, proj_weight, up_weight, down_weight = own_weights
    wires = Wires(sizes, send, recv)
    local = Local(sems)
    own_rows = pl.ds(pl.multiple_of(wires.col * half, half), half)
    other_place = 2 * wires.pipe + 1 - wires.col
    own_x = local.start(inputs_ref.at[wires.place, 0], x.at[own_rows])
    own_cot = local.start(cot_ref.at[wires.place, 0], cot.at[own_rows])
    width, size = (sizes.width, sizes.hidden)
    for kind in range(3):
        early_block[:, kind * width : (kind + 1) * width] = qkv_weight[0, kind]
    early_block[:, 3 * width :] = proj_weight[0].T
    start = 0
    for part in vector_parts:
        vector_block[:, start : start + part.shape[1]] = part[...]
        start += part.shape[1]
    early_gather = Gather(wires, early_block, early)
    late_gather = Gather(wires, late_block, late)
    early_gather.place_own()
    vectors[wires.place] = vector_block[...]
    wires.greet()
    early_gather.x.start()
    vector_copies = [
        wires.copy(vector_block, vectors.at[wires.place], partner)
        for partner in (wires.across_x, wires.across_y, wires.across_both)
    ]
    for copy in vector_copies:
        copy.start()
    x_copy = wires.copy(inputs_ref.at[other_place, 0], x.at[own_rows], wires.across_y)
    x_copy.start()
    late_block[:, :size] = up_weight[0]
    late_block[:, size:] = down_weight[0].T
    late_gather.place_own()
    late_gather.x.start()
    trade = Trade(sizes, wires, local, 0, sent_ref, states_out)
    cot_copy = wires.copy(cot_ref.at[other_place, 0], cot.at[own_rows], wires.across_y)
    early_gather.x.wait_recv()
    early_gather.start_z(0)
    own_x.wait()
    x_copy.wait_recv()
    for copy in vector_copies:
        copy.wait_recv()
    early_gather.end_z(0)
    late_gather.x.wait_recv()
    late_gather.start_z(0)
    forward_norm(sizes, 0, x, vectors, normed)
    early_gather.end_first(0)
    local.keep(x, x_out)
    early_gather.end_second(0)

    def second_pair():
        late_gather.end_first(0)

    def third_pair():
        late_gather.end_second(0)
        early_gather.end_z(1)
        late_gather.start_z(1)

    def later_second_pair():
        late_gather.end_second(1)
        cot_copy.start()
        trade.start()

    attention_hooks = [{0: second_pair, 2: third_pair}, {1: later_second_pair}]
    rest_hooks = [
        {
            0: functools.partial(early_gather.end_first, 1),
            1: functools.partial(late_gather.end_z, 1),
            2: functools.partial(early_gather.end_second, 1),
            3: functools.partial(late_gather.end_first, 1),
        },
        {},
    ]
    for layer in range(2):
        values = (x, sent_ref)[layer]
        output = (sent_ref, final_ref)[layer]
        if layer == 1:
            forward_norm(sizes, 1, values, vectors, normed)
        early_gather.arrive(layer)
        both = pl.ds(2 * layer, 2)
        local.keep(early.at[both], early_out.at[both])
        if layer == 0:
            late_gather.end_z(0)
            early_gather.start_z(1)
        forward_qkv(sizes, layer, normed, early, vectors, qkv.at[layer])
        local.keep(qkv.at[layer], qkv_out.at[layer])
        attention_forward(
            sizes, qkv.at[layer], context.at[layer], lse_ref.at[layer], attention_hooks[layer]
        )
        local.keep(context.at[layer], context_out.at[layer])
        late_gather.arrive(layer)
        local.keep(late.at[both], late_out.at[both])
        saves = []
        for first in (0, half):
            rows = pl.ds(first, half)
            saves.append(
                [
                    local.later(source.at[layer, rows], target.at[layer, rows])
                    for source, target in (
                        (hidden, hidden_out),
                        (active, active_out),
                        (slope, slope_out),
                    )
                ]
            )

        def save_half(copies=saves[0], hook=rest_hooks[layer].get(sizes.tiles // 2 - 1)):
            for copy in copies:
                copy.start()
            if hook is not None:
                hook()

        rest_hooks[layer][sizes.tiles // 2 - 1] = save_half
        forward_rest(
            sizes,
            layer,
            values,
            early,
            late,
            vectors,
            context.at[layer],
            hidden.at[layer],
            active.at[layer],
            slope.at[layer],
            output,
            rest_hooks[layer],
        )
        for copy in saves[1]:
            copy.start()
    own_cot.wait()
    cot_copy.wait_recv()
    local.keep(cot, cot_out)
    vector_out[...] = vectors[...]
    for copy in vector_copies + [x_copy, cot_copy]:
        copy.wait_send()
    early_gather.finish()
    late_gather.finish()
    trade.finish()
    local.finish()


def saved_shapes(sizes):
    frames, features = (sizes.frames, sizes.features)
    return [
        ((2, frames, 6 * sizes.width), jnp.bfloat16),
        ((2, frames, 2 * sizes.width), jnp.bfloat16),
        ((2, frames, features), jnp.float32),
        ((2, frames, 2 * sizes.hidden), jnp.bfloat16),
        ((2, frames, 2 * sizes.hidden), jnp.bfloat16),
    ]


def run_forward(sizes, inputs, cot, weights, vector_parts):
    frames, features = (sizes.frames, sizes.features)
    vmem = pl.BlockSpec(memory_space=pltpu.VMEM)
    hbm = pl.BlockSpec(memory_space=pl.ANY)
    saved = saved_shapes(sizes)
    low = jnp.bfloat16
    rows = ((frames, features), low)
    early, late = (((4,) + sizes.early, low), ((4,) + sizes.late, low))
    vectors = ((4, 1, sizes.vector), jnp.float32)
    states = ((4, sizes.half, features), low)
    blocks = [(sizes.early[1:], low), (sizes.late[1:], low), (vectors[0][1:], jnp.float32)]
    outs = [rows, rows, ((2, 2 * sizes.per, 2, frames), jnp.float32)]
    outs += [states, rows, rows, early, late, vectors] + saved
    count = 2 * (1 + 2 * (sizes.depth - 1 + 5)) + 5 + 3
    return pl.pallas_call(
        functools.partial(forward_kernel, sizes),
        in_specs=[hbm, hbm] + [vmem] * 13,
        out_specs=[vmem] * 3 + [hbm] * 5 + [vmem] + [hbm] * 5,
        out_shape=[jax.ShapeDtypeStruct(shape, dtype) for shape, dtype in outs],
        scratch_shapes=[
            pltpu.VMEM(shape, dtype)
            for shape, dtype in saved + [rows, rows, early, late, vectors, rows] + blocks
        ]
        + [
            pltpu.SemaphoreType.DMA((count,)),
            pltpu.SemaphoreType.DMA((count,)),
            pltpu.SemaphoreType.DMA((25,)),
        ],
        compiler_params=pltpu.CompilerParams(
            vmem_limit_bytes=VMEM_BYTES, collective_id=0, has_side_effects=True
        ),
        name="layers_forward",
    )(inputs, cot, *weights, *vector_parts)


def add_row(sums, layer, start, value):
    where = (layer, slice(None), slice(start, start + value.shape[1]))
    sums[where] = sums[where] + value


def column_sum(values):
    return jnp.sum(values, axis=0, keepdims=True)


def put_block(target, part, start, value):
    depth, block = (target.shape[1] // 2, target.shape[2])
    low = value.astype(jnp.bfloat16)
    for row in range(2 * depth):
        target[part, (row % 2) * depth + row // 2, :, start : start + value.shape[1]] = low[
            row * block : (row + 1) * block
        ]


def backward_mlp(
    sizes,
    layer,
    hidden,
    active,
    slope,
    late,
    vectors,
    grad,
    sums,
    normed_t,
    grad_t,
    grad_late,
    hooks,
    after_rows,
):
    features, width, size = (sizes.features, sizes.width, sizes.hidden)
    whole, split = vector_reader(sizes, vectors, layer)

    def one_tile(index, carry):
        rows = tile_rows(index)
        grad_out = grad[rows, :]
        add_row(sums, layer, 5 * features, column_sum(grad_out))
        grad_low = grad_out.astype(jnp.bfloat16)
        grad_t[:, rows] = grad_low.T
        centered, inv_std = norm_rows(hidden[rows, :])
        normed_t[:, rows] = (centered * whole(3) + whole(4)).astype(jnp.bfloat16).T
        grad_normed = jnp.zeros((TILE, features), jnp.float32)
        for part in range(2):
            for start in range(0, size, CHUNK):
                first = part * size + start
                grad_act = contract(grad_low, whole_weight(late, part, size + start, CHUNK), 1, 0)
                grad_pre = grad_act * slope[rows, first : first + CHUNK].astype(jnp.float32)
                add_row(
                    sums,
                    layer,
                    sizes.tails + part * sizes.tail + 2 * width + start,
                    column_sum(grad_pre),
                )
                low = grad_pre.astype(jnp.bfloat16)
                slope[rows, first : first + CHUNK] = low
                grad_normed = grad_normed + contract(
                    low, whole_weight(late, part, start, CHUNK), 1, 1
                )
        add_row(sums, layer, 3 * features, column_sum(grad_normed * centered))
        add_row(sums, layer, 4 * features, column_sum(grad_normed))
        grad_hidden = grad_out + norm_rows_backward(grad_normed, centered, inv_std, whole(3))
        add_row(sums, layer, 2 * features, column_sum(grad_hidden))
        grad[rows, :] = grad_hidden
        run_hooks(hooks, index)
        return carry

    lax.fori_loop(0, sizes.tiles, one_tile, 0)
    after_rows()
    for part in range(2):
        for start in range(0, size, 256):
            first = part * size + start
            up = contract(normed_t[...], slope[:, first : first + 256], 1, 0)
            put_block(grad_late, part, start, up)
            down = contract(grad_t[...], active[:, first : first + 256], 1, 0)
            put_block(grad_late, part, size + start, down)


def backward_context(
    sizes, layer, values, early, vectors, grad, normed_t, grad_t, grad_context
):
    width = sizes.width
    whole, split = vector_reader(sizes, vectors, layer)

    def to_context(index, carry):
        rows = tile_rows(index)
        low = grad[rows, :].astype(jnp.bfloat16)
        grad_t[:, rows] = low.T
        for part in range(2):
            grad_context[rows, part * width : (part + 1) * width] = contract(
                low, whole_weight(early, part, 3 * width, width), 1, 0
            ).astype(jnp.bfloat16)
        centered, unused = norm_rows(values[rows, :].astype(jnp.float32))
        normed_t[:, rows] = (centered * whole(0) + whole(1)).astype(jnp.bfloat16).T
        return carry

    lax.fori_loop(0, sizes.tiles, to_context, 0)


def backward_early_weights(sizes, qkv, context, normed_t, grad_t, grad_early):
    width = sizes.width
    for part in range(2):
        for kind in range(3):
            first = (3 * part + kind) * width
            result = contract(normed_t[...], qkv[:, first : first + width], 1, 0)
            put_block(grad_early, part, kind * width, result)
        result = contract(grad_t[...], context[:, part * width : (part + 1) * width], 1, 0)
        put_block(grad_early, part, 3 * width, result)


def backward_input(sizes, layer, values, qkv, early, vectors, grad, sums, grad_in):
    features, width = (sizes.features, sizes.width)
    whole, split = vector_reader(sizes, vectors, layer)

    def to_input(index, carry):
        rows = tile_rows(index)
        grad_normed = jnp.zeros((TILE, features), jnp.float32)
        for part in range(2):
            grad_normed = grad_normed + contract(
                qkv[rows, part * 3 * width : (part + 1) * 3 * width],
                whole_weight(early, part, 0, 3 * width),
                1,
                1,
            )
        centered, inv_std = norm_rows(values[rows, :].astype(jnp.float32))
        add_row(sums, layer, 0, column_sum(grad_normed * centered))
        add_row(sums, layer, features, column_sum(grad_normed))
        low = (
            grad[rows, :] + norm_rows_backward(grad_normed, centered, inv_std, whole(0))
        ).astype(jnp.bfloat16)
        grad_in[rows, :] = low
        grad[rows, :] = low.astype(jnp.float32)
        return carry

    lax.fori_loop(0, sizes.tiles, to_input, 0)


def add_low(left, right):
    return (left.astype(jnp.float32) + right.astype(jnp.float32)).astype(jnp.bfloat16)


class Reduce:
    def __init__(self, wires, grads, from_core, x_one, y_one, y_two, x_two, joined, from_z, total, low, from_x):
        self.wires, self.grads, self.from_core = (wires, grads, from_core)
        self.x_one, self.y_one, self.y_two, self.x_two = (x_one, y_one, y_two, x_two)
        self.joined, self.from_z = (joined, from_z)
        self.total, self.from_x, self.low = (total, from_x, low)
        depth, half = (wires.depth, grads.shape[2] // 2)
        middle = grads.shape[3] // 2
        self.half, self.middle = (half, middle)
        left, right = (pl.ds(0, middle), pl.ds(middle, middle))
        self.left, self.right = (slice(0, middle), slice(middle, 2 * middle))
        slots = pl.ds((1 - wires.core) * depth, depth)
        self.mine = pl.ds(pl.multiple_of(wires.pipe * half, half), half)
        self.theirs = pl.ds(pl.multiple_of((1 - wires.pipe) * half, half), half)
        col, planes, rows = (1 - wires.col, pl.ds(0, depth), pl.ds(0, 2 * half))
        self.core, self.first, self.second, self.z = ([], [], [], [])
        for layer in range(2):
            self.core.append(
                wires.copy(grads.at[:, slots], from_core.at[layer], wires.across_core)
            )
            held = from_core.at[layer]
            self.first.append(
                [
                    wires.copy(
                        held.at[pl.ds(0, 2), planes, self.theirs, left],
                        x_one.at[layer],
                        wires.across_x,
                    ),
                    wires.copy(
                        held.at[col, planes, rows, right], y_one.at[layer], wires.across_y
                    ),
                ]
            )
            self.second.append(
                [
                    wires.copy(x_one.at[layer, col], y_two.at[layer], wires.across_y),
                    wires.copy(
                        y_one.at[layer, planes, self.theirs], x_two.at[layer], wires.across_x
                    ),
                ]
            )
            self.z.append(
                [
                    wires.copy(
                        joined.at[layer, wires.plane_at(step)],
                        from_z.at[layer, wires.plane],
                        wires.along_z(step),
                    )
                    for step in range(1, depth)
                ]
            )
        self.x = wires.copy(low.at[1 - wires.pipe], from_x, wires.across_x)

    def each_plane(self, body):
        def one(plane, carry):
            body(plane)
            return carry

        lax.fori_loop(0, self.wires.depth, one, 0)

    def end_core(self, layer):
        wires, held = (self.wires, self.from_core)
        self.core[layer].wait()

        def add(plane):
            for part in range(2):
                held[layer, part, plane] = add_low(
                    held[layer, part, plane],
                    self.grads[part, wires.core * wires.depth + plane],
                )

        self.each_plane(add)
        for copy in self.first[layer]:
            copy.start()

    def end_first(self, layer):
        held, x_one, y_one = (self.from_core, self.x_one, self.y_one)
        for copy in self.first[layer]:
            copy.wait_recv()

        def add(plane):
            for part in range(2):
                x_one[layer, part, plane] = add_low(
                    x_one[layer, part, plane], held[layer, part, plane, self.mine, self.left]
                )
            y_one[layer, plane] = add_low(
                y_one[layer, plane], held[layer, self.wires.col, plane, :, self.right]
            )

        self.each_plane(add)
        for copy in self.second[layer]:
            copy.start()

    def end_second(self, layer):
        joined = self.joined
        for copy in self.second[layer]:
            copy.wait_recv()

        def add(plane):
            joined[layer, plane, :, self.left] = add_low(
                self.y_two[layer, plane], self.x_one[layer, self.wires.col, plane]
            )
            joined[layer, plane, :, self.right] = add_low(
                self.x_two[layer, plane], self.y_one[layer, plane, self.mine, :]
            )

        self.each_plane(add)
        for copy in self.z[layer]:
            copy.start()

    def end_z(self, layer):
        wires = self.wires
        for copy in self.z[layer]:
            copy.wait_recv()
        total = self.joined[layer, wires.plane].astype(jnp.float32)
        for step in range(1, wires.depth):
            total = total + self.from_z[layer, wires.plane_at(step)].astype(jnp.float32)
        self.total[layer] = total
        self.low[layer] = total.astype(jnp.bfloat16)

    def end_x(self, target):
        self.x.wait()
        target[self.mine, :] = self.total[self.wires.pipe]
        target[self.theirs, :] = self.from_x[...].astype(jnp.float32)
        for layer in range(2):
            for copy in self.first[layer] + self.second[layer] + self.z[layer]:
                copy.wait_send()


class ReduceSums:
    def __init__(self, wires, sums, second, third, from_all, from_x):
        self.wires = wires
        self.stages = (sums, second, third)
        self.from_all, self.from_x = (from_all, from_x)
        self.core, self.y, self.z = ([], [], [])
        for layer in range(2):
            self.core.append(
                wires.copy(sums.at[layer], from_all.at[layer, 0], wires.across_core)
            )
            self.y.append(wires.copy(second.at[layer], from_all.at[layer, 1], wires.across_y))
            self.z.append(
                [
                    wires.copy(
                        third.at[layer], from_all.at[layer, 2 + wires.plane], wires.along_z(step)
                    )
                    for step in range(1, wires.depth)
                ]
            )
        self.x = wires.copy(sums.at[1 - wires.pipe], from_x, wires.across_x)

    def end_core(self, layer):
        self.core[layer].wait()
        self.stages[1][layer] = self.stages[0][layer] + self.from_all[layer, 0]
        self.y[layer].start()

    def end_y(self, layer):
        self.y[layer].wait()
        self.stages[2][layer] = self.stages[1][layer] + self.from_all[layer, 1]
        for copy in self.z[layer]:
            copy.start()

    def end_z(self, layer):
        wires = self.wires
        for copy in self.z[layer]:
            copy.wait()
        self.from_all[layer, 2 + wires.plane] = self.stages[2][layer]
        total = self.from_all[layer, 2]
        for plane in range(1, wires.depth):
            total = total + self.from_all[layer, 2 + plane]
        self.stages[0][layer] = total

    def end_x(self, target):
        self.x.wait()
        target[...] = self.stages[0][self.wires.pipe] + self.from_x[...]


class Trade:
    def __init__(self, sizes, wires, local, layer, source, target):
        half = sizes.half
        self.wires, self.layer = (wires, layer)
        self.copies = []
        for step in range(1, 4):
            pipe = wires.pipe if step < 2 else 1 - wires.pipe
            col = wires.col if step == 2 else 1 - wires.col
            rows = pl.ds(pl.multiple_of(col * half, half), half)
            copy = wires.copy(
                source.at[rows], target.at[wires.place], (pipe, wires.row, col)
            )
            self.copies.append((pipe == layer, copy))
        rows = pl.ds(pl.multiple_of(wires.col * half, half), half)
        self.own = pltpu.make_async_copy(
            source.at[rows], target.at[wires.place], local.sems.at[local.used]
        )
        local.used += 1

    def start(self):
        for wanted, copy in self.copies:
            pl.when(wanted)(copy.start)
        pl.when(self.wires.pipe == self.layer)(self.own.start)

    def finish(self):
        for wanted, copy in self.copies:
            pl.when(wanted)(copy.wait_send)

        def arrive():
            self.own.wait()
            for wanted, copy in self.copies:
                copy.wait_recv()

        pl.when(self.wires.pipe == self.layer)(arrive)


def backward_kernel(
    sizes,
    live_ref,
    cot_ref,
    x_ref,
    sent_ref,
    final_ref,
    vectors,
    lse_ref,
    early_in,
    late_in,
    qkv_in,
    context_in,
    hidden_in,
    active_in,
    slope_in,
    states_in,
    states_out,
    grads_out,
    sums_out,
    early_out,
    late_out,
    qkv,
    context,
    hidden,
    active,
    slope,
    early,
    late,
    mid,
    first,
    values,
    grad,
    normed_t,
    grad_t,
    grad_context,
    grad_early,
    grad_late,
    early_core,
    early_x_one,
    early_y_one,
    early_y_two,
    early_x_two,
    early_joined,
    early_z,
    early_total,
    early_low,
    early_x,
    late_core,
    late_x_one,
    late_y_one,
    late_y_two,
    late_x_two,
    late_joined,
    late_z,
    late_total,
    late_low,
    late_x,
    sums,
    sums_second,
    sums_third,
    sums_all,
    sums_x,
    send,
    recv,
    sems,
):
    wires = Wires(sizes, send, recv)
    local = Local(sems)

    def load(source, target, layer):
        return local.start(source.at[layer], target)

    def load_pair(source, target, layer):
        return local.start(source.at[pl.ds(2 * layer, 2)], target)

    cot_copy = local.start(cot_ref, first)
    late_copy = load_pair(late_in, late, 1)
    slope_copy = load(slope_in, slope, 1)
    hidden_copy = load(hidden_in, hidden, 1)
    active_copy = load(active_in, active, 1)
    early_copy = load_pair(early_in, early, 1)
    attention_copies = [
        load(qkv_in, qkv, 1),
        load(context_in, context, 1),
        local.start(sent_ref, values),
    ]
    sums[...] = jnp.zeros_like(sums)
    wires.greet()
    trades = [Trade(sizes, wires, local, 1, final_ref, states_out)]
    trades[0].start()
    cot_copy.wait()
    grad[...] = first[...].astype(jnp.float32) * live_ref[wires.place, 0].astype(jnp.float32)
    early_sum = Reduce(
        wires,
        grad_early,
        early_core,
        early_x_one,
        early_y_one,
        early_y_two,
        early_x_two,
        early_joined,
        early_z,
        early_total,
        early_low,
        early_x,
    )
    late_sum = Reduce(
        wires,
        grad_late,
        late_core,
        late_x_one,
        late_y_one,
        late_y_two,
        late_x_two,
        late_joined,
        late_z,
        late_total,
        late_low,
        late_x,
    )
    small_sum = ReduceSums(wires, sums, sums_second, sums_third, sums_all, sums_x)

    def no_wait():
        pass

    def mlp_one():
        late_sum.end_second(1)

    def mlp_two():
        early_sum.end_first(1)
        small_sum.end_y(1)

    def after_mlp_rows():
        late_sum.end_z(1)
        early_sum.end_second(1)
        small_sum.end_z(1)

    def after_rows_of(layer, copy):
        copy.wait()
        if layer == 0:
            after_mlp_rows()

    def pair_zero():
        late_sum.end_core(0)
        early_sum.end_z(1)

    for layer in (1, 0):
        late_copy.wait()
        slope_copy.wait()
        hidden_copy.wait()
        backward_mlp(
            sizes,
            layer,
            hidden,
            active,
            slope,
            late,
            vectors,
            grad,
            sums,
            normed_t,
            grad_t,
            grad_late,
            {} if layer == 1 else {1: mlp_one, 2: mlp_two},
            functools.partial(after_rows_of, layer, active_copy),
        )
        late_sum.core[layer].start()
        if layer == 1:
            late_copy = load_pair(late_in, late, 0)
            slope_copy = load(slope_in, slope, 0)
            hidden_copy = load(hidden_in, hidden, 0)
            active_copy = load(active_in, active, 0)
        early_copy.wait()
        for copy in attention_copies:
            copy.wait()
        backward_context(
            sizes, layer, values, early, vectors, grad, normed_t, grad_t, grad_context
        )

        def add_bias(offset):
            def add(part, index, value):
                start = sizes.tails + part * sizes.tail + offset + index * LANES
                where = (layer, slice(None), lane_block(start))
                sums[where] = sums[where] + value

            return add

        if layer == 1:
            hooks = {0: functools.partial(late_sum.end_core, 1)}
        else:
            hooks = {0: pair_zero, 1: functools.partial(late_sum.end_first, 0)}
        attention_backward(
            sizes,
            qkv,
            context,
            grad_context,
            lse_ref.at[layer],
            add_bias(0),
            add_bias(sizes.width),
            hooks,
        )
        if layer == 1:
            late_sum.end_first(1)
        else:
            late_sum.end_second(0)
        grad_in = (first, mid)[layer]
        backward_input(sizes, layer, values, qkv, early, vectors, grad, sums, grad_in)
        trades.append(Trade(sizes, wires, local, layer, grad_in, grads_out))
        if layer == 0:
            for trade in trades[-2:]:
                trade.start()
        small_sum.core[layer].start()
        backward_early_weights(sizes, qkv, context, normed_t, grad_t, grad_early)
        early_sum.core[layer].start()
        small_sum.end_core(layer)
        early_sum.end_core(layer)
        if layer == 1:
            early_copy = load_pair(early_in, early, 0)
            attention_copies = [
                load(qkv_in, qkv, 0),
                load(context_in, context, 0),
                local.start(x_ref, values),
            ]
    early_sum.end_first(0)
    small_sum.end_y(0)
    late_sum.end_z(0)
    late_sum.x.start()
    early_sum.end_second(0)
    small_sum.end_z(0)
    small_sum.x.start()
    early_sum.end_z(0)
    early_sum.x.start()
    late_sum.end_x(late_out)
    early_sum.end_x(early_out)
    small_sum.end_x(sums_out)
    for trade in trades:
        trade.finish()


def run_backward(sizes, live, cot, values, sent, final, vectors, lse, early, late, states, saved):
    frames, features, depth = (sizes.frames, sizes.features, sizes.depth)
    vmem = pl.BlockSpec(memory_space=pltpu.VMEM)
    hbm = pl.BlockSpec(memory_space=pl.ANY)
    smem = pl.BlockSpec(memory_space=pltpu.SMEM)
    low, high = (jnp.bfloat16, jnp.float32)

    def reduce_shapes(block):
        rows, columns = block[1:]
        half, middle = (rows // 2, columns // 2)
        return [
            ((2, 2, depth, rows, columns), low),
            ((2, 2, depth, half, middle), low),
            ((2, depth, rows, middle), low),
            ((2, depth, half, middle), low),
            ((2, depth, half, middle), low),
            ((2, depth, half, columns), low),
            ((2, depth, half, columns), low),
            ((2, half, columns), high),
            ((2, half, columns), low),
            ((half, columns), low),
        ]

    row = (1, sizes.sums)
    scratch = [(shape[1:], dtype) for shape, dtype in saved_shapes(sizes)]
    scratch += [((2,) + sizes.early, low), ((2,) + sizes.late, low)]
    scratch += [((frames, features), low)] * 3 + [((frames, features), high)]
    scratch += [((features, frames), low)] * 2 + [((frames, 2 * sizes.width), low)]
    scratch += [((2,) + sizes.early, low), ((2,) + sizes.late, low)]
    scratch += reduce_shapes(sizes.early) + reduce_shapes(sizes.late)
    scratch += [((2,) + row, high)] * 3 + [((2, 2 + depth) + row, high), (row, high)]
    count = 9 + 2 * (2 * (5 + depth - 1) + 2 + depth - 1) + 3
    return pl.pallas_call(
        functools.partial(backward_kernel, sizes),
        in_specs=[smem] + [hbm] * 4 + [vmem] * 2 + [hbm] * 8,
        out_specs=[hbm, hbm, vmem, vmem, vmem],
        out_shape=[
            jax.ShapeDtypeStruct((4, sizes.half, features), low),
            jax.ShapeDtypeStruct((4, sizes.half, features), low),
            jax.ShapeDtypeStruct(row, high),
            jax.ShapeDtypeStruct(sizes.early[1:], high),
            jax.ShapeDtypeStruct(sizes.late[1:], high),
        ],
        scratch_shapes=[pltpu.VMEM(shape, dtype) for shape, dtype in scratch]
        + [
            pltpu.SemaphoreType.DMA((count,)),
            pltpu.SemaphoreType.DMA((count,)),
            pltpu.SemaphoreType.DMA((21,)),
        ],
        compiler_params=pltpu.CompilerParams(
            vmem_limit_bytes=VMEM_BYTES, collective_id=1, has_side_effects=True
        ),
        input_output_aliases={14: 0},
        name="layers_backward",
    )(live, cot, values, sent, final, vectors, lse, early, late, *saved, states)


def on_device_clip(
    inputs,
    first_gain,
    first_shift,
    qkv_weight,
    query_bias,
    value_bias,
    proj_weight,
    proj_bias,
    second_gain,
    second_shift,
    up_weight,
    up_bias,
    down_weight,
    down_bias,
    cotangent,
    live_clips,
):
    col = lax.axis_index("col")
    width, hidden_width = (qkv_weight.shape[3], up_weight.shape[2])
    features = inputs.shape[3]
    sizes = Sizes(
        2 * inputs.shape[2], features, width, hidden_width, lax.axis_size("row") // 2
    )
    vector_parts = (
        first_gain,
        first_shift,
        proj_bias,
        second_gain,
        second_shift,
        down_bias,
        query_bias,
        value_bias,
        up_bias,
    )
    sent, final, lse, states, values, cot, early, late, vectors, *saved = run_forward(
        sizes,
        inputs,
        cotangent,
        (qkv_weight, proj_weight, up_weight, down_weight),
        vector_parts,
    )
    states, grads_in, sums, own_early, own_late = run_backward(
        sizes, live_clips, cot, values, sent, final, vectors, lse, early, late, states, saved
    )
    split_out = lax.dynamic_slice(sums, (0, sizes.tails + col * sizes.tail), (1, sizes.tail))
    whole_out = [sums[:, index * features : (index + 1) * features] for index in range(6)]
    return (
        states[None, :, None],
        grads_in.astype(jnp.float32)[None, :, None],
        whole_out[0],
        whole_out[1],
        jnp.stack([own_early[:, part * width : (part + 1) * width] for part in range(3)])[None],
        split_out[:, :width],
        split_out[:, width : 2 * width],
        own_early[:, 3 * width :].T[None],
        whole_out[2],
        whole_out[3],
        whole_out[4],
        own_late[:, :hidden_width][None],
        split_out[:, 2 * width :],
        own_late[:, hidden_width:].T[None],
        whole_out[5],
    )


def one_clip_each(mesh):
    sizes = dict(mesh.shape)
    return sizes["pipe"] == 2 and sizes["col"] == 2


def choose(mesh):
    def body(*arrays):
        fits = one_clip_each(mesh) and arrays[0].shape[:2] == (4, 1)
        return (on_device_clip if fits else on_device)(*arrays)

    return body


def solution(mesh):
    placed = (
        P(None, "row", "col", None),
        P("pipe", None),
        P("pipe", None),
        P("pipe", None, "row", "col"),
        P("pipe", "col"),
        P("pipe", "col"),
        P("pipe", "col", "row"),
        P("pipe", None),
        P("pipe", None),
        P("pipe", None),
        P("pipe", "row", "col"),
        P("pipe", "col"),
        P("pipe", "col", "row"),
        P("pipe", None),
        P(None, "row", "col", None),
        P(None, "row"),
    )
    return jax.shard_map(
        choose(mesh),
        mesh=mesh,
        in_specs=placed,
        out_specs=(
            P("pipe", None, "row", "col", None),
            P("pipe", None, "row", "col", None),
            P("pipe", None),
            P("pipe", None),
            P("pipe", None, "row", "col"),
            P("pipe", "col"),
            P("pipe", "col"),
            P("pipe", "col", "row"),
            P("pipe", None),
            P("pipe", None),
            P("pipe", None),
            P("pipe", "row", "col"),
            P("pipe", "col"),
            P("pipe", "col", "row"),
            P("pipe", None),
        ),
        check_vma=False,
    )
```
